32 devices in a mesh: section: 4 (over x, core), seq: 2 (over y), dp: 4 (over z).
Axes of the slice: x: 2, y: 2, z: 4, core: 2. Of those that a mesh axis runs over, the one named last changes fastest.
Arguments:
- tile_feats: bfloat16 [4, 1024, 1536], P('dp', 'seq', 'section'), may hold values from -6 to 6
- tile_gain: float32 [1536], replicated, may hold values from 0.25 to 1.75
- w_gate: bfloat16 [1536, 4096], P(('seq', 'dp'), 'section'), may hold values from -0.15625 to 0.15625
- w_up: bfloat16 [1536, 4096], P(('seq', 'dp'), 'section'), may hold values from -0.15625 to 0.15625
- w_down: bfloat16 [4096, 1536], P('section', ('seq', 'dp')), may hold values from -0.09375 to 0.09375
- w_proj: bfloat16 [1536, 768], P('section'), may hold values from -0.15625 to 0.15625
- slide_gain: float32 [768], replicated, may hold values from 0.25 to 1.75
- w_qkv: bfloat16 [3, 768, 768], P(None, None, 'section'), may hold values from -0.7647408 to 0.7647408
- w_out: bfloat16 [768, 768], P('section'), may hold values from -0.21875 to 0.21875
- lengths: int32 [4, 3], P('dp'), may hold values from 1 to 768, 1024 in all within a row
- seg_len: int32 [16], P('section'), may hold values from 512 to 1024
- rate: int32 [16], P('section'), may hold values from 1 to 4
Outputs:
- slide_out: bfloat16 [4, 1024, 768], P('dp', 'seq', 'section')
The draws below stay inside these ranges and needn't reach their ends.
Inputs may be any that keep to these rules, and one draw needn't show every extreme that they name: Each row of lengths sums to 1024, and one slide of each pack has 768 tiles.
All inputs are finite; a program needn't handle non-finite values.
Results may differ from the reference program's by a relative error of at most 0.0087.
Values may be sent and summed in bfloat16 or wider, within the bound.
No kernel may reach another device: no remote copies, remote signals or barrier semaphores. Data moves between devices by JAX's collectives and lax.ppermute only.
A program may use at most 192 MiB of HBM per device.

```python
import math
import jax
import jax.numpy as jnp
import numpy as np
from jax import lax

TILE_D = 1536
TILE_FF = 4096
HEADS = 16
HEAD_DIM = 48
TOK_DEV = 512
SLIDES = 3
SLIDE_D = 768
SEQ = 1024
PACKS = 4


def draw_w_qkv(key, part):
    streams = jax.random.split(jax.random.fold_in(key, 7), 6)
    background = jax.random.truncated_normal(streams[0], -4.0, 4.0, (3, SLIDE_D, SLIDE_D), jnp.float32) / math.sqrt(SLIDE_D)
    lowest, highest = (3.0, 8.0)
    choose = jax.random.randint(streams[1], (HEADS // 2,), 0, 2)
    strong_head = jnp.stack([choose == 0, choose == 1], axis=1).reshape(HEADS)
    strong = jnp.exp(jax.random.uniform(streams[2], (HEADS,), jnp.float32, math.log(lowest), math.log(highest)))
    gentle = jnp.exp(jax.random.uniform(streams[3], (HEADS,), jnp.float32, math.log(0.3), math.log(2.0)))
    strength = jnp.where(strong_head, strong, gentle)
    amplitude = jnp.sqrt(strength / math.sqrt(HEAD_DIM))
    direction = jax.random.truncated_normal(streams[4], -4.0, 4.0, (SLIDE_D, HEADS), jnp.float32) / math.sqrt(SLIDE_D)
    pattern = jax.random.truncated_normal(streams[5], -4.0, 4.0, (HEADS, HEAD_DIM), jnp.float32)
    planted = (direction[:, :, None] * (amplitude[:, None] * pattern)[None, :, :]).reshape(SLIDE_D, HEADS * HEAD_DIM)
    nothing = jnp.zeros_like(planted)
    return (background + jnp.stack([planted, planted, nothing])).astype(jnp.bfloat16)


def plant(result, own_key, low, largest):
    longest = result.shape.index(max(result.shape))
    spots = []
    for shift in (0, 1):
        where = [jax.random.randint(jax.random.fold_in(own_key, axis), (), 0, length) for axis, length in enumerate(result.shape)]
        where[longest] = (where[longest] + shift) % result.shape[longest]
        spots.append(tuple(where))
    return result.at[spots[0]].set(low).at[spots[1]].set(largest)


def level_of(key, extent, pieces, least, top_value):
    level = 1.0
    for position, parts in pieces:
        draws = jax.random.uniform(jax.random.fold_in(jax.random.fold_in(key, 6), position), (parts,), jnp.float32, least / len(pieces), top_value / len(pieces))
        level = level * jnp.repeat(jnp.exp(draws), extent[position] // parts).reshape((-1,) + (1,) * (len(extent) - 1 - position))
    return level


def profile(amount, total, limit, lean):
    portions = [(1 << 20) // math.isqrt(rank ** lean) + 1 for rank in range(2, amount + 1)]
    spare, counts = total - limit - (amount - 1), [1] * (amount - 1)
    while spare > 0:
        candidates = [i for i in range(amount - 1) if counts[i] < limit]
        pool, left = sum([portions[i] for i in candidates]), spare
        for i in candidates:
            extra = min(limit - counts[i], max(1, left * portions[i] // pool), spare)
            counts[i] = counts[i] + extra
            spare = spare - extra
    return np.array([limit] + counts)


def uneven(rng, amount, total, bound, slope):
    if amount == 2:
        one = jax.random.randint(rng, (), max(1, total - bound), min(bound, total - 1) + 1)
        return jnp.stack([one, total - one])
    sizes = jnp.asarray(profile(amount, total, bound, slope), jnp.int32)
    couples = (amount - 1) // 2
    source_of, receiver = sizes[1:1 + 2 * couples:2], sizes[2:2 + 2 * couples:2]
    margin = jnp.minimum(source_of - 1, bound - receiver)
    shifted = jax.random.randint(jax.random.fold_in(rng, 1), (couples,), 0, 1 << 20) % (margin + 1)
    sizes = sizes.at[1:1 + 2 * couples:2].set(source_of - shifted).at[2:2 + 2 * couples:2].set(receiver + shifted)
    return sizes[jax.random.permutation(jax.random.fold_in(rng, 2), amount)]


def normal_values(key, dims, deviation, limit, cuts=(), kind=jnp.bfloat16):
    entries = jax.random.normal(key, dims, jnp.float32) * deviation
    if len(cuts) > 0:
        entries = level_of(key, dims, cuts, -0.22, 0.18) * entries
    return jnp.clip(entries, min=-limit, max=limit).astype(kind)


def setup_inputs(seed: int = 0) -> dict:
    arg_keys = jax.random.split(jax.random.key(seed), 13)
    tile_feats = normal_values(arg_keys[0], (PACKS, SEQ, TILE_D), 1.0, 6.0, ((0, 4), (1, 2), (2, 4)))
    tile_gain = jnp.clip(1.0 + 0.15 * jax.random.normal(arg_keys[1], (TILE_D,), jnp.float32), 0.25, 1.75)
    w_gate = normal_values(arg_keys[2], (TILE_D, TILE_FF), TILE_D ** -0.5, 0.15625, ((0, 8), (1, 4)))
    w_up = normal_values(arg_keys[3], (TILE_D, TILE_FF), TILE_D ** -0.5, 0.15625, ((0, 8), (1, 4)))
    w_down = normal_values(arg_keys[4], (TILE_FF, TILE_D), TILE_FF ** -0.5, 0.09375, ((0, 4), (1, 8)))
    w_proj = normal_values(arg_keys[5], (TILE_D, SLIDE_D), TILE_D ** -0.5, 0.15625, ((0, 4),))
    slide_gain = jnp.clip(1.0 + 0.15 * jax.random.normal(arg_keys[6], (SLIDE_D,), jnp.float32), 0.25, 1.75)
    w_qkv = draw_w_qkv(jax.random.fold_in(arg_keys[12], 71), 0)
    w_out = normal_values(arg_keys[8], (SLIDE_D, SLIDE_D), SLIDE_D ** -0.5, 0.21875, ((0, 4),))
    lengths = jax.vmap(lambda own: uneven(own, SLIDES, SEQ, 3 * SEQ // 4, 2))(jax.random.split(arg_keys[9], PACKS)).reshape((PACKS, SLIDES)).astype(jnp.int32)
    seg_len = plant(jax.random.randint(arg_keys[10], (HEADS,), TOK_DEV, SEQ + 1), jax.random.fold_in(arg_keys[10], 1), TOK_DEV, SEQ).astype(jnp.int32)
    rate = plant(jax.random.randint(arg_keys[11], (HEADS,), 1, 5), jax.random.fold_in(arg_keys[11], 1), 1, 4).astype(jnp.int32)
    return {"tile_feats": tile_feats, "tile_gain": tile_gain, "w_gate": w_gate, "w_up": w_up, "w_down": w_down, "w_proj": w_proj, "slide_gain": slide_gain, "w_qkv": w_qkv, "w_out": w_out, "lengths": lengths, "seg_len": seg_len, "rate": rate}


def layer_norm(rows, gain):
    mean = lax.optimization_barrier(jnp.mean(rows, axis=-1, keepdims=True))
    centered = rows - mean
    var = lax.optimization_barrier(jnp.mean(centered * centered, axis=-1, keepdims=True))
    return centered * lax.rsqrt(var + 1e-06) * gain

def slide_place(lengths_row, index):
    ends = jnp.cumsum(lengths_row, dtype=jnp.int32)
    after = index[:, None] >= ends[None, :]
    slide = lax.optimization_barrier(jnp.sum(after.astype(jnp.int32), axis=1, dtype=jnp.int32))
    before = lax.optimization_barrier(jnp.sum(jnp.where(after, lengths_row[None, :], 0), axis=1, dtype=jnp.int32))
    return (slide, index - before)

def allowed(q_slide, q_pos, q_idx, k_slide, k_pos, k_idx, seg, rate, heads):
    width = seg[:, None, None]
    step = rate[:, None, None]
    offset = (heads % rate)[:, None, None]
    same = (q_slide[:, None] == k_slide[None, :])[None]
    block = q_pos[None, :, None] // width == k_pos[None, None, :] // width
    pick = (k_pos[None, None, :] % step == offset) | (q_idx[:, None] == k_idx[None, :])[None]
    return same & block & pick

def pack_attention(query, key, value, lengths_row, seg_len, rate):
    index = jnp.arange(SEQ, dtype=jnp.int32)
    slide, pos = slide_place(lengths_row, index)
    heads = jnp.arange(HEADS, dtype=jnp.int32)
    qb = math.gcd(SEQ, 512)
    keys = key.reshape(SEQ, HEADS, HEAD_DIM).astype(jnp.float32)
    values = value.reshape(SEQ, HEADS, HEAD_DIM).astype(jnp.float32)
    scale = 1.0 / math.sqrt(HEAD_DIM)

    def one_block(number):
        start = (number * qb).astype(jnp.int32)
        rows = lax.dynamic_slice_in_dim(query, start, qb, 0).reshape(qb, HEADS, HEAD_DIM).astype(jnp.float32)
        q_idx = lax.dynamic_slice_in_dim(index, start, qb, 0)
        q_slide = lax.dynamic_slice_in_dim(slide, start, qb, 0)
        q_pos = lax.dynamic_slice_in_dim(pos, start, qb, 0)
        mask = allowed(q_slide, q_pos, q_idx, slide, pos, index, seg_len, rate, heads)
        scores = jnp.einsum('qhd,khd->hqk', rows, keys) * scale
        scores = jnp.where(mask, scores, -1e+30)
        top = lax.optimization_barrier(jnp.max(scores, axis=-1, keepdims=True))
        weights = jnp.where(mask, jnp.exp(scores - top), 0.0)
        weights = weights / lax.optimization_barrier(jnp.sum(weights, axis=-1, keepdims=True))
        out = jnp.einsum('hqk,khd->qhd', weights, values)
        return out.reshape(qb, SLIDE_D).astype(jnp.bfloat16)
    blocks = lax.map(one_block, jnp.arange(SEQ // qb, dtype=jnp.int32))
    return blocks.reshape(SEQ, SLIDE_D)

def reference(tile_feats, tile_gain, w_gate, w_up, w_down, w_proj, slide_gain, w_qkv, w_out, lengths, seg_len, rate):
    rows = tile_feats.reshape(PACKS * SEQ, TILE_D)
    normed = layer_norm(rows.astype(jnp.float32), tile_gain).astype(jnp.bfloat16)
    gate = jnp.dot(normed, w_gate, preferred_element_type=jnp.float32)
    up = jnp.dot(normed, w_up, preferred_element_type=jnp.float32)
    hidden = (jax.nn.silu(gate) * up).astype(jnp.bfloat16)
    tile_out = (rows.astype(jnp.float32) + jnp.dot(hidden, w_down, preferred_element_type=jnp.float32)).astype(jnp.bfloat16)
    emb = jnp.dot(tile_out, w_proj, preferred_element_type=jnp.float32)
    slide_normed = layer_norm(emb, slide_gain).astype(jnp.bfloat16)
    query = jnp.dot(slide_normed, w_qkv[0], preferred_element_type=jnp.float32).astype(jnp.bfloat16)
    key = jnp.dot(slide_normed, w_qkv[1], preferred_element_type=jnp.float32).astype(jnp.bfloat16)
    value = jnp.dot(slide_normed, w_qkv[2], preferred_element_type=jnp.float32).astype(jnp.bfloat16)
    outputs = []
    for pack in range(PACKS):
        lo = pack * SEQ
        outputs.append(pack_attention(query[lo:lo + SEQ], key[lo:lo + SEQ], value[lo:lo + SEQ], lengths[pack], seg_len, rate))
    att = jnp.concatenate(outputs, axis=0)
    slide_out = emb + jnp.dot(att, w_out, preferred_element_type=jnp.float32)
    return slide_out.astype(jnp.bfloat16).reshape(PACKS, SEQ, SLIDE_D)
```

```python
import math

import jax
import jax.numpy as jnp
from jax import lax
from jax.experimental import pallas as pl
from jax.experimental.pallas import tpu as pltpu
from jax.sharding import PartitionSpec as P

NEG = -1e30
AXES = ("section", "seq", "dp")


def layer_norm(rows, gain):
    mean = jnp.mean(rows, axis=-1, keepdims=True)
    centered = rows - mean
    var = jnp.mean(centered * centered, axis=-1, keepdims=True)
    return centered * lax.rsqrt(var + 1e-06) * gain


def slide_place(lengths_row, index):
    ends = jnp.cumsum(lengths_row, dtype=jnp.int32)
    after = index[:, None] >= ends[None, :]
    slide = jnp.sum(after.astype(jnp.int32), axis=1, dtype=jnp.int32)
    before = jnp.sum(jnp.where(after, lengths_row[None, :], 0), axis=1, dtype=jnp.int32)
    return (slide, index - before)


def attend_block(sec, mine, keys, weights, out_weights, emb, q_code, k_code, heads):
    rows, count = mine.shape[0], keys.shape[0]
    width = weights[0].shape[2]
    size = width // heads
    scale = math.log2(math.e) / math.sqrt(size)
    lane_head = lax.broadcasted_iota(jnp.int32, (rows, width), 1) // size
    diag = lax.broadcasted_iota(jnp.int32, (rows, count), 0) == lax.broadcasted_iota(
        jnp.int32, (rows, count), 1
    )
    total = emb[...]
    for m in range(len(weights)):
        query = jnp.dot(mine, weights[m][0], preferred_element_type=jnp.float32).astype(jnp.bfloat16)
        key = jnp.dot(keys, weights[m][1], preferred_element_type=jnp.float32).astype(jnp.bfloat16)
        value = jnp.dot(keys, weights[m][2], preferred_element_type=jnp.float32).astype(jnp.bfloat16)
        split = jnp.concatenate(
            [jnp.where(lane_head == h, query, jnp.zeros_like(query)) for h in range(heads)], axis=0
        )
        scores = lax.dot_general(
            split, key, (((1,), (1,)), ((), ())), preferred_element_type=jnp.float32
        )
        parts, sums = [], []
        for h in range(heads):
            at = m * heads + h
            ok = (q_code[:, at : at + 1] == k_code[at : at + 1, :]) | diag
            own = jnp.where(ok, scores[h * rows : (h + 1) * rows], NEG)
            top = jnp.max(own, axis=1, keepdims=True)
            weight = jnp.exp2((own - top) * scale)
            sums.append(jnp.sum(weight, axis=1, keepdims=True))
            parts.append(weight.astype(jnp.bfloat16))
        mixed = jnp.dot(jnp.concatenate(parts, axis=0), value, preferred_element_type=jnp.float32)
        att = jnp.zeros((rows, width), jnp.float32)
        for h in range(heads):
            att = jnp.where(lane_head == h, mixed[h * rows : (h + 1) * rows] / sums[h], att)
        total = total + jnp.dot(
            att.astype(jnp.bfloat16), out_weights[m][...], preferred_element_type=jnp.float32
        )
    return total


def attend_kernel(sec_ref, mine_ref, near_ref, far_ref, *refs, heads, parts):
    weights, out_weights = refs[:parts], refs[parts : 2 * parts]
    emb_ref, q_ref, k_ref, out_ref = refs[2 * parts :]
    mine = mine_ref[...]
    keys = jnp.concatenate(
        [mine]
        + [near_ref[i] for i in range(near_ref.shape[0])]
        + [far_ref[i] for i in range(far_ref.shape[0])],
        axis=0,
    )
    total = attend_block(
        sec_ref[0], mine, keys, weights, out_weights, emb_ref, q_ref[...], k_ref, heads
    )
    width = out_ref.shape[2]
    for j in range(parts):
        out_ref[j ^ sec_ref[0]] = total[:, j * width : (j + 1) * width].astype(out_ref.dtype)


def build(n_sec, n_seq, n_dp):
    sizes = {"section": n_sec, "seq": n_seq, "dp": n_dp}

    def flip(x, **masks):
        names = tuple(a for a in AXES if masks.get(a))
        pairs = []
        total = math.prod(sizes[a] for a in names)
        for source in range(total):
            rest, coords = source, []
            for a in reversed(names):
                coords.append(rest % sizes[a])
                rest //= sizes[a]
            target = 0
            for a, c in zip(names, reversed(coords)):
                target = target * sizes[a] + (c ^ masks[a])
            pairs.append((source, target))
        return lax.ppermute(x, names if len(names) > 1 else names[0], pairs)

    def rotate(x, k):
        return lax.ppermute(x, "dp", [(i, (i + k) % n_dp) for i in range(n_dp)])

    def gather_section(x):
        across = flip(x, section=2)
        return [x, flip(x, section=1), across, flip(across, section=1)]

    def gather_rows(same, other, seq_at, dp_at):
        got = [same] + [rotate(other if k % 2 else same, k) for k in range(1, n_dp)]
        mats, rows, units = same.shape
        if n_seq == 2:
            whole = jnp.zeros((mats, n_seq * n_dp * rows, units), same.dtype)
            for k, block in enumerate(got):
                z = (dp_at - k) % n_dp
                theirs = flip(block, seq=1)
                whole = lax.dynamic_update_slice(whole, block, (0, (seq_at * n_dp + z) * rows, 0))
                whole = lax.dynamic_update_slice(
                    whole, theirs, (0, ((1 - seq_at) * n_dp + z) * rows, 0)
                )
            return whole
        part = jnp.zeros((mats, n_dp * rows, units), same.dtype)
        for k, block in enumerate(got):
            part = lax.dynamic_update_slice(part, block, (0, ((dp_at - k) % n_dp) * rows, 0))
        return lax.all_gather(part, "seq", axis=1, tiled=True)

    def per_device(
        tile_feats,
        tile_gain,
        w_gate,
        w_up,
        w_down,
        w_proj,
        slide_gain,
        w_qkv,
        w_out,
        lengths,
        seg_len,
        rate,
    ):
        sec = lax.axis_index("section")
        seq_at = lax.axis_index("seq")
        dp_at = lax.axis_index("dp")
        core, side, odd = sec % 2, sec // 2, dp_at % 2
        mine = tile_feats[0]
        tokens, feats = mine.shape
        own_rows = tokens // n_sec
        half = w_gate.shape[1] // 2

        def absolute(blocks):
            stacked = jnp.stack(blocks)
            return [lax.dynamic_index_in_dim(stacked, sec ^ j, 0, False) for j in range(n_sec)]

        both = jnp.concatenate([mine, flip(mine, dp=1)], axis=0)
        rows = jnp.concatenate(absolute(gather_section(both)), axis=1)

        down = w_down.T

        def halves(x, which):
            return lax.dynamic_slice_in_dim(x, which * half, half, x.ndim - 1)

        pair = jnp.stack([w_gate, w_up])
        gate_up = gather_rows(halves(pair, odd), halves(pair, 1 - odd), seq_at, dp_at)
        down_all = gather_rows(halves(down[None], odd), halves(down[None], 1 - odd), seq_at, dp_at)[0]

        proj = jnp.concatenate(absolute(gather_section(w_proj)), axis=0)
        qkv = gather_section(w_qkv)
        outs = gather_section(w_out)
        head_info = gather_section(jnp.stack([seg_len, rate]))

        normed = layer_norm(rows.astype(jnp.float32), tile_gain).astype(jnp.bfloat16)
        gate = jnp.dot(normed, gate_up[0], preferred_element_type=jnp.float32)
        up = jnp.dot(normed, gate_up[1], preferred_element_type=jnp.float32)
        hidden = (jax.nn.silu(gate) * up).astype(jnp.bfloat16)
        hidden = hidden.reshape(2, n_sec // 2, 2, own_rows, half)
        folded = lax.dot_general(
            proj, down_all, (((0,), (0,)), ((), ())), preferred_element_type=jnp.float32
        ).astype(jnp.bfloat16)

        def project(units):
            return lax.dot_general(
                units, folded, (((4 - 1,), (1,)), ((), ())), preferred_element_type=jnp.float32
            )

        send = project(lax.dynamic_index_in_dim(hidden, 1 - core, 2, False)).astype(jnp.bfloat16)
        got = flip(send, section=1)
        kept = project(lax.dynamic_index_in_dim(hidden, core, 2, False)) + got.astype(jnp.float32)
        here = lax.dynamic_index_in_dim(kept, side, 1, False)
        there = lax.dynamic_index_in_dim(kept, 1 - side, 1, False).astype(jnp.bfloat16)
        from_x = flip(there[0], section=2)
        from_z = flip(here[1].astype(jnp.bfloat16), dp=1)
        from_xz = flip(there[1], section=2, dp=1)
        residual = jnp.dot(
            lax.dynamic_slice_in_dim(rows[:tokens], sec * own_rows, own_rows, 0),
            proj,
            preferred_element_type=jnp.float32,
        )
        emb = (
            residual
            + here[0]
            + from_x.astype(jnp.float32)
            + from_z.astype(jnp.float32)
            + from_xz.astype(jnp.float32)
        )
        slide_normed = layer_norm(emb, slide_gain).astype(jnp.bfloat16)

        my_start = seq_at * tokens + sec * own_rows
        span = jnp.arange(own_rows, dtype=jnp.int32)
        if n_seq == 2:
            near = jnp.stack(
                [
                    flip(slide_normed, section=2),
                    flip(slide_normed, seq=1),
                    flip(slide_normed, section=2, seq=1),
                ]
            )
            far = flip(jnp.concatenate([slide_normed[None], near]), section=1)
            order = [(s, q) for s in (0, 1) for q in ((0, 0), (2, 0), (0, 1), (2, 1))]
            starts = [(seq_at ^ q[1]) * tokens + (sec ^ q[0] ^ s) * own_rows for s, q in order]
            k_idx = jnp.concatenate([start + span for start in starts])
        else:
            every = lax.all_gather(slide_normed, ("seq", "section"), axis=0, tiled=True)
            count = every.shape[0]
            keys = jnp.concatenate([slide_normed, jnp.roll(every, -my_start, axis=0)[own_rows:]])
            k_idx = (my_start + jnp.arange(count, dtype=jnp.int32)) % count
        count = k_idx.shape[0]

        local_heads = seg_len.shape[0]
        heads = jnp.concatenate(
            [(sec ^ m) * local_heads + jnp.arange(local_heads, dtype=jnp.int32) for m in range(n_sec)]
        )
        seg_all = jnp.concatenate([info[0] for info in head_info])
        rate_all = jnp.concatenate([info[1] for info in head_info])
        slide, pos = slide_place(lengths[0], k_idx)
        block = slide[None, :] * count + pos[None, :] // seg_all[:, None]
        picked = pos[None, :] % rate_all[:, None] == (heads % rate_all)[:, None]
        k_code = jnp.where(picked, block, -1)
        q_code = block[:, :own_rows].T

        width = w_qkv.shape[2]
        if n_seq == 2:
            params = dict(
                compiler_params=pltpu.CompilerParams(vmem_limit_bytes=48 * 2**20),
                cost_estimate=pl.CostEstimate(
                    flops=2 * n_sec * count * width * (2 * 768 + 2 * local_heads * own_rows),
                    bytes_accessed=8 * 2**20,
                    transcendentals=n_sec * local_heads * own_rows * count,
                ),
            )
            vmem = pl.BlockSpec(memory_space=pltpu.VMEM)
            final = pl.pallas_call(
                lambda *refs: attend_kernel(*refs, heads=local_heads, parts=n_sec),
                out_shape=jax.ShapeDtypeStruct((n_sec, own_rows, width), jnp.bfloat16),
                in_specs=[pl.BlockSpec(memory_space=pltpu.SMEM)] + [vmem] * (6 + 2 * n_sec),
                out_specs=vmem,
                **params,
            )(sec[None], slide_normed, near, far, *qkv, *outs, emb, q_code, k_code)
        else:
            total = emb
            for m in range(n_sec):
                query = jnp.dot(slide_normed, qkv[m][0], preferred_element_type=jnp.float32)
                key = jnp.dot(keys, qkv[m][1], preferred_element_type=jnp.float32)
                value = jnp.dot(keys, qkv[m][2], preferred_element_type=jnp.float32)
                size = width // local_heads

                def one_head(args):
                    q, k, v, q_row, k_row = args
                    scores = jnp.dot(q, k.T, preferred_element_type=jnp.float32) / math.sqrt(size)
                    diag = jnp.arange(own_rows)[:, None] == jnp.arange(count)[None, :]
                    ok = (q_row[:, None] == k_row[None, :]) | diag
                    weight = jax.nn.softmax(jnp.where(ok, scores, NEG), axis=-1)
                    return jnp.dot(weight, v, preferred_element_type=jnp.float32)

                def by_head(x):
                    return x.astype(jnp.bfloat16).reshape(-1, local_heads, size).transpose(1, 0, 2)

                at = slice(m * local_heads, (m + 1) * local_heads)
                att = lax.map(
                    one_head,
                    (by_head(query), by_head(key), by_head(value), q_code.T[at], k_code[at]),
                )
                att = att.transpose(1, 0, 2).reshape(own_rows, width).astype(jnp.bfloat16)
                total = total + jnp.dot(att, outs[m], preferred_element_type=jnp.float32)
            cut = total.astype(jnp.bfloat16).reshape(own_rows, n_sec, width).transpose(1, 0, 2)
            final = jnp.stack(
                [lax.dynamic_index_in_dim(cut, sec ^ m, 0, False) for m in range(n_sec)]
            )

        pieces = [final[0]] + [flip(final[m], section=m) for m in range(1, n_sec)]
        return jnp.concatenate(absolute(pieces), axis=0)[None]

    return per_device


def solution(mesh):
    placed = (
        P("dp", "seq", "section"),
        P(),
        P(("seq", "dp"), "section"),
        P(("seq", "dp"), "section"),
        P("section", ("seq", "dp")),
        P("section", None),
        P(),
        P(None, None, "section"),
        P("section", None),
        P("dp", None),
        P("section"),
        P("section"),
    )
    shape = mesh.shape
    return jax.shard_map(
        build(shape["section"], shape["seq"], shape["dp"]),
        mesh=mesh,
        in_specs=placed,
        out_specs=P("dp", "seq", "section"),
        check_vma=False,
    )
```

```python
import math

import jax
import jax.numpy as jnp
from jax import lax
from jax.experimental import pallas as pl
from jax.experimental.pallas import tpu as pltpu
from jax.sharding import PartitionSpec as P

NEG = -1e30
AXES = ("section", "seq", "dp")


def layer_norm(rows, gain):
    mean = jnp.mean(rows, axis=-1, keepdims=True)
    centered = rows - mean
    var = jnp.mean(centered * centered, axis=-1, keepdims=True)
    return centered * lax.rsqrt(var + 1e-06) * gain


def slide_place(lengths_row, index):
    ends = jnp.cumsum(lengths_row, dtype=jnp.int32)
    after = index[:, None] >= ends[None, :]
    slide = jnp.sum(after.astype(jnp.int32), axis=1, dtype=jnp.int32)
    before = jnp.sum(jnp.where(after, lengths_row[None, :], 0), axis=1, dtype=jnp.int32)
    return (slide, index - before)


def attend_kernel(sec_ref, mine_ref, *refs, heads, size):
    near, (far_ref, w_ref, emb_ref, q_ref, k_ref, out_ref) = refs[:-6], refs[-6:]
    parts, _, width, _ = w_ref.shape
    rows = mine_ref.shape[0]
    mine = mine_ref[...]
    keys = jnp.concatenate(
        [mine] + [ref[...] for ref in near] + [far_ref[i] for i in range(far_ref.shape[0])], axis=0
    )
    count = keys.shape[0]
    scale = math.log2(math.e) / math.sqrt(size)

    def project(x, which):
        matrix = jnp.concatenate([w_ref[m, which] for m in range(parts)], axis=0)
        return lax.dot_general(
            x, matrix, (((1,), (1,)), ((), ())), preferred_element_type=jnp.float32
        ).astype(jnp.bfloat16)

    query, key, value = project(mine, 0), project(keys, 1), project(keys, 2)
    out_matrix = jnp.concatenate([w_ref[m, 3] for m in range(parts)], axis=0)
    diag = lax.broadcasted_iota(jnp.int32, (rows, count), 0) == lax.broadcasted_iota(
        jnp.int32, (rows, count), 1
    )
    total = emb_ref[...]
    for m in range(parts):
        lo = m * width // 128 * 128
        hi = -(-(m + 1) * width // 128) * 128
        lane_head = (lax.broadcasted_iota(jnp.int32, (rows, hi - lo), 1) + lo) // size
        q_part = query[:, lo:hi]
        split = jnp.concatenate(
            [
                jnp.where(lane_head == m * heads + h, q_part, jnp.zeros_like(q_part))
                for h in range(heads)
            ],
            axis=0,
        )
        scores = lax.dot_general(
            split, key[:, lo:hi], (((1,), (1,)), ((), ())), preferred_element_type=jnp.float32
        )
        weights, sums = [], []
        for h in range(heads):
            at = m * heads + h
            ok = (q_ref[:, at : at + 1] == k_ref[at : at + 1, :]) | diag
            own = jnp.where(ok, scores[h * rows : (h + 1) * rows], NEG)
            top = jnp.max(own, axis=1, keepdims=True)
            weight = jnp.exp2((own - top) * scale)
            sums.append(jnp.sum(weight, axis=1, keepdims=True))
            weights.append(weight.astype(jnp.bfloat16))
        mixed = jnp.dot(
            jnp.concatenate(weights, axis=0), value[:, lo:hi], preferred_element_type=jnp.float32
        )
        att = jnp.zeros((rows, hi - lo), jnp.float32)
        for h in range(heads):
            att = jnp.where(
                lane_head == m * heads + h, mixed[h * rows : (h + 1) * rows] / sums[h], att
            )
        total = total + jnp.dot(
            att.astype(jnp.bfloat16), out_matrix[lo:hi], preferred_element_type=jnp.float32
        )
    for j in range(parts):
        out_ref[j ^ sec_ref[0]] = total[:, j * width : (j + 1) * width].astype(out_ref.dtype)


def build(n_sec, n_seq, n_dp):
    sizes = {"section": n_sec, "seq": n_seq, "dp": n_dp}

    def flip(x, **masks):
        names = tuple(a for a in AXES if masks.get(a))
        pairs = []
        total = math.prod(sizes[a] for a in names)
        for source in range(total):
            rest, coords = source, []
            for a in reversed(names):
                coords.append(rest % sizes[a])
                rest //= sizes[a]
            target = 0
            for a, c in zip(names, reversed(coords)):
                target = target * sizes[a] + (c ^ masks[a])
            pairs.append((source, target))
        return lax.ppermute(x, names if len(names) > 1 else names[0], pairs)

    def rotate(x, k):
        return lax.ppermute(x, "dp", [(i, (i + k) % n_dp) for i in range(n_dp)])

    def gather_section(x):
        across = flip(x, section=2)
        return [x, flip(x, section=1), across, flip(across, section=1)]

    def gather_rows(same, other, seq_at, dp_at):
        got = {0: same}
        mats, rows, units = same.shape
        last = n_dp // 2
        for k in [k for k in range(1, n_dp) if k != last] + [last]:
            block = other if k % 2 else same
            if k == last and n_dp > 2:
                block, got[1] = lax.optimization_barrier((block, got[1]))
            got[k] = rotate(block, k)
        if n_seq == 2:
            whole = jnp.zeros((mats, n_seq * n_dp * rows, units), same.dtype)
            for k, block in got.items():
                z = (dp_at - k) % n_dp
                theirs = flip(block, seq=1)
                whole = lax.dynamic_update_slice(whole, block, (0, (seq_at * n_dp + z) * rows, 0))
                whole = lax.dynamic_update_slice(
                    whole, theirs, (0, ((1 - seq_at) * n_dp + z) * rows, 0)
                )
            return whole
        part = jnp.zeros((mats, n_dp * rows, units), same.dtype)
        for k, block in got.items():
            part = lax.dynamic_update_slice(part, block, (0, ((dp_at - k) % n_dp) * rows, 0))
        return lax.all_gather(part, "seq", axis=1, tiled=True)

    def per_device(
        tile_feats,
        tile_gain,
        w_gate,
        w_up,
        w_down,
        w_proj,
        slide_gain,
        w_qkv,
        w_out,
        lengths,
        seg_len,
        rate,
    ):
        sec = lax.axis_index("section")
        seq_at = lax.axis_index("seq")
        dp_at = lax.axis_index("dp")
        core, side, odd = sec % 2, sec // 2, dp_at % 2
        mine = tile_feats[0]
        tokens, feats = mine.shape
        own_rows = tokens // n_sec
        half = w_gate.shape[1] // 2

        def absolute(blocks):
            stacked = jnp.stack(blocks)
            return [lax.dynamic_index_in_dim(stacked, sec ^ j, 0, False) for j in range(n_sec)]

        both = jnp.concatenate([mine, flip(mine, dp=1)], axis=0)
        rows = jnp.concatenate(absolute(gather_section(both)), axis=1)

        matrices = jnp.stack([w_gate, w_up, w_down.T])

        def halves(which):
            return lax.dynamic_slice_in_dim(matrices, which * half, half, 2)

        units = gather_rows(halves(odd), halves(1 - odd), seq_at, dp_at)

        proj = lax.all_gather(w_proj, "section", axis=0, tiled=True)
        slide_w = jnp.concatenate([jnp.swapaxes(w_qkv, 1, 2), w_out[None]], axis=0)
        slide_w = lax.all_gather(slide_w, "section", axis=0)
        head_info = lax.all_gather(jnp.stack([seg_len, rate]), "section", axis=1, tiled=True)

        normed = layer_norm(rows.astype(jnp.float32), tile_gain).astype(jnp.bfloat16)
        gate = jnp.dot(normed, units[0], preferred_element_type=jnp.float32)
        up = jnp.dot(normed, units[1], preferred_element_type=jnp.float32)
        hidden = (jax.nn.silu(gate) * up).astype(jnp.bfloat16)
        hidden = hidden.reshape(2, n_sec // 2, 2, own_rows, half)
        folded = lax.dot_general(
            proj, units[2], (((0,), (0,)), ((), ())), preferred_element_type=jnp.float32
        ).astype(jnp.bfloat16)

        def project(x):
            return lax.dot_general(
                x, folded, (((x.ndim - 1,), (1,)), ((), ())), preferred_element_type=jnp.float32
            )

        send = project(lax.dynamic_index_in_dim(hidden, 1 - core, 2, False)).astype(jnp.bfloat16)
        got = flip(send, section=1)
        kept = project(lax.dynamic_index_in_dim(hidden, core, 2, False)) + got.astype(jnp.float32)
        here = lax.dynamic_index_in_dim(kept, side, 1, False)
        there = lax.dynamic_index_in_dim(kept, 1 - side, 1, False).astype(jnp.bfloat16)
        from_x = flip(there[0], section=2)
        from_z = flip(here[1].astype(jnp.bfloat16), dp=1)
        from_xz = flip(there[1], section=2, dp=1)
        residual = jnp.dot(
            lax.dynamic_slice_in_dim(rows[:tokens], sec * own_rows, own_rows, 0),
            proj,
            preferred_element_type=jnp.float32,
        )
        emb = (
            residual
            + here[0]
            + from_x.astype(jnp.float32)
            + from_z.astype(jnp.float32)
            + from_xz.astype(jnp.float32)
        )
        slide_normed = layer_norm(emb, slide_gain).astype(jnp.bfloat16)

        my_start = seq_at * tokens + sec * own_rows
        span = jnp.arange(own_rows, dtype=jnp.int32)
        if n_seq == 2:
            near = [
                flip(slide_normed, section=2),
                flip(slide_normed, seq=1),
                flip(slide_normed, section=2, seq=1),
            ]
            far = flip(jnp.stack([slide_normed] + near), section=1)
            order = [(s, q) for s in (0, 1) for q in ((0, 0), (2, 0), (0, 1), (2, 1))]
            starts = [(seq_at ^ q[1]) * tokens + (sec ^ q[0] ^ s) * own_rows for s, q in order]
            k_idx = jnp.concatenate([start + span for start in starts])
        else:
            every = lax.all_gather(slide_normed, ("seq", "section"), axis=0, tiled=True)
            count = every.shape[0]
            keys = jnp.concatenate([slide_normed, jnp.roll(every, -my_start, axis=0)[own_rows:]])
            k_idx = (my_start + jnp.arange(count, dtype=jnp.int32)) % count
        count = k_idx.shape[0]

        local_heads = seg_len.shape[0]
        seg_all, rate_all = head_info[0], head_info[1]
        heads = jnp.arange(n_sec * local_heads, dtype=jnp.int32)
        slide, pos = slide_place(lengths[0], k_idx)
        block = slide[None, :] * count + pos[None, :] // seg_all[:, None]
        picked = pos[None, :] % rate_all[:, None] == (heads % rate_all)[:, None]
        k_code = jnp.where(picked, block, -1)
        q_code = block[:, :own_rows].T

        width = w_qkv.shape[2]
        size = width // local_heads
        if n_seq == 2:
            vmem = pl.BlockSpec(memory_space=pltpu.VMEM)
            final = pl.pallas_call(
                lambda *refs: attend_kernel(*refs, heads=local_heads, size=size),
                out_shape=jax.ShapeDtypeStruct((n_sec, own_rows, width), jnp.bfloat16),
                in_specs=[pl.BlockSpec(memory_space=pltpu.SMEM)] + [vmem] * 9,
                out_specs=vmem,
                compiler_params=pltpu.CompilerParams(vmem_limit_bytes=48 * 2**20),
                cost_estimate=pl.CostEstimate(
                    flops=2 * n_sec * count * width * (2 * 768 + 2 * local_heads * own_rows),
                    bytes_accessed=8 * 2**20,
                    transcendentals=n_sec * local_heads * own_rows * count,
                ),
            )(sec[None], slide_normed, *near, far, slide_w, emb, q_code, k_code)
        else:
            total = emb
            for m in range(n_sec):
                at = slice(m * local_heads, (m + 1) * local_heads)

                def by_head(x, matrix):
                    x = jnp.dot(x, matrix.T, preferred_element_type=jnp.float32)
                    return x.astype(jnp.bfloat16).reshape(-1, local_heads, size).transpose(1, 0, 2)

                def one_head(args):
                    q, k, v, q_row, k_row = args
                    scores = jnp.dot(q, k.T, preferred_element_type=jnp.float32) / math.sqrt(size)
                    diag = jnp.arange(own_rows)[:, None] == jnp.arange(count)[None, :]
                    ok = (q_row[:, None] == k_row[None, :]) | diag
                    weight = jax.nn.softmax(jnp.where(ok, scores, NEG), axis=-1)
                    return jnp.dot(weight, v, preferred_element_type=jnp.float32)

                att = lax.map(
                    one_head,
                    (
                        by_head(slide_normed, slide_w[m, 0]),
                        by_head(keys, slide_w[m, 1]),
                        by_head(keys, slide_w[m, 2]),
                        q_code.T[at],
                        k_code[at],
                    ),
                )
                att = att.transpose(1, 0, 2).reshape(own_rows, width).astype(jnp.bfloat16)
                total = total + jnp.dot(att, slide_w[m, 3], preferred_element_type=jnp.float32)
            cut = total.astype(jnp.bfloat16).reshape(own_rows, n_sec, width).transpose(1, 0, 2)
            final = jnp.stack(
                [lax.dynamic_index_in_dim(cut, sec ^ m, 0, False) for m in range(n_sec)]
            )

        pieces = [final[0]] + [flip(final[m], section=m) for m in range(1, n_sec)]
        return jnp.concatenate(absolute(pieces), axis=0)[None]

    return per_device


def solution(mesh):
    placed = (
        P("dp", "seq", "section"),
        P(),
        P(("seq", "dp"), "section"),
        P(("seq", "dp"), "section"),
        P("section", ("seq", "dp")),
        P("section", None),
        P(),
        P(None, None, "section"),
        P("section", None),
        P("dp", None),
        P("section"),
        P("section"),
    )
    shape = mesh.shape
    return jax.shard_map(
        build(shape["section"], shape["seq"], shape["dp"]),
        mesh=mesh,
        in_specs=placed,
        out_specs=P("dp", "seq", "section"),
        check_vma=False,
    )
```

```python
import math

import jax
import jax.numpy as jnp
from jax import lax
from jax.experimental import pallas as pl
from jax.experimental.pallas import tpu as pltpu
from jax.sharding import PartitionSpec as P

NEG = -1e30
AXES = ("section", "seq", "dp")


def layer_norm(rows, gain):
    mean = jnp.mean(rows, axis=-1, keepdims=True)
    centered = rows - mean
    var = jnp.mean(centered * centered, axis=-1, keepdims=True)
    return centered * lax.rsqrt(var + 1e-06) * gain


def slide_place(lengths_row, index):
    ends = jnp.cumsum(lengths_row, dtype=jnp.int32)
    after = index[:, None] >= ends[None, :]
    slide = jnp.sum(after.astype(jnp.int32), axis=1, dtype=jnp.int32)
    before = jnp.sum(jnp.where(after, lengths_row[None, :], 0), axis=1, dtype=jnp.int32)
    return (slide, index - before)


def attend_kernel(sec_ref, mine_ref, *refs, heads, size):
    near, refs = refs[:-8], refs[-8:]
    far_ref, w_any, emb_ref, q_ref, k_ref, out_ref, w_ref, w_sem = refs
    _, parts, width, _ = w_ref.shape
    copies = {}
    for which in (1, 0, 2, 3):
        for m in range(parts):
            copies[which, m] = pltpu.make_async_copy(
                w_any.at[m, which], w_ref.at[which, m], w_sem.at[which, m]
            )
            copies[which, m].start()
    rows = mine_ref.shape[0]
    mine = mine_ref[...]
    keys = jnp.concatenate(
        [mine] + [ref[...] for ref in near] + [far_ref[i] for i in range(far_ref.shape[0])], axis=0
    )
    count = keys.shape[0]
    scale = math.log2(math.e) / math.sqrt(size)

    def matrix(which):
        for m in range(parts):
            copies[which, m].wait()
        return jnp.concatenate([w_ref[which, m] for m in range(parts)], axis=0)

    def project(x, which):
        return lax.dot_general(
            x, matrix(which), (((1,), (1,)), ((), ())), preferred_element_type=jnp.float32
        ).astype(jnp.bfloat16)

    key = project(keys, 1)
    query, value, out_matrix = project(mine, 0), project(keys, 2), matrix(3)
    diag = lax.broadcasted_iota(jnp.int32, (rows, count), 0) == lax.broadcasted_iota(
        jnp.int32, (rows, count), 1
    )
    total = emb_ref[...]
    for m in range(parts):
        lo = m * width // 128 * 128
        hi = -(-(m + 1) * width // 128) * 128
        lane_head = (lax.broadcasted_iota(jnp.int32, (rows, hi - lo), 1) + lo) // size
        q_part = query[:, lo:hi]
        split = jnp.concatenate(
            [
                jnp.where(lane_head == m * heads + h, q_part, jnp.zeros_like(q_part))
                for h in range(heads)
            ],
            axis=0,
        )
        scores = lax.dot_general(
            split, key[:, lo:hi], (((1,), (1,)), ((), ())), preferred_element_type=jnp.float32
        )
        weights, sums = [], []
        for h in range(heads):
            at = m * heads + h
            ok = (q_ref[:, at : at + 1] == k_ref[at : at + 1, :]) | diag
            own = jnp.where(ok, scores[h * rows : (h + 1) * rows], NEG)
            top = jnp.max(own, axis=1, keepdims=True)
            weight = jnp.exp2((own - top) * scale)
            sums.append(jnp.sum(weight, axis=1, keepdims=True))
            weights.append(weight.astype(jnp.bfloat16))
        mixed = jnp.dot(
            jnp.concatenate(weights, axis=0), value[:, lo:hi], preferred_element_type=jnp.float32
        )
        att = jnp.zeros((rows, hi - lo), jnp.float32)
        for h in range(heads):
            att = jnp.where(
                lane_head == m * heads + h, mixed[h * rows : (h + 1) * rows] / sums[h], att
            )
        total = total + jnp.dot(
            att.astype(jnp.bfloat16), out_matrix[lo:hi], preferred_element_type=jnp.float32
        )
    for j in range(parts):
        out_ref[j ^ sec_ref[0]] = total[:, j * width : (j + 1) * width].astype(out_ref.dtype)


def build(n_sec, n_seq, n_dp):
    sizes = {"section": n_sec, "seq": n_seq, "dp": n_dp}

    def flip(x, **masks):
        names = tuple(a for a in AXES if masks.get(a))
        pairs = []
        total = math.prod(sizes[a] for a in names)
        for source in range(total):
            rest, coords = source, []
            for a in reversed(names):
                coords.append(rest % sizes[a])
                rest //= sizes[a]
            target = 0
            for a, c in zip(names, reversed(coords)):
                target = target * sizes[a] + (c ^ masks[a])
            pairs.append((source, target))
        return lax.ppermute(x, names if len(names) > 1 else names[0], pairs)

    def rotate(x, k):
        return lax.ppermute(x, "dp", [(i, (i + k) % n_dp) for i in range(n_dp)])

    def after(x, *others):
        return lax.optimization_barrier((x,) + others)[0]

    def gather_section(x):
        across = flip(x, section=2)
        return [x, flip(after(x, across), section=1), across, flip(across, section=1)]

    def gather_rows(same, other, seq_at, dp_at):
        mats, rows, units = same.shape
        part = jnp.zeros((mats, n_dp * rows, units), same.dtype)
        for k in range(n_dp):
            block = rotate(other if k % 2 else same, k) if k else same
            part = lax.dynamic_update_slice(part, block, (0, ((dp_at - k) % n_dp) * rows, 0))
        return lax.all_gather(part, "seq", axis=1, tiled=True)

    def place_rows(blocks):
        seq_at, dp_at = lax.axis_index("seq"), lax.axis_index("dp")
        mats, rows, units = blocks[0, 0].shape
        whole = jnp.zeros((mats, n_seq * n_dp * rows, units), blocks[0, 0].dtype)
        for (y, k), block in blocks.items():
            at = ((seq_at ^ y) * n_dp + (dp_at - k) % n_dp) * rows
            whole = lax.dynamic_update_slice(whole, block, (0, at, 0))
        return whole

    def per_device(
        tile_feats,
        tile_gain,
        w_gate,
        w_up,
        w_down,
        w_proj,
        slide_gain,
        w_qkv,
        w_out,
        lengths,
        seg_len,
        rate,
    ):
        sec = lax.axis_index("section")
        seq_at = lax.axis_index("seq")
        dp_at = lax.axis_index("dp")
        core, side, odd = sec % 2, sec // 2, dp_at % 2
        mine = tile_feats[0]
        tokens, feats = mine.shape
        own_rows = tokens // n_sec
        half = w_gate.shape[1] // 2

        def absolute(blocks):
            stacked = jnp.stack(blocks)
            return [lax.dynamic_index_in_dim(stacked, sec ^ j, 0, False) for j in range(n_sec)]

        def halves(x, which):
            return lax.dynamic_slice_in_dim(x, which * half, half, x.ndim - 1)

        pair = jnp.stack([w_gate, w_up])
        pair_same, pair_other = halves(pair, odd), halves(pair, 1 - odd)
        down = w_down.T[None]
        down_same, down_other = halves(down, odd), halves(down, 1 - odd)
        ordered = n_seq == 2 and n_dp == 4

        local_heads = seg_len.shape[0]
        info = jnp.concatenate([seg_len // 64, seg_len % 64, rate]).astype(jnp.bfloat16)
        info = jnp.pad(info[None], ((0, 15), (0, feats - 3 * local_heads)))
        beside = flip(mine, dp=1)
        both = jnp.concatenate([mine, beside, info], axis=0)
        blocks = absolute(gather_section(both))
        rows = jnp.concatenate([block[: 2 * tokens] for block in blocks], axis=1)
        info = [
            block[2 * tokens, : 3 * local_heads].astype(jnp.int32).reshape(3, local_heads)
            for block in blocks
        ]
        seg_all = jnp.concatenate([x[0] * 64 + x[1] for x in info])
        rate_all = jnp.concatenate([x[2] for x in info])
        normed = layer_norm(rows.astype(jnp.float32), tile_gain).astype(jnp.bfloat16)

        if ordered:
            g = {(0, 0): pair_same, (0, 1): rotate(pair_other, 1), (0, 3): rotate(pair_other, 3)}
            g[0, 2] = rotate(after(pair_same, g[0, 1]), 2)
            for k in (0, 1, 3, 2):
                g[1, k] = flip(g[0, k], seq=1)
            gate_up = place_rows(g)
            d = {(0, 0): down_same}
            d[0, 1] = rotate(after(down_other, g[0, 2]), 1)
            d[0, 3] = rotate(after(down_other, g[0, 2]), 3)
            d[0, 2] = rotate(after(down_same, d[0, 1], normed), 2)
            d[1, 0] = flip(after(down_same, beside), seq=1)
            d[1, 1], d[1, 3] = flip(d[0, 1], seq=1), flip(d[0, 3], seq=1)
        else:
            gate_up = gather_rows(pair_same, pair_other, seq_at, dp_at)
            down_all = gather_rows(down_same, down_other, seq_at, dp_at)[0]

        proj = lax.all_gather(w_proj, "section", axis=0, tiled=True)
        slide_w = jnp.concatenate([jnp.swapaxes(w_qkv, 1, 2), w_out[None]], axis=0)
        slide_w = lax.all_gather(slide_w, "section", axis=0)

        gate = jnp.dot(normed, gate_up[0], preferred_element_type=jnp.float32)
        up = jnp.dot(normed, gate_up[1], preferred_element_type=jnp.float32)
        hidden = (jax.nn.silu(gate) * up).astype(jnp.bfloat16)
        hidden = hidden.reshape(2, n_sec // 2, 2, own_rows, half)

        def fold(proj_rows, down_rows):
            return lax.dot_general(
                proj_rows, down_rows, (((0,), (0,)), ((), ())), preferred_element_type=jnp.float32
            )

        if ordered:
            folded = fold(proj, place_rows(d)[0])
            d[1, 2] = flip(after(d[0, 2], hidden, folded), seq=1)
            down_rows = d[1, 2].shape[1]
            at = ((1 - seq_at) * n_dp + (dp_at - 2) % n_dp) * down_rows
            folded = folded + fold(lax.dynamic_slice_in_dim(proj, at, down_rows, 0), d[1, 2][0])
        else:
            folded = fold(proj, down_all)
        folded = folded.astype(jnp.bfloat16)

        def project(x):
            return lax.dot_general(
                x, folded, (((x.ndim - 1,), (1,)), ((), ())), preferred_element_type=jnp.float32
            )

        send = project(lax.dynamic_index_in_dim(hidden, 1 - core, 2, False)).astype(jnp.bfloat16)
        got = flip(send, section=1)
        kept = project(lax.dynamic_index_in_dim(hidden, core, 2, False)) + got.astype(jnp.float32)
        here = lax.dynamic_index_in_dim(kept, side, 1, False)
        there = lax.dynamic_index_in_dim(kept, 1 - side, 1, False).astype(jnp.bfloat16)
        from_x = flip(there[0], section=2)
        from_z = flip(here[1].astype(jnp.bfloat16), dp=1)
        from_xz = flip(there[1], section=2, dp=1)
        residual = jnp.dot(
            lax.dynamic_slice_in_dim(rows[:tokens], sec * own_rows, own_rows, 0),
            proj,
            preferred_element_type=jnp.float32,
        )
        emb = (
            residual
            + here[0]
            + from_x.astype(jnp.float32)
            + from_z.astype(jnp.float32)
            + from_xz.astype(jnp.float32)
        )
        slide_normed = layer_norm(emb, slide_gain).astype(jnp.bfloat16)

        my_start = seq_at * tokens + sec * own_rows
        span = jnp.arange(own_rows, dtype=jnp.int32)
        if n_seq == 2:
            near = [
                flip(slide_normed, section=2),
                flip(slide_normed, seq=1),
                flip(slide_normed, section=2, seq=1),
            ]
            far = flip(jnp.stack([slide_normed] + near), section=1)
            order = [(s, q) for s in (0, 1) for q in ((0, 0), (2, 0), (0, 1), (2, 1))]
            starts = [(seq_at ^ q[1]) * tokens + (sec ^ q[0] ^ s) * own_rows for s, q in order]
            k_idx = jnp.concatenate([start + span for start in starts])
        else:
            every = lax.all_gather(slide_normed, ("seq", "section"), axis=0, tiled=True)
            count = every.shape[0]
            keys = jnp.concatenate([slide_normed, jnp.roll(every, -my_start, axis=0)[own_rows:]])
            k_idx = (my_start + jnp.arange(count, dtype=jnp.int32)) % count
        count = k_idx.shape[0]

        heads = jnp.arange(n_sec * local_heads, dtype=jnp.int32)
        slide, pos = slide_place(lengths[0], k_idx)
        block = slide[None, :] * count + pos[None, :] // seg_all[:, None]
        picked = pos[None, :] % rate_all[:, None] == (heads % rate_all)[:, None]
        k_code = jnp.where(picked, block, -1)
        q_code = block[:, :own_rows].T

        width = w_qkv.shape[2]
        size = width // local_heads
        if n_seq == 2:
            vmem = pl.BlockSpec(memory_space=pltpu.VMEM)
            final = pl.pallas_call(
                lambda *refs: attend_kernel(*refs, heads=local_heads, size=size),
                out_shape=jax.ShapeDtypeStruct((n_sec, own_rows, width), jnp.bfloat16),
                in_specs=[pl.BlockSpec(memory_space=pltpu.SMEM)]
                + [vmem] * 5
                + [pl.BlockSpec(memory_space=pl.ANY)]
                + [vmem] * 3,
                out_specs=vmem,
                scratch_shapes=[
                    pltpu.VMEM((4,) + (n_sec,) + slide_w.shape[2:], jnp.bfloat16),
                    pltpu.SemaphoreType.DMA((4, n_sec)),
                ],
                compiler_params=pltpu.CompilerParams(vmem_limit_bytes=48 * 2**20),
                cost_estimate=pl.CostEstimate(
                    flops=2 * n_sec * count * width * (2 * 768 + 2 * local_heads * own_rows),
                    bytes_accessed=8 * 2**20,
                    transcendentals=n_sec * local_heads * own_rows * count,
                ),
            )(sec[None], slide_normed, *near, far, slide_w, emb, q_code, k_code)
        else:
            total = emb
            for m in range(n_sec):
                at = slice(m * local_heads, (m + 1) * local_heads)

                def by_head(x, matrix):
                    x = jnp.dot(x, matrix.T, preferred_element_type=jnp.float32)
                    return x.astype(jnp.bfloat16).reshape(-1, local_heads, size).transpose(1, 0, 2)

                def one_head(args):
                    q, k, v, q_row, k_row = args
                    scores = jnp.dot(q, k.T, preferred_element_type=jnp.float32) / math.sqrt(size)
                    diag = jnp.arange(own_rows)[:, None] == jnp.arange(count)[None, :]
                    ok = (q_row[:, None] == k_row[None, :]) | diag
                    weight = jax.nn.softmax(jnp.where(ok, scores, NEG), axis=-1)
                    return jnp.dot(weight, v, preferred_element_type=jnp.float32)

                att = lax.map(
                    one_head,
                    (
                        by_head(slide_normed, slide_w[m, 0]),
                        by_head(keys, slide_w[m, 1]),
                        by_head(keys, slide_w[m, 2]),
                        q_code.T[at],
                        k_code[at],
                    ),
                )
                att = att.transpose(1, 0, 2).reshape(own_rows, width).astype(jnp.bfloat16)
                total = total + jnp.dot(att, slide_w[m, 3], preferred_element_type=jnp.float32)
            cut = total.astype(jnp.bfloat16).reshape(own_rows, n_sec, width).transpose(1, 0, 2)
            final = jnp.stack(
                [lax.dynamic_index_in_dim(cut, sec ^ m, 0, False) for m in range(n_sec)]
            )

        pieces = [final[0]] + [flip(final[m], section=m) for m in range(1, n_sec)]
        return jnp.concatenate(absolute(pieces), axis=0)[None]

    return per_device


def solution(mesh):
    placed = (
        P("dp", "seq", "section"),
        P(),
        P(("seq", "dp"), "section"),
        P(("seq", "dp"), "section"),
        P("section", ("seq", "dp")),
        P("section", None),
        P(),
        P(None, None, "section"),
        P("section", None),
        P("dp", None),
        P("section"),
        P("section"),
    )
    shape = mesh.shape
    return jax.shard_map(
        build(shape["section"], shape["seq"], shape["dp"]),
        mesh=mesh,
        in_specs=placed,
        out_specs=P("dp", "seq", "section"),
        check_vma=False,
    )
```

```python
import math

import jax
import jax.numpy as jnp
from jax import lax
from jax.experimental import pallas as pl
from jax.experimental.pallas import tpu as pltpu
from jax.sharding import PartitionSpec as P

NEG = -1e30
AXES = ("section", "seq", "dp")


def layer_norm(rows, gain):
    mean = jnp.mean(rows, axis=-1, keepdims=True)
    centered = rows - mean
    var = jnp.mean(centered * centered, axis=-1, keepdims=True)
    return centered * lax.rsqrt(var + 1e-06) * gain


def slide_place(lengths_row, index):
    ends = jnp.cumsum(lengths_row, dtype=jnp.int32)
    after = index[:, None] >= ends[None, :]
    slide = jnp.sum(after.astype(jnp.int32), axis=1, dtype=jnp.int32)
    before = jnp.sum(jnp.where(after, lengths_row[None, :], 0), axis=1, dtype=jnp.int32)
    return (slide, index - before)


def attend_kernel(sec_ref, near_ref, *refs, heads, masks):
    far, refs = refs[:3], refs[3:]
    core_ref, w_ref, out_w_ref, emb_ref, q_ref, k_ref, keep_ref, send_ref = refs
    own = near_ref.shape[0]
    keys = jnp.concatenate(
        [near_ref[...], far[0][...], core_ref[0], core_ref[1], far[1][...], far[2][...]]
        + [core_ref[2], core_ref[3]],
        axis=0,
    )
    count, rows = keys.shape[0], q_ref.shape[0]
    width = w_ref.shape[1]
    size = width // heads
    scale = math.log2(math.e) / math.sqrt(size)

    def project(x, which):
        return lax.dot_general(
            x, w_ref[which], (((1,), (1,)), ((), ())), preferred_element_type=jnp.float32
        ).astype(jnp.bfloat16)

    key, query, value = project(keys, 1), project(keys[:rows], 0), project(keys, 2)
    lane_head = lax.broadcasted_iota(jnp.int32, (rows, width), 1) // size
    diag = lax.broadcasted_iota(jnp.int32, (rows, count), 0) == lax.broadcasted_iota(
        jnp.int32, (rows, count), 1
    )
    att = jnp.zeros((rows, width), jnp.float32)
    for h in range(heads):
        scores = lax.dot_general(
            jnp.where(lane_head == h, query, jnp.zeros_like(query)),
            key,
            (((1,), (1,)), ((), ())),
            preferred_element_type=jnp.float32,
        )
        ok = (q_ref[:, h : h + 1] == k_ref[h : h + 1, :]) | diag
        scores = jnp.where(ok, scores, NEG)
        top = jnp.max(scores, axis=1, keepdims=True)
        weight = jnp.exp2((scores - top) * scale)
        total = jnp.sum(weight, axis=1, keepdims=True)
        mixed = jnp.dot(weight.astype(jnp.bfloat16), value, preferred_element_type=jnp.float32)
        att = jnp.where(lane_head == h, mixed / total, att)
    att = att.astype(jnp.bfloat16)
    for m in range(len(masks)):
        part = jnp.dot(att, out_w_ref[m], preferred_element_type=jnp.float32)
        target = send_ref if m % 2 else keep_ref
        for block, mask in enumerate(masks):
            piece = part[block * own : (block + 1) * own]
            if block == 0:
                piece = piece + emb_ref[m]
            at = pl.multiple_of((mask ^ sec_ref[0]) * own, own)
            target[m // 2, pl.ds(at, own), :] = piece.astype(target.dtype)


def build(n_sec, n_seq, n_dp):
    sizes = {"section": n_sec, "seq": n_seq, "dp": n_dp}

    def flip(x, **masks):
        names = tuple(a for a in AXES if masks.get(a))
        pairs = []
        total = math.prod(sizes[a] for a in names)
        for source in range(total):
            rest, coords = source, []
            for a in reversed(names):
                coords.append(rest % sizes[a])
                rest //= sizes[a]
            target = 0
            for a, c in zip(names, reversed(coords)):
                target = target * sizes[a] + (c ^ masks[a])
            pairs.append((source, target))
        return lax.ppermute(x, names if len(names) > 1 else names[0], pairs)

    def rotate(x, k):
        return lax.ppermute(x, "dp", [(i, (i + k) % n_dp) for i in range(n_dp)])

    def after(x, *others):
        return lax.optimization_barrier((x,) + others)[0]

    def gather_section(x):
        across = flip(x, section=2)
        return [x, flip(after(x, across), section=1), across, flip(across, section=1)]

    def gather_rows(same, other, seq_at, dp_at):
        mats, rows, units = same.shape
        part = jnp.zeros((mats, n_dp * rows, units), same.dtype)
        for k in range(n_dp):
            block = rotate(other if k % 2 else same, k) if k else same
            part = lax.dynamic_update_slice(part, block, (0, ((dp_at - k) % n_dp) * rows, 0))
        return lax.all_gather(part, "seq", axis=1, tiled=True)

    def place_rows(blocks):
        seq_at, dp_at = lax.axis_index("seq"), lax.axis_index("dp")
        mats, rows, units = blocks[0, 0].shape
        whole = jnp.zeros((mats, n_seq * n_dp * rows, units), blocks[0, 0].dtype)
        for (y, k), block in blocks.items():
            at = ((seq_at ^ y) * n_dp + (dp_at - k) % n_dp) * rows
            whole = lax.dynamic_update_slice(whole, block, (0, at, 0))
        return whole

    def per_device(
        tile_feats,
        tile_gain,
        w_gate,
        w_up,
        w_down,
        w_proj,
        slide_gain,
        w_qkv,
        w_out,
        lengths,
        seg_len,
        rate,
    ):
        sec = lax.axis_index("section")
        seq_at = lax.axis_index("seq")
        dp_at = lax.axis_index("dp")
        core, side, odd = sec % 2, sec // 2, dp_at % 2
        mine = tile_feats[0]
        tokens, feats = mine.shape
        own_rows = tokens // n_sec
        half = w_gate.shape[1] // 2

        def absolute(blocks):
            stacked = jnp.stack(blocks)
            return [lax.dynamic_index_in_dim(stacked, sec ^ j, 0, False) for j in range(n_sec)]

        def halves(x, which):
            return lax.dynamic_slice_in_dim(x, which * half, half, x.ndim - 1)

        pair = jnp.stack([w_gate, w_up])
        pair_same, pair_other = halves(pair, odd), halves(pair, 1 - odd)
        down = w_down.T[None]
        down_same, down_other = halves(down, odd), halves(down, 1 - odd)
        ordered = n_seq == 2 and n_dp == 4

        beside = flip(mine, dp=1)
        both = jnp.concatenate([mine, beside], axis=0)
        rows = jnp.concatenate(absolute(gather_section(both)), axis=1)
        normed = layer_norm(rows.astype(jnp.float32), tile_gain).astype(jnp.bfloat16)

        if ordered:
            g = {(0, 0): pair_same, (0, 2): rotate(pair_same, 2)}
            g[0, 1] = rotate(after(pair_other, g[0, 2]), 1)
            g[0, 3] = rotate(after(pair_other, g[0, 2]), 3)
            for k in (0, 2, 1, 3):
                g[1, k] = flip(g[0, k], seq=1)
            gate_up = place_rows(g)
            d = {(0, 0): down_same, (0, 2): rotate(after(down_same, g[0, 1]), 2)}
            d[0, 1] = rotate(after(down_other, d[0, 2], normed), 1)
            d[0, 3] = rotate(after(down_other, d[0, 2], normed), 3)
            for k in (0, 2, 1, 3):
                d[1, k] = flip(d[0, k], seq=1)
        else:
            gate_up = gather_rows(pair_same, pair_other, seq_at, dp_at)
            down_all = gather_rows(down_same, down_other, seq_at, dp_at)[0]

        proj = lax.all_gather(w_proj, "section", axis=0, tiled=True)
        gate = jnp.dot(normed, gate_up[0], preferred_element_type=jnp.float32)
        up = jnp.dot(normed, gate_up[1], preferred_element_type=jnp.float32)
        hidden = (jax.nn.silu(gate) * up).astype(jnp.bfloat16)
        hidden = hidden.reshape(2, n_sec // 2, 2, own_rows, half)

        def fold(proj_rows, down_rows):
            return lax.dot_general(
                proj_rows, down_rows, (((0,), (0,)), ((), ())), preferred_element_type=jnp.float32
            )

        if ordered:
            late = [d.pop((1, 1)), d.pop((1, 3))]
            folded = fold(proj, place_rows(d)[0])
            for k, block in zip((1, 3), late):
                at = ((1 - seq_at) * n_dp + (dp_at - k) % n_dp) * block.shape[1]
                folded = folded + fold(
                    lax.dynamic_slice_in_dim(proj, at, block.shape[1], 0), block[0]
                )
        else:
            folded = fold(proj, down_all)
        folded = folded.astype(jnp.bfloat16)

        def project(x):
            return lax.dot_general(
                x, folded, (((x.ndim - 1,), (1,)), ((), ())), preferred_element_type=jnp.float32
            )

        send = project(lax.dynamic_index_in_dim(hidden, 1 - core, 2, False)).astype(jnp.bfloat16)
        got = flip(send, section=1)
        kept = project(lax.dynamic_index_in_dim(hidden, core, 2, False)) + got.astype(jnp.float32)
        here = lax.dynamic_index_in_dim(kept, side, 1, False)
        there = lax.dynamic_index_in_dim(kept, 1 - side, 1, False).astype(jnp.bfloat16)
        from_x = flip(there[0], section=2)
        from_z = flip(here[1].astype(jnp.bfloat16), dp=1)
        from_xz = flip(there[1], section=2, dp=1)
        residual = jnp.dot(
            lax.dynamic_slice_in_dim(rows[:tokens], sec * own_rows, own_rows, 0),
            proj,
            preferred_element_type=jnp.float32,
        )
        emb = (
            residual
            + here[0]
            + from_x.astype(jnp.float32)
            + from_z.astype(jnp.float32)
            + from_xz.astype(jnp.float32)
        )
        slide_normed = layer_norm(emb, slide_gain).astype(jnp.bfloat16)

        span = jnp.arange(own_rows, dtype=jnp.int32)
        if n_seq == 2:
            near = [
                flip(slide_normed, section=2),
                flip(slide_normed, seq=1),
                flip(slide_normed, section=2, seq=1),
            ]
            from_core = flip(jnp.stack([slide_normed] + near), section=1)
            masks = (0, 2, 1, 3)
            k_idx = jnp.concatenate(
                [(seq_at ^ y) * tokens + (sec ^ m) * own_rows + span for y in (0, 1) for m in masks]
            )
            q_idx = k_idx[:tokens]
        else:
            keys = lax.all_gather(slide_normed, ("seq", "section"), axis=0, tiled=True)
            k_idx = jnp.arange(keys.shape[0], dtype=jnp.int32)
            q_idx = seq_at * tokens + jnp.arange(tokens, dtype=jnp.int32)

        count = k_idx.shape[0]
        local_heads = seg_len.shape[0]
        heads = sec * local_heads + jnp.arange(local_heads, dtype=jnp.int32)

        def codes(index):
            slide, pos = slide_place(lengths[0], index)
            block = slide[None, :] * count + pos[None, :] // seg_len[:, None]
            return block, pos[None, :] % rate[:, None] == (heads % rate)[:, None]

        k_block, picked = codes(k_idx)
        k_code = jnp.where(picked, k_block, -1)
        q_code = codes(q_idx)[0].T

        width = w_qkv.shape[2]
        qkv = jnp.swapaxes(w_qkv, 1, 2)
        out_w = jnp.stack(absolute(list(jnp.split(w_out, n_sec, axis=1))))
        emb_cut = jnp.stack(absolute(list(jnp.split(emb, n_sec, axis=1))))
        if n_seq == 2:
            vmem = pl.BlockSpec(memory_space=pltpu.VMEM)
            keep, send = pl.pallas_call(
                lambda *refs: attend_kernel(*refs, heads=local_heads, masks=masks),
                out_shape=[
                    jax.ShapeDtypeStruct((2, tokens, width), jnp.float32),
                    jax.ShapeDtypeStruct((2, tokens, width), jnp.bfloat16),
                ],
                in_specs=[pl.BlockSpec(memory_space=pltpu.SMEM)] + [vmem] * 10,
                out_specs=[vmem] * 2,
                compiler_params=pltpu.CompilerParams(vmem_limit_bytes=40 * 2**20),
                cost_estimate=pl.CostEstimate(
                    flops=2 * count * width * (3 * 768 + 2 * local_heads * tokens),
                    bytes_accessed=8 * 2**20,
                    transcendentals=local_heads * tokens * count,
                ),
            )(sec[None], slide_normed, *near, from_core, qkv, out_w, emb_cut, q_code, k_code)
        else:

            def by_head(x, matrix):
                x = jnp.dot(x, matrix.T, preferred_element_type=jnp.float32)
                x = x.astype(jnp.bfloat16).reshape(x.shape[0], local_heads, width // local_heads)
                return x.transpose(1, 0, 2)

            def one_head(args):
                q, k, v, q_row, k_row = args
                scores = jnp.dot(q, k.T, preferred_element_type=jnp.float32)
                scores = scores / math.sqrt(width // local_heads)
                ok = (q_row[:, None] == k_row[None, :]) | (q_idx[:, None] == k_idx[None, :])
                weight = jax.nn.softmax(jnp.where(ok, scores, NEG), axis=-1)
                return jnp.dot(weight, v, preferred_element_type=jnp.float32)

            queries = lax.dynamic_slice_in_dim(keys, seq_at * tokens, tokens, 0)
            att = lax.map(
                one_head,
                (by_head(queries, qkv[0]), by_head(keys, qkv[1]), by_head(keys, qkv[2]))
                + (q_code.T, k_code),
            )
            att = att.transpose(1, 0, 2).reshape(tokens, width).astype(jnp.bfloat16)
            parts = jnp.einsum("re,mec->mrc", att, out_w, preferred_element_type=jnp.float32)
            old = lax.dynamic_slice_in_dim(parts, sec * own_rows, own_rows, 1)
            parts = lax.dynamic_update_slice_in_dim(parts, old + emb_cut, sec * own_rows, 1)
            keep, send = parts[0::2], parts[1::2].astype(jnp.bfloat16)

        kept = keep + flip(send, section=1).astype(jnp.float32)
        out = kept[0] + flip(kept[1].astype(jnp.bfloat16), section=2).astype(jnp.float32)
        return out.astype(jnp.bfloat16)[None]

    return per_device


def solution(mesh):
    placed = (
        P("dp", "seq", "section"),
        P(),
        P(("seq", "dp"), "section"),
        P(("seq", "dp"), "section"),
        P("section", ("seq", "dp")),
        P("section", None),
        P(),
        P(None, None, "section"),
        P("section", None),
        P("dp", None),
        P("section"),
        P("section"),
    )
    shape = mesh.shape
    return jax.shard_map(
        build(shape["section"], shape["seq"], shape["dp"]),
        mesh=mesh,
        in_specs=placed,
        out_specs=P("dp", "seq", "section"),
        check_vma=False,
    )
```

```python
import math

import jax
import jax.numpy as jnp
from jax import lax
from jax.experimental import pallas as pl
from jax.experimental.pallas import tpu as pltpu
from jax.sharding import PartitionSpec as P

NEG = -1e30
AXES = ("section", "seq", "dp")


def layer_norm(rows, gain):
    mean = jnp.mean(rows, axis=-1, keepdims=True)
    centered = rows - mean
    var = jnp.mean(centered * centered, axis=-1, keepdims=True)
    return centered * lax.rsqrt(var + 1e-06) * gain


def slide_place(lengths_row, index):
    ends = jnp.cumsum(lengths_row, dtype=jnp.int32)
    after = index[:, None] >= ends[None, :]
    slide = jnp.sum(after.astype(jnp.int32), axis=1, dtype=jnp.int32)
    before = jnp.sum(jnp.where(after, lengths_row[None, :], 0), axis=1, dtype=jnp.int32)
    return (slide, index - before)


def attend_kernel(sec_ref, near_ref, *refs, heads, masks):
    far, refs = refs[:3], refs[3:]
    core_ref, w_ref, out_w_ref, emb_ref, q_ref, k_ref, keep_ref, send_ref = refs
    core, side = sec_ref[0] % 2, sec_ref[0] // 2
    own = near_ref.shape[0]
    keys = jnp.concatenate(
        [near_ref[...], far[0][...], core_ref[0], core_ref[1], far[1][...], far[2][...]]
        + [core_ref[2], core_ref[3]],
        axis=0,
    )
    count, rows = keys.shape[0], q_ref.shape[0]
    width = w_ref.shape[1]
    size = width // heads
    scale = math.log2(math.e) / math.sqrt(size)

    def project(x, which):
        return lax.dot_general(
            x, w_ref[which], (((1,), (1,)), ((), ())), preferred_element_type=jnp.float32
        ).astype(jnp.bfloat16)

    key, query, value = project(keys, 1), project(keys[:rows], 0), project(keys, 2)
    lane_head = lax.broadcasted_iota(jnp.int32, (rows, width), 1) // size
    diag = lax.broadcasted_iota(jnp.int32, (rows, count), 0) == lax.broadcasted_iota(
        jnp.int32, (rows, count), 1
    )
    att = jnp.zeros((rows, width), jnp.float32)
    for h in range(heads):
        scores = lax.dot_general(
            jnp.where(lane_head == h, query, jnp.zeros_like(query)),
            key,
            (((1,), (1,)), ((), ())),
            preferred_element_type=jnp.float32,
        )
        ok = (q_ref[:, h : h + 1] == k_ref[h : h + 1, :]) | diag
        scores = jnp.where(ok, scores, NEG)
        top = jnp.max(scores, axis=1, keepdims=True)
        weight = jnp.exp2((scores - top) * scale)
        total = jnp.sum(weight, axis=1, keepdims=True)
        mixed = jnp.dot(weight.astype(jnp.bfloat16), value, preferred_element_type=jnp.float32)
        att = jnp.where(lane_head == h, mixed / total, att)
    part = jnp.dot(att.astype(jnp.bfloat16), out_w_ref[...], preferred_element_type=jnp.float32)
    for block, mask in enumerate(masks):
        piece = part[block * own : (block + 1) * own]
        if block == 0:
            piece = piece + emb_ref[...]
        at = pl.multiple_of((mask ^ sec_ref[0]) * own, own)
        for j in range(part.shape[1] // width // 2):
            low = piece[:, 2 * j * width : (2 * j + 1) * width]
            high = piece[:, (2 * j + 1) * width : (2 * j + 2) * width]
            keep_ref[j ^ side, pl.ds(at, own), :] = jnp.where(core == 0, low, high)
            send_ref[j ^ side, pl.ds(at, own), :] = jnp.where(core == 0, high, low).astype(
                send_ref.dtype
            )


def build(n_sec, n_seq, n_dp):
    sizes = {"section": n_sec, "seq": n_seq, "dp": n_dp}

    def flip(x, **masks):
        names = tuple(a for a in AXES if masks.get(a))
        pairs = []
        total = math.prod(sizes[a] for a in names)
        for source in range(total):
            rest, coords = source, []
            for a in reversed(names):
                coords.append(rest % sizes[a])
                rest //= sizes[a]
            target = 0
            for a, c in zip(names, reversed(coords)):
                target = target * sizes[a] + (c ^ masks[a])
            pairs.append((source, target))
        return lax.ppermute(x, names if len(names) > 1 else names[0], pairs)

    def rotate(x, k):
        return lax.ppermute(x, "dp", [(i, (i + k) % n_dp) for i in range(n_dp)])

    def after(x, *others):
        return lax.optimization_barrier((x,) + others)[0]

    def absolute(blocks):
        stacked, sec = jnp.stack(blocks), lax.axis_index("section")
        return [lax.dynamic_index_in_dim(stacked, sec ^ j, 0, False) for j in range(n_sec)]

    def gather_section(x):
        across = flip(x, section=2)
        return [x, flip(after(x, across), section=1), across, flip(across, section=1)]

    def gather_rows(same, other, seq_at, dp_at):
        mats, rows, units = same.shape
        part = jnp.zeros((mats, n_dp * rows, units), same.dtype)
        for k in range(n_dp):
            block = rotate(other if k % 2 else same, k) if k else same
            part = lax.dynamic_update_slice(part, block, (0, ((dp_at - k) % n_dp) * rows, 0))
        whole = lax.all_gather(part, "seq", axis=1, tiled=True)
        return jnp.concatenate(absolute(jnp.split(whole, n_sec, axis=1)), axis=1)

    def row_of(y, k, rows):
        sec, seq_at, dp_at = (lax.axis_index(a) for a in AXES)
        block = (seq_at ^ y) * n_dp + (dp_at - k) % n_dp
        each = n_seq * n_dp // n_sec
        return ((block // each ^ sec) * each + block % each) * rows

    def place_rows(blocks):
        first = blocks[0, 2]
        mats, rows, units = first.shape
        whole = after(jnp.zeros((mats, n_seq * n_dp * rows, units), first.dtype), first)
        for (y, k), block in blocks.items():
            whole = lax.dynamic_update_slice(whole, block, (0, row_of(y, k, rows), 0))
        return whole

    def per_device(
        tile_feats,
        tile_gain,
        w_gate,
        w_up,
        w_down,
        w_proj,
        slide_gain,
        w_qkv,
        w_out,
        lengths,
        seg_len,
        rate,
    ):
        sec = lax.axis_index("section")
        seq_at = lax.axis_index("seq")
        dp_at = lax.axis_index("dp")
        core, side, odd = sec % 2, sec // 2, dp_at % 2
        mine = tile_feats[0]
        tokens, feats = mine.shape
        own_rows = tokens // n_sec
        half = w_gate.shape[1] // 2

        def halves(x, which):
            return lax.dynamic_slice_in_dim(x, which * half, half, x.ndim - 1)

        pair = jnp.stack([w_gate, w_up])
        pair_same, pair_other = halves(pair, odd), halves(pair, 1 - odd)
        down = w_down.T[None]
        down_same, down_other = halves(down, odd), halves(down, 1 - odd)
        ordered = n_seq == 2 and n_dp == 4

        beside = flip(mine, dp=1)
        both = jnp.concatenate([mine, beside], axis=0)
        row_blocks = gather_section(both)
        rows = jnp.concatenate(row_blocks, axis=1)
        gain = jnp.concatenate(absolute(jnp.split(tile_gain, n_sec)))
        normed = layer_norm(rows.astype(jnp.float32), gain).astype(jnp.bfloat16)
        proj_blocks = gather_section(w_proj)
        proj = jnp.concatenate(proj_blocks, axis=0)

        if ordered:
            g = {(0, 0): pair_same, (0, 2): rotate(pair_same, 2)}
            g[0, 1] = rotate(after(pair_other, g[0, 2]), 1)
            g[0, 3] = rotate(after(pair_other, g[0, 2]), 3)
            g[1, 0], g[1, 2], g[1, 1] = (flip(g[0, k], seq=1) for k in (0, 2, 1))
            g[1, 3] = flip(after(g[0, 3], normed), seq=1)
            gate_up = place_rows(g)
            d = {(0, 0): down_same, (0, 2): rotate(after(down_same, g[0, 1]), 2)}
            d[1, 0] = flip(down_same, seq=1)
            there = [row_blocks[1], row_blocks[3], proj_blocks[1], proj_blocks[3], d[1, 0]]
            d[0, 1] = rotate(after(down_other, d[0, 2], *there), 1)
            d[0, 3] = rotate(after(down_other, d[0, 2], *there), 3)
            for k in (2, 1, 3):
                d[1, k] = flip(d[0, k], seq=1)
        else:
            gate_up = gather_rows(pair_same, pair_other, seq_at, dp_at)
            down_all = gather_rows(down_same, down_other, seq_at, dp_at)[0]

        gate = jnp.dot(normed, gate_up[0], preferred_element_type=jnp.float32)
        up = jnp.dot(normed, gate_up[1], preferred_element_type=jnp.float32)
        hidden = (jax.nn.silu(gate) * up).astype(jnp.bfloat16)
        hidden = hidden.reshape(2, n_sec // 2, 2, own_rows, half)

        def fold(proj_rows, down_rows):
            return lax.dot_general(
                proj_rows, down_rows, (((0,), (0,)), ((), ())), preferred_element_type=jnp.float32
            )

        if ordered:
            late = [d.pop((1, 1)), d.pop((1, 3))]
            folded = fold(proj, after(place_rows(d)[0], hidden))
            for k, block in zip((1, 3), late):
                at = row_of(1, k, block.shape[1])
                folded = folded + fold(
                    lax.dynamic_slice_in_dim(proj, at, block.shape[1], 0), block[0]
                )
        else:
            folded = fold(proj, down_all)
        folded = folded.astype(jnp.bfloat16)

        def project(x):
            return lax.dot_general(
                x, folded, (((x.ndim - 1,), (1,)), ((), ())), preferred_element_type=jnp.float32
            )

        send = project(lax.dynamic_index_in_dim(hidden, 1 - core, 2, False)).astype(jnp.bfloat16)
        got = flip(send, section=1)
        kept = project(lax.dynamic_index_in_dim(hidden, core, 2, False)) + got.astype(jnp.float32)
        here = lax.dynamic_index_in_dim(kept, side, 1, False)
        there = lax.dynamic_index_in_dim(kept, 1 - side, 1, False).astype(jnp.bfloat16)
        from_x = flip(there[0], section=2)
        from_z = flip(here[1].astype(jnp.bfloat16), dp=1)
        from_xz = flip(there[1], section=2, dp=1)
        residual = jnp.dot(
            lax.dynamic_slice_in_dim(rows[:tokens], sec * own_rows, own_rows, 0),
            proj,
            preferred_element_type=jnp.float32,
        )
        emb = (
            residual
            + here[0]
            + from_x.astype(jnp.float32)
            + from_z.astype(jnp.float32)
            + from_xz.astype(jnp.float32)
        )
        slide_normed = layer_norm(emb, slide_gain).astype(jnp.bfloat16)

        span = jnp.arange(own_rows, dtype=jnp.int32)
        if n_seq == 2:
            near = [
                flip(slide_normed, section=2),
                flip(slide_normed, seq=1),
                flip(slide_normed, section=2, seq=1),
            ]
            from_core = flip(jnp.stack([slide_normed] + near), section=1)
            masks = (0, 2, 1, 3)
            k_idx = jnp.concatenate(
                [(seq_at ^ y) * tokens + (sec ^ m) * own_rows + span for y in (0, 1) for m in masks]
            )
            q_idx = k_idx[:tokens]
        else:
            keys = lax.all_gather(slide_normed, ("seq", "section"), axis=0, tiled=True)
            k_idx = jnp.arange(keys.shape[0], dtype=jnp.int32)
            q_idx = seq_at * tokens + jnp.arange(tokens, dtype=jnp.int32)

        count = k_idx.shape[0]
        local_heads = seg_len.shape[0]
        heads = sec * local_heads + jnp.arange(local_heads, dtype=jnp.int32)

        def codes(index):
            slide, pos = slide_place(lengths[0], index)
            block = slide[None, :] * count + pos[None, :] // seg_len[:, None]
            return block, pos[None, :] % rate[:, None] == (heads % rate)[:, None]

        k_block, picked = codes(k_idx)
        k_code = jnp.where(picked, k_block, -1)
        q_code = codes(q_idx)[0].T

        width = w_qkv.shape[2]
        qkv = jnp.swapaxes(w_qkv, 1, 2)
        if n_seq == 2:
            vmem = pl.BlockSpec(memory_space=pltpu.VMEM)
            keep, send = pl.pallas_call(
                lambda *refs: attend_kernel(*refs, heads=local_heads, masks=masks),
                out_shape=[
                    jax.ShapeDtypeStruct((2, tokens, width), jnp.float32),
                    jax.ShapeDtypeStruct((2, tokens, width), jnp.bfloat16),
                ],
                in_specs=[pl.BlockSpec(memory_space=pltpu.SMEM)] + [vmem] * 10,
                out_specs=[vmem] * 2,
                compiler_params=pltpu.CompilerParams(vmem_limit_bytes=40 * 2**20),
                cost_estimate=pl.CostEstimate(
                    flops=2 * count * width * (3 * 768 + 2 * local_heads * tokens),
                    bytes_accessed=8 * 2**20,
                    transcendentals=local_heads * tokens * count,
                ),
            )(sec[None], slide_normed, *near, from_core, qkv, w_out, emb, q_code, k_code)
        else:

            def by_head(x, matrix):
                x = jnp.dot(x, matrix.T, preferred_element_type=jnp.float32)
                x = x.astype(jnp.bfloat16).reshape(x.shape[0], local_heads, width // local_heads)
                return x.transpose(1, 0, 2)

            def one_head(args):
                q, k, v, q_row, k_row = args
                scores = jnp.dot(q, k.T, preferred_element_type=jnp.float32)
                scores = scores / math.sqrt(width // local_heads)
                ok = (q_row[:, None] == k_row[None, :]) | (q_idx[:, None] == k_idx[None, :])
                weight = jax.nn.softmax(jnp.where(ok, scores, NEG), axis=-1)
                return jnp.dot(weight, v, preferred_element_type=jnp.float32)

            queries = lax.dynamic_slice_in_dim(keys, seq_at * tokens, tokens, 0)
            att = lax.map(
                one_head,
                (by_head(queries, qkv[0]), by_head(keys, qkv[1]), by_head(keys, qkv[2]))
                + (q_code.T, k_code),
            )
            att = att.transpose(1, 0, 2).reshape(tokens, width).astype(jnp.bfloat16)
            parts = jnp.dot(att, w_out, preferred_element_type=jnp.float32)
            old = lax.dynamic_slice_in_dim(parts, sec * own_rows, own_rows, 0)
            parts = lax.dynamic_update_slice_in_dim(parts, old + emb, sec * own_rows, 0)
            parts = jnp.stack(absolute(jnp.split(parts, n_sec, axis=1)))
            keep, send = parts[0::2], parts[1::2].astype(jnp.bfloat16)

        kept = keep + flip(send, section=1).astype(jnp.float32)
        out = kept[0] + flip(kept[1].astype(jnp.bfloat16), section=2).astype(jnp.float32)
        return out.astype(jnp.bfloat16)[None]

    return per_device


def solution(mesh):
    placed = (
        P("dp", "seq", "section"),
        P(),
        P(("seq", "dp"), "section"),
        P(("seq", "dp"), "section"),
        P("section", ("seq", "dp")),
        P("section", None),
        P(),
        P(None, None, "section"),
        P("section", None),
        P("dp", None),
        P("section"),
        P("section"),
    )
    shape = mesh.shape
    return jax.shard_map(
        build(shape["section"], shape["seq"], shape["dp"]),
        mesh=mesh,
        in_specs=placed,
        out_specs=P("dp", "seq", "section"),
        check_vma=False,
    )
```

```python
import math

import jax
import jax.numpy as jnp
from jax import lax
from jax.experimental import pallas as pl
from jax.experimental.pallas import tpu as pltpu
from jax.sharding import PartitionSpec as P

NEG = -1e30
AXES = ("section", "seq", "dp")


def layer_norm(rows, gain):
    mean = jnp.mean(rows, axis=-1, keepdims=True)
    centered = rows - mean
    var = jnp.mean(centered * centered, axis=-1, keepdims=True)
    return centered * lax.rsqrt(var + 1e-06) * gain


def slide_place(lengths_row, index):
    ends = jnp.cumsum(lengths_row, dtype=jnp.int32)
    after = index[:, None] >= ends[None, :]
    slide = jnp.sum(after.astype(jnp.int32), axis=1, dtype=jnp.int32)
    before = jnp.sum(jnp.where(after, lengths_row[None, :], 0), axis=1, dtype=jnp.int32)
    return (slide, index - before)


def attend_kernel(sec_ref, near_ref, *refs, heads, masks):
    far, refs = refs[:3], refs[3:]
    core_ref, w_ref, out_w_ref, emb_ref, q_ref, k_ref, keep_ref, send_ref = refs
    core, side = sec_ref[0] % 2, sec_ref[0] // 2
    own = near_ref.shape[0]
    keys = jnp.concatenate(
        [near_ref[...], far[0][...], core_ref[0], core_ref[1], far[1][...], far[2][...]]
        + [core_ref[2], core_ref[3]],
        axis=0,
    )
    count, rows = keys.shape[0], q_ref.shape[0]
    width = w_ref.shape[1]
    size = width // heads
    scale = math.log2(math.e) / math.sqrt(size)

    def project(x, which):
        return lax.dot_general(
            x, w_ref[which], (((1,), (1,)), ((), ())), preferred_element_type=jnp.float32
        ).astype(jnp.bfloat16)

    key, query, value = project(keys, 1), project(keys[:rows], 0), project(keys, 2)
    lane_head = lax.broadcasted_iota(jnp.int32, (rows, width), 1) // size
    diag = lax.broadcasted_iota(jnp.int32, (rows, count), 0) == lax.broadcasted_iota(
        jnp.int32, (rows, count), 1
    )
    att = jnp.zeros((rows, width), jnp.float32)
    for h in range(heads):
        scores = lax.dot_general(
            jnp.where(lane_head == h, query, jnp.zeros_like(query)),
            key,
            (((1,), (1,)), ((), ())),
            preferred_element_type=jnp.float32,
        )
        ok = (q_ref[:, h : h + 1] == k_ref[h : h + 1, :]) | diag
        scores = jnp.where(ok, scores, NEG)
        top = jnp.max(scores, axis=1, keepdims=True)
        weight = jnp.exp2((scores - top) * scale)
        total = jnp.sum(weight, axis=1, keepdims=True)
        mixed = jnp.dot(weight.astype(jnp.bfloat16), value, preferred_element_type=jnp.float32)
        att = jnp.where(lane_head == h, mixed / total, att)
    part = jnp.dot(
        out_w_ref[...], jnp.transpose(att).astype(jnp.bfloat16), preferred_element_type=jnp.float32
    )
    emb = jnp.transpose(emb_ref[...])
    for block, mask in enumerate(masks):
        piece = part[:, block * own : (block + 1) * own]
        if block == 0:
            piece = piece + emb
        at = pl.ds(pl.multiple_of((mask ^ sec_ref[0]) * own, own), own)
        for j in range(part.shape[0] // width // 2):
            low = piece[2 * j * width : (2 * j + 1) * width]
            high = piece[(2 * j + 1) * width : (2 * j + 2) * width]
            keep_ref[j ^ side, :, at] = jnp.where(core == 0, low, high)
            send_ref[j ^ side, :, at] = jnp.where(core == 0, high, low).astype(send_ref.dtype)


def build(n_sec, n_seq, n_dp):
    sizes = {"section": n_sec, "seq": n_seq, "dp": n_dp}

    def flip(x, **masks):
        names = tuple(a for a in AXES if masks.get(a))
        pairs = []
        total = math.prod(sizes[a] for a in names)
        for source in range(total):
            rest, coords = source, []
            for a in reversed(names):
                coords.append(rest % sizes[a])
                rest //= sizes[a]
            target = 0
            for a, c in zip(names, reversed(coords)):
                target = target * sizes[a] + (c ^ masks[a])
            pairs.append((source, target))
        return lax.ppermute(x, names if len(names) > 1 else names[0], pairs)

    def rotate(x, k):
        return lax.ppermute(x, "dp", [(i, (i + k) % n_dp) for i in range(n_dp)])

    def after(x, *others):
        return lax.optimization_barrier((x,) + others)[0]

    def absolute(blocks):
        stacked, sec = jnp.stack(blocks), lax.axis_index("section")
        return [lax.dynamic_index_in_dim(stacked, sec ^ j, 0, False) for j in range(n_sec)]

    def gather_section(x):
        across = flip(x, section=2)
        return [x, flip(after(x, across), section=1), across, flip(across, section=1)]

    def gather_rows(same, other, seq_at, dp_at):
        mats, rows, units = same.shape
        part = jnp.zeros((mats, n_dp * rows, units), same.dtype)
        for k in range(n_dp):
            block = rotate(other if k % 2 else same, k) if k else same
            part = lax.dynamic_update_slice(part, block, (0, ((dp_at - k) % n_dp) * rows, 0))
        whole = lax.all_gather(part, "seq", axis=1, tiled=True)
        return jnp.concatenate(absolute(jnp.split(whole, n_sec, axis=1)), axis=1)

    def row_of(y, k, rows):
        sec, seq_at, dp_at = (lax.axis_index(a) for a in AXES)
        block = (seq_at ^ y) * n_dp + (dp_at - k) % n_dp
        each = n_seq * n_dp // n_sec
        return ((block // each ^ sec) * each + block % each) * rows

    def place_rows(blocks):
        first = blocks[0, 2]
        mats, rows, units = first.shape
        whole = after(jnp.zeros((mats, n_seq * n_dp * rows, units), first.dtype), first)
        for (y, k), block in blocks.items():
            whole = lax.dynamic_update_slice(whole, block, (0, row_of(y, k, rows), 0))
        return whole

    def per_device(
        tile_feats,
        tile_gain,
        w_gate,
        w_up,
        w_down,
        w_proj,
        slide_gain,
        w_qkv,
        w_out,
        lengths,
        seg_len,
        rate,
    ):
        sec = lax.axis_index("section")
        seq_at = lax.axis_index("seq")
        dp_at = lax.axis_index("dp")
        core, side, odd = sec % 2, sec // 2, dp_at % 2
        mine = tile_feats[0]
        tokens, feats = mine.shape
        own_rows = tokens // n_sec
        half = w_gate.shape[1] // 2

        def halves(x, which):
            return lax.dynamic_slice_in_dim(x, which * half, half, x.ndim - 1)

        pair = jnp.stack([w_gate, w_up])
        pair_same, pair_other = halves(pair, odd), halves(pair, 1 - odd)
        down = w_down.T[None]
        down_same, down_other = halves(down, odd), halves(down, 1 - odd)
        ordered = n_seq == 2 and n_dp == 4

        beside = flip(mine, dp=1)
        both = jnp.concatenate([mine, beside], axis=0)
        row_blocks = gather_section(both)
        rows = jnp.concatenate(row_blocks, axis=1)
        gain = jnp.concatenate(absolute(jnp.split(tile_gain, n_sec)))
        normed = layer_norm(rows.astype(jnp.float32), gain).astype(jnp.bfloat16)
        proj_blocks = gather_section(w_proj)
        proj = jnp.concatenate(proj_blocks, axis=0)

        if n_seq == 2:
            masks = (0, 2, 1, 3)
            span = jnp.arange(own_rows, dtype=jnp.int32)
            k_idx = jnp.concatenate(
                [(seq_at ^ y) * tokens + (sec ^ m) * own_rows + span for y in (0, 1) for m in masks]
            )
            q_idx = k_idx[:tokens]
        else:
            k_idx = jnp.arange(n_seq * tokens, dtype=jnp.int32)
            q_idx = seq_at * tokens + jnp.arange(tokens, dtype=jnp.int32)
        count = k_idx.shape[0]
        local_heads = seg_len.shape[0]
        heads = sec * local_heads + jnp.arange(local_heads, dtype=jnp.int32)

        def codes(index):
            slide, pos = slide_place(lengths[0], index)
            block = slide[None, :] * count + pos[None, :] // seg_len[:, None]
            return block, pos[None, :] % rate[:, None] == (heads % rate)[:, None]

        k_block, picked = codes(k_idx)
        k_code = jnp.where(picked, k_block, -1)
        q_code = codes(q_idx)[0].T

        if ordered:
            g = {(0, 0): pair_same, (0, 2): rotate(pair_same, 2)}
            d = {(0, 0): down_same, (1, 0): flip(down_same, seq=1)}
            g[0, 1] = rotate(after(pair_other, g[0, 2], d[1, 0]), 1)
            g[0, 3] = rotate(after(pair_other, g[0, 2], d[1, 0]), 3)
            g[1, 0], g[1, 2], g[1, 1] = (flip(g[0, k], seq=1) for k in (0, 2, 1))
            g[1, 3] = flip(after(g[0, 3], normed), seq=1)
            gate_up = place_rows(g)
            d[0, 2] = rotate(after(down_same, g[0, 1], proj_blocks[1], proj_blocks[3]), 2)
            there = [row_blocks[1], row_blocks[3], k_code, q_code]
            d[0, 1] = rotate(after(down_other, d[0, 2], *there), 1)
            d[0, 3] = rotate(after(down_other, d[0, 2], *there), 3)
            for k in (2, 1, 3):
                d[1, k] = flip(d[0, k], seq=1)
        else:
            gate_up = gather_rows(pair_same, pair_other, seq_at, dp_at)
            down_all = gather_rows(down_same, down_other, seq_at, dp_at)[0]

        gate = jnp.dot(normed, gate_up[0], preferred_element_type=jnp.float32)
        up = jnp.dot(normed, gate_up[1], preferred_element_type=jnp.float32)
        hidden = (jax.nn.silu(gate) * up).astype(jnp.bfloat16)
        hidden = hidden.reshape(2, n_sec // 2, 2, own_rows, half)

        def fold(proj_rows, down_rows):
            return lax.dot_general(
                proj_rows, down_rows, (((0,), (0,)), ((), ())), preferred_element_type=jnp.float32
            )

        if ordered:
            late = [d.pop((1, 1)), d.pop((1, 3))]
            folded = fold(proj, after(place_rows(d)[0], hidden))
            for k, block in zip((1, 3), late):
                at = row_of(1, k, block.shape[1])
                folded = folded + fold(
                    lax.dynamic_slice_in_dim(proj, at, block.shape[1], 0), block[0]
                )
        else:
            folded = fold(proj, down_all)
        folded = folded.astype(jnp.bfloat16)

        def project(x):
            return lax.dot_general(
                x, folded, (((x.ndim - 1,), (1,)), ((), ())), preferred_element_type=jnp.float32
            )

        send = project(lax.dynamic_index_in_dim(hidden, 1 - core, 2, False)).astype(jnp.bfloat16)
        got = flip(send, section=1)
        kept = project(lax.dynamic_index_in_dim(hidden, core, 2, False)) + got.astype(jnp.float32)
        here = lax.dynamic_index_in_dim(kept, side, 1, False)
        there = lax.dynamic_index_in_dim(kept, 1 - side, 1, False).astype(jnp.bfloat16)
        from_x = flip(there[0], section=2)
        from_z = flip(here[1].astype(jnp.bfloat16), dp=1)
        from_xz = flip(there[1], section=2, dp=1)
        residual = jnp.dot(
            lax.dynamic_slice_in_dim(rows[:tokens], sec * own_rows, own_rows, 0),
            proj,
            preferred_element_type=jnp.float32,
        )
        emb = (
            residual
            + here[0]
            + from_x.astype(jnp.float32)
            + from_z.astype(jnp.float32)
            + from_xz.astype(jnp.float32)
        )
        slide_normed = layer_norm(emb, slide_gain).astype(jnp.bfloat16)

        if n_seq == 2:
            near = [
                flip(slide_normed, section=2),
                flip(slide_normed, seq=1),
                flip(slide_normed, section=2, seq=1),
            ]
            from_core = flip(jnp.stack([slide_normed] + near), section=1)
        else:
            keys = lax.all_gather(slide_normed, ("seq", "section"), axis=0, tiled=True)

        width = w_qkv.shape[2]
        qkv = jnp.swapaxes(w_qkv, 1, 2)
        if n_seq == 2:
            vmem = pl.BlockSpec(memory_space=pltpu.VMEM)
            keep, send = pl.pallas_call(
                lambda *refs: attend_kernel(*refs, heads=local_heads, masks=masks),
                out_shape=[
                    jax.ShapeDtypeStruct((2, width, tokens), jnp.float32),
                    jax.ShapeDtypeStruct((2, width, tokens), jnp.bfloat16),
                ],
                in_specs=[pl.BlockSpec(memory_space=pltpu.SMEM)] + [vmem] * 10,
                out_specs=[vmem] * 2,
                compiler_params=pltpu.CompilerParams(vmem_limit_bytes=40 * 2**20),
                cost_estimate=pl.CostEstimate(
                    flops=2 * count * width * (3 * 768 + 2 * local_heads * tokens),
                    bytes_accessed=8 * 2**20,
                    transcendentals=local_heads * tokens * count,
                ),
            )(sec[None], slide_normed, *near, from_core, qkv, w_out.T, emb, q_code, k_code)
        else:

            def by_head(x, matrix):
                x = jnp.dot(x, matrix.T, preferred_element_type=jnp.float32)
                x = x.astype(jnp.bfloat16).reshape(x.shape[0], local_heads, width // local_heads)
                return x.transpose(1, 0, 2)

            def one_head(args):
                q, k, v, q_row, k_row = args
                scores = jnp.dot(q, k.T, preferred_element_type=jnp.float32)
                scores = scores / math.sqrt(width // local_heads)
                ok = (q_row[:, None] == k_row[None, :]) | (q_idx[:, None] == k_idx[None, :])
                weight = jax.nn.softmax(jnp.where(ok, scores, NEG), axis=-1)
                return jnp.dot(weight, v, preferred_element_type=jnp.float32)

            queries = lax.dynamic_slice_in_dim(keys, seq_at * tokens, tokens, 0)
            att = lax.map(
                one_head,
                (by_head(queries, qkv[0]), by_head(keys, qkv[1]), by_head(keys, qkv[2]))
                + (q_code.T, k_code),
            )
            att = att.transpose(1, 0, 2).reshape(tokens, width).astype(jnp.bfloat16)
            parts = jnp.dot(att, w_out, preferred_element_type=jnp.float32)
            old = lax.dynamic_slice_in_dim(parts, sec * own_rows, own_rows, 0)
            parts = lax.dynamic_update_slice_in_dim(parts, old + emb, sec * own_rows, 0)
            parts = jnp.stack(absolute(jnp.split(parts.T, n_sec, axis=0)))
            keep, send = parts[0::2], parts[1::2].astype(jnp.bfloat16)

        kept = keep + flip(send, section=1).astype(jnp.float32)
        out = kept[0] + flip(kept[1].astype(jnp.bfloat16), section=2).astype(jnp.float32)
        return out.astype(jnp.bfloat16).T[None]

    return per_device


def solution(mesh):
    placed = (
        P("dp", "seq", "section"),
        P(),
        P(("seq", "dp"), "section"),
        P(("seq", "dp"), "section"),
        P("section", ("seq", "dp")),
        P("section", None),
        P(),
        P(None, None, "section"),
        P("section", None),
        P("dp", None),
        P("section"),
        P("section"),
    )
    shape = mesh.shape
    return jax.shard_map(
        build(shape["section"], shape["seq"], shape["dp"]),
        mesh=mesh,
        in_specs=placed,
        out_specs=P("dp", "seq", "section"),
        check_vma=False,
    )
```

```python
import math

import jax
import jax.numpy as jnp
from jax import lax
from jax.experimental import pallas as pl
from jax.experimental.pallas import tpu as pltpu
from jax.sharding import PartitionSpec as P

NEG = -1e30
AXES = ("section", "seq", "dp")


def layer_norm(rows, gain):
    mean = jnp.mean(rows, axis=-1, keepdims=True)
    centered = rows - mean
    var = jnp.mean(centered * centered, axis=-1, keepdims=True)
    return centered * lax.rsqrt(var + 1e-06) * gain


def slide_place(lengths_row, index):
    ends = jnp.cumsum(lengths_row, dtype=jnp.int32)
    after = index[:, None] >= ends[None, :]
    slide = jnp.sum(after.astype(jnp.int32), axis=1, dtype=jnp.int32)
    before = jnp.sum(jnp.where(after, lengths_row[None, :], 0), axis=1, dtype=jnp.int32)
    return (slide, index - before)


def attend_kernel(sec_ref, near_ref, *refs, heads, masks):
    far, refs = refs[:3], refs[3:]
    core_ref, w_ref, out_w_ref, emb_ref, q_ref, k_ref, keep_ref, send_ref = refs
    core, side = sec_ref[0] % 2, sec_ref[0] // 2
    own = near_ref.shape[0]
    keys = jnp.concatenate(
        [near_ref[...], far[0][...], core_ref[0], core_ref[1], far[1][...], far[2][...]]
        + [core_ref[2], core_ref[3]],
        axis=0,
    )
    count, rows = keys.shape[0], q_ref.shape[0]
    width = w_ref.shape[1]
    size = width // heads
    scale = math.log2(math.e) / math.sqrt(size)

    def project(x, which):
        return lax.dot_general(
            x, w_ref[which], (((1,), (1,)), ((), ())), preferred_element_type=jnp.float32
        ).astype(jnp.bfloat16)

    key, query, value = project(keys, 1), project(keys[:rows], 0), project(keys, 2)
    lane_head = lax.broadcasted_iota(jnp.int32, (rows, width), 1) // size
    diag = lax.broadcasted_iota(jnp.int32, (rows, count), 0) == lax.broadcasted_iota(
        jnp.int32, (rows, count), 1
    )
    att = jnp.zeros((rows, width), jnp.float32)
    for h in range(heads):
        scores = lax.dot_general(
            jnp.where(lane_head == h, query, jnp.zeros_like(query)),
            key,
            (((1,), (1,)), ((), ())),
            preferred_element_type=jnp.float32,
        )
        ok = (q_ref[:, h : h + 1] == k_ref[h : h + 1, :]) | diag
        scores = jnp.where(ok, scores, NEG)
        top = jnp.max(scores, axis=1, keepdims=True)
        weight = jnp.exp2((scores - top) * scale)
        total = jnp.sum(weight, axis=1, keepdims=True)
        mixed = jnp.dot(weight.astype(jnp.bfloat16), value, preferred_element_type=jnp.float32)
        att = jnp.where(lane_head == h, mixed / total, att)
    part = jnp.dot(
        out_w_ref[...], jnp.transpose(att).astype(jnp.bfloat16), preferred_element_type=jnp.float32
    )
    emb = jnp.transpose(emb_ref[...])
    for block, mask in enumerate(masks):
        piece = part[:, block * own : (block + 1) * own]
        if block == 0:
            piece = piece + emb
        at = pl.ds(pl.multiple_of((mask ^ sec_ref[0]) * own, own), own)
        for j in range(part.shape[0] // width // 2):
            low = piece[2 * j * width : (2 * j + 1) * width]
            high = piece[(2 * j + 1) * width : (2 * j + 2) * width]
            keep_ref[j ^ side, :, at] = jnp.where(core == 0, low, high)
            send_ref[j ^ side, :, at] = jnp.where(core == 0, high, low).astype(send_ref.dtype)


def norm_kernel(gain_ref, *refs):
    out_ref = refs[-1]
    parts = (len(refs) - 1) // 2
    tokens, width = refs[0].shape
    step = 64
    for pack in range(2):
        pieces = refs[pack * parts : (pack + 1) * parts]

        def rows(i, carry, pack=pack, pieces=pieces):
            at = pl.multiple_of(i * step, step)
            x = [piece[pl.ds(at, step), :].astype(jnp.float32) for piece in pieces]
            total = sum(jnp.sum(part, axis=1, keepdims=True) for part in x)
            x = [part - total / (width * parts) for part in x]
            square = sum(jnp.sum(part * part, axis=1, keepdims=True) for part in x)
            factor = lax.rsqrt(square / (width * parts) + 1e-06)
            to = pl.ds(pl.multiple_of(pack * tokens + i * step, step), step)
            for m, part in enumerate(x):
                out_ref[to, m * width : (m + 1) * width] = (part * factor * gain_ref[m]).astype(
                    out_ref.dtype
                )
            return carry

        lax.fori_loop(0, tokens // step, rows, 0, unroll=2)


def gate_kernel(at_ref, normed_ref, *refs):
    blocks, (out_ref, all_ref, sem) = refs[:-3], refs[-3:]
    rows = blocks[0].shape[1]
    copies = []
    for i, block in enumerate(blocks):
        to = pl.ds(pl.multiple_of(at_ref[i], rows), rows)
        copies.append(pltpu.make_async_copy(block, all_ref.at[:, to, :], sem.at[i]))
        copies[-1].start()
    for copy in copies:
        copy.wait()
    step = 256
    for i in range(normed_ref.shape[0] // step):
        x = normed_ref[i * step : (i + 1) * step, :]
        gate = jnp.dot(x, all_ref[0], preferred_element_type=jnp.float32)
        up = jnp.dot(x, all_ref[1], preferred_element_type=jnp.float32)
        out_ref[i * step : (i + 1) * step, :] = (gate * jax.nn.sigmoid(gate) * up).astype(
            out_ref.dtype
        )


def project_kernel(at_ref, core_ref, hidden_ref, proj_ref, *refs):
    blocks, (send_ref, keep_ref, all_ref, sem) = refs[:-4], refs[-4:]
    rows = blocks[0].shape[1]
    copies = []
    for i, block in enumerate(blocks):
        to = pl.ds(pl.multiple_of(at_ref[i], rows), rows)
        copies.append(pltpu.make_async_copy(block.at[0], all_ref.at[to, :], sem.at[i]))
        copies[-1].start()
    for copy in copies:
        copy.wait()
    folded = jnp.dot(proj_ref[...], all_ref[...], preferred_element_type=jnp.float32)
    folded = folded.astype(jnp.bfloat16)
    packs, sides, _, own, units = hidden_ref.shape
    core = core_ref[0]
    for target, which in ((send_ref, 1 - core), (keep_ref, core)):
        x = jnp.concatenate(
            [hidden_ref[p, x, which] for p in range(packs) for x in range(sides)], axis=0
        )
        x = lax.dot_general(
            x, folded, (((1,), (1,)), ((), ())), preferred_element_type=jnp.float32
        ).astype(target.dtype)
        for p in range(packs):
            for j in range(sides):
                i = p * sides + j
                target[p, j] = x[i * own : (i + 1) * own]


def build(n_sec, n_seq, n_dp):
    sizes = {"section": n_sec, "seq": n_seq, "dp": n_dp}

    def flip(x, **masks):
        names = tuple(a for a in AXES if masks.get(a))
        pairs = []
        total = math.prod(sizes[a] for a in names)
        for source in range(total):
            rest, coords = source, []
            for a in reversed(names):
                coords.append(rest % sizes[a])
                rest //= sizes[a]
            target = 0
            for a, c in zip(names, reversed(coords)):
                target = target * sizes[a] + (c ^ masks[a])
            pairs.append((source, target))
        return lax.ppermute(x, names if len(names) > 1 else names[0], pairs)

    def rotate(x, k):
        return lax.ppermute(x, "dp", [(i, (i + k) % n_dp) for i in range(n_dp)])

    def after(x, *others):
        return lax.optimization_barrier((x,) + others)[0]

    def absolute(blocks):
        stacked, sec = jnp.stack(blocks), lax.axis_index("section")
        return [lax.dynamic_index_in_dim(stacked, sec ^ j, 0, False) for j in range(n_sec)]

    def gather_section(x):
        across = flip(x, section=2)
        return [x, flip(after(x, across), section=1), across, flip(across, section=1)]

    def gather_rows(same, other, seq_at, dp_at):
        mats, rows, units = same.shape
        part = jnp.zeros((mats, n_dp * rows, units), same.dtype)
        for k in range(n_dp):
            block = rotate(other if k % 2 else same, k) if k else same
            part = lax.dynamic_update_slice(part, block, (0, ((dp_at - k) % n_dp) * rows, 0))
        whole = lax.all_gather(part, "seq", axis=1, tiled=True)
        return jnp.concatenate(absolute(jnp.split(whole, n_sec, axis=1)), axis=1)

    def row_of(y, k, rows):
        sec, seq_at, dp_at = (lax.axis_index(a) for a in AXES)
        block = (seq_at ^ y) * n_dp + (dp_at - k) % n_dp
        each = n_seq * n_dp // n_sec
        return ((block // each ^ sec) * each + block % each) * rows

    def per_device(
        tile_feats,
        tile_gain,
        w_gate,
        w_up,
        w_down,
        w_proj,
        slide_gain,
        w_qkv,
        w_out,
        lengths,
        seg_len,
        rate,
    ):
        sec = lax.axis_index("section")
        seq_at = lax.axis_index("seq")
        dp_at = lax.axis_index("dp")
        core, side, odd = sec % 2, sec // 2, dp_at % 2
        mine = tile_feats[0]
        tokens, feats = mine.shape
        own_rows = tokens // n_sec
        half = w_gate.shape[1] // 2

        def halves(x, which):
            return lax.dynamic_slice_in_dim(x, which * half, half, x.ndim - 1)

        pair = jnp.stack([w_gate, w_up])
        pair_same, pair_other = halves(pair, odd), halves(pair, 1 - odd)
        down = w_down.T[None]
        down_same, down_other = halves(down, odd), halves(down, 1 - odd)
        ordered = n_seq == 2 and n_dp == 4

        if n_seq == 2:
            masks = (0, 2, 1, 3)
            span = jnp.arange(own_rows, dtype=jnp.int32)
            k_idx = jnp.concatenate(
                [(seq_at ^ y) * tokens + (sec ^ m) * own_rows + span for y in (0, 1) for m in masks]
            )
            q_idx = k_idx[:tokens]
        else:
            k_idx = jnp.arange(n_seq * tokens, dtype=jnp.int32)
            q_idx = seq_at * tokens + jnp.arange(tokens, dtype=jnp.int32)
        count = k_idx.shape[0]
        local_heads = seg_len.shape[0]
        heads = sec * local_heads + jnp.arange(local_heads, dtype=jnp.int32)

        def codes(index):
            slide, pos = slide_place(lengths[0], index)
            block = slide[None, :] * count + pos[None, :] // seg_len[:, None]
            return block, pos[None, :] % rate[:, None] == (heads % rate)[:, None]

        k_block, picked = codes(k_idx)
        k_code = jnp.where(picked, k_block, -1)
        q_code = codes(q_idx)[0].T

        gain = jnp.stack(absolute(jnp.split(tile_gain, n_sec)))
        own_at = sec * own_rows
        vmem = pl.BlockSpec(memory_space=pltpu.VMEM)
        anywhere = pl.BlockSpec(memory_space=pl.ANY)
        smem = pl.BlockSpec(memory_space=pltpu.SMEM)

        def residual_of(blocks, proj):
            rows = [lax.dynamic_slice_in_dim(block, own_at, own_rows, 0) for block in blocks]
            return jnp.dot(
                jnp.concatenate(rows, axis=1), proj, preferred_element_type=jnp.float32
            )

        if ordered:
            g, d = {(0, 0): pair_same}, {(0, 0): down_same}
            beside = flip(mine, dp=1)
            mine_x = flip(mine, section=2)
            proj_x = flip(w_proj, section=2)
            g[0, 2] = rotate(pair_same, 2)
            g[1, 0] = flip(pair_same, seq=1)
            d[1, 0] = flip(after(down_same, g[1, 0]), seq=1)
            mine_c = flip(after(mine, mine_x), section=1)
            mine_xc = flip(mine_x, section=1)
            beside_x = flip(after(beside, mine_c, mine_xc), section=2)
            for k in (1, 3):
                g[0, k] = rotate(after(pair_other, g[0, 2], d[1, 0], proj_x), k)
            g[1, 2] = flip(g[0, 2], seq=1)
            proj_c = flip(after(w_proj, proj_x), section=1)
            proj_xc = flip(proj_x, section=1)
            beside_c = flip(after(beside, beside_x), section=1)
            beside_xc = flip(beside_x, section=1)
            d[0, 2] = rotate(
                after(down_same, g[0, 1], g[1, 2], proj_c, proj_xc, k_code, q_code), 2
            )
            g[1, 1], g[1, 3] = flip(g[0, 1], seq=1), flip(g[0, 3], seq=1)
            normed = pl.pallas_call(
                norm_kernel,
                out_shape=jax.ShapeDtypeStruct((2 * tokens, feats * n_sec), jnp.bfloat16),
                in_specs=[vmem] * 9,
                out_specs=vmem,
                compiler_params=pltpu.CompilerParams(vmem_limit_bytes=16 * 2**20),
                cost_estimate=pl.CostEstimate(
                    flops=16 * tokens * feats * n_sec,
                    bytes_accessed=8 * tokens * feats * n_sec,
                    transcendentals=2 * tokens,
                ),
            )(
                gain[:, None, :],
                *(mine, mine_c, mine_x, mine_xc),
                *(beside, beside_c, beside_x, beside_xc),
            )
            proj = jnp.concatenate([w_proj, proj_c, proj_x, proj_xc], axis=0)
            proj_t = proj.T
            residual = residual_of((mine, mine_c, mine_x, mine_xc), proj)
            for k in (1, 3):
                d[0, k] = rotate(after(down_other, d[0, 2], normed, proj_t, residual), k)
            d[1, 2], d[1, 1], d[1, 3] = (flip(d[0, k], seq=1) for k in (2, 1, 3))

            order = list(g)
            places = jnp.stack([row_of(y, k, pair.shape[1]) for y, k in order])
            normed = after(normed, d[0, 1], d[0, 3])
            hidden = pl.pallas_call(
                gate_kernel,
                out_shape=jax.ShapeDtypeStruct((2 * tokens, half), jnp.bfloat16),
                in_specs=[smem, vmem] + [anywhere] * len(order),
                out_specs=vmem,
                scratch_shapes=[
                    pltpu.VMEM((2, feats * n_sec, half), jnp.bfloat16),
                    pltpu.SemaphoreType.DMA((len(order),)),
                ],
                compiler_params=pltpu.CompilerParams(vmem_limit_bytes=24 * 2**20),
                cost_estimate=pl.CostEstimate(
                    flops=8 * tokens * feats * n_sec * half,
                    bytes_accessed=8 * 2**20,
                    transcendentals=2 * tokens * half,
                ),
            )(places, normed, *(g[at] for at in order))
            hidden = hidden.reshape(2, n_sec // 2, 2, own_rows, half)
            sums = (2, n_sec // 2, own_rows, proj.shape[1])
            send, kept = pl.pallas_call(
                project_kernel,
                out_shape=[
                    jax.ShapeDtypeStruct(sums, jnp.bfloat16),
                    jax.ShapeDtypeStruct(sums, jnp.float32),
                ],
                in_specs=[smem, smem, vmem, vmem] + [anywhere] * len(order),
                out_specs=[vmem] * 2,
                scratch_shapes=[
                    pltpu.VMEM((feats * n_sec, half), jnp.bfloat16),
                    pltpu.SemaphoreType.DMA((len(order),)),
                ],
                compiler_params=pltpu.CompilerParams(vmem_limit_bytes=24 * 2**20),
                cost_estimate=pl.CostEstimate(
                    flops=2 * half * proj.shape[1] * (feats * n_sec + 2 * tokens),
                    bytes_accessed=8 * 2**20,
                    transcendentals=0,
                ),
            )(places, core[None], hidden, proj_t, *(d[at] for at in order))
        else:
            gate_up = gather_rows(pair_same, pair_other, seq_at, dp_at)
            down_all = gather_rows(down_same, down_other, seq_at, dp_at)[0]
            blocks = gather_section(jnp.concatenate([mine, flip(mine, dp=1)], axis=0))
            proj = jnp.concatenate(gather_section(w_proj), axis=0)
            residual = residual_of([block[:tokens] for block in blocks], proj)
            rows = jnp.concatenate(blocks, axis=1).astype(jnp.float32)
            normed = layer_norm(rows, gain.reshape(-1)).astype(jnp.bfloat16)
            gate = jnp.dot(normed, gate_up[0], preferred_element_type=jnp.float32)
            up = jnp.dot(normed, gate_up[1], preferred_element_type=jnp.float32)
            hidden = (jax.nn.silu(gate) * up).astype(jnp.bfloat16)
            folded = lax.dot_general(
                down_all, proj, (((0,), (0,)), ((), ())), preferred_element_type=jnp.float32
            ).astype(jnp.bfloat16)
            sums = jnp.dot(hidden, folded, preferred_element_type=jnp.float32)
            sums = sums.reshape(2, n_sec // 2, 2, own_rows, proj.shape[1])
            send = lax.dynamic_index_in_dim(sums, 1 - core, 2, False).astype(jnp.bfloat16)
            kept = lax.dynamic_index_in_dim(sums, core, 2, False)

        kept = kept + flip(send, section=1).astype(jnp.float32)
        here = lax.dynamic_index_in_dim(kept, side, 1, False)
        there = lax.dynamic_index_in_dim(kept, 1 - side, 1, False).astype(jnp.bfloat16)
        from_x = flip(there[0], section=2)
        from_z = flip(here[1].astype(jnp.bfloat16), dp=1)
        from_xz = flip(there[1], section=2, dp=1)
        emb = (
            residual
            + here[0]
            + from_x.astype(jnp.float32)
            + from_z.astype(jnp.float32)
            + from_xz.astype(jnp.float32)
        )
        slide_normed = layer_norm(emb, slide_gain).astype(jnp.bfloat16)

        if n_seq == 2:
            near = [
                flip(slide_normed, section=2),
                flip(slide_normed, seq=1),
                flip(slide_normed, section=2, seq=1),
            ]
            from_core = flip(jnp.stack([slide_normed] + near), section=1)
        else:
            keys = lax.all_gather(slide_normed, ("seq", "section"), axis=0, tiled=True)

        width = w_qkv.shape[2]
        qkv = jnp.swapaxes(w_qkv, 1, 2)
        if n_seq == 2:
            keep, send = pl.pallas_call(
                lambda *refs: attend_kernel(*refs, heads=local_heads, masks=masks),
                out_shape=[
                    jax.ShapeDtypeStruct((2, width, tokens), jnp.float32),
                    jax.ShapeDtypeStruct((2, width, tokens), jnp.bfloat16),
                ],
                in_specs=[smem] + [vmem] * 10,
                out_specs=[vmem] * 2,
                compiler_params=pltpu.CompilerParams(vmem_limit_bytes=40 * 2**20),
                cost_estimate=pl.CostEstimate(
                    flops=2 * count * width * (3 * 768 + 2 * local_heads * tokens),
                    bytes_accessed=8 * 2**20,
                    transcendentals=local_heads * tokens * count,
                ),
            )(sec[None], slide_normed, *near, from_core, qkv, w_out.T, emb, q_code, k_code)
        else:

            def by_head(x, matrix):
                x = jnp.dot(x, matrix.T, preferred_element_type=jnp.float32)
                x = x.astype(jnp.bfloat16).reshape(x.shape[0], local_heads, width // local_heads)
                return x.transpose(1, 0, 2)

            def one_head(args):
                q, k, v, q_row, k_row = args
                scores = jnp.dot(q, k.T, preferred_element_type=jnp.float32)
                scores = scores / math.sqrt(width // local_heads)
                ok = (q_row[:, None] == k_row[None, :]) | (q_idx[:, None] == k_idx[None, :])
                weight = jax.nn.softmax(jnp.where(ok, scores, NEG), axis=-1)
                return jnp.dot(weight, v, preferred_element_type=jnp.float32)

            queries = lax.dynamic_slice_in_dim(keys, seq_at * tokens, tokens, 0)
            att = lax.map(
                one_head,
                (by_head(queries, qkv[0]), by_head(keys, qkv[1]), by_head(keys, qkv[2]))
                + (q_code.T, k_code),
            )
            att = att.transpose(1, 0, 2).reshape(tokens, width).astype(jnp.bfloat16)
            parts = jnp.dot(att, w_out, preferred_element_type=jnp.float32)
            old = lax.dynamic_slice_in_dim(parts, sec * own_rows, own_rows, 0)
            parts = lax.dynamic_update_slice_in_dim(parts, old + emb, sec * own_rows, 0)
            parts = jnp.stack(absolute(jnp.split(parts.T, n_sec, axis=0)))
            keep, send = parts[0::2], parts[1::2].astype(jnp.bfloat16)

        kept = keep + flip(send, section=1).astype(jnp.float32)
        out = kept[0] + flip(kept[1].astype(jnp.bfloat16), section=2).astype(jnp.float32)
        return out.astype(jnp.bfloat16).T[None]

    return per_device


def solution(mesh):
    placed = (
        P("dp", "seq", "section"),
        P(),
        P(("seq", "dp"), "section"),
        P(("seq", "dp"), "section"),
        P("section", ("seq", "dp")),
        P("section", None),
        P(),
        P(None, None, "section"),
        P("section", None),
        P("dp", None),
        P("section"),
        P("section"),
    )
    shape = mesh.shape
    return jax.shard_map(
        build(shape["section"], shape["seq"], shape["dp"]),
        mesh=mesh,
        in_specs=placed,
        out_specs=P("dp", "seq", "section"),
        check_vma=False,
    )
```

```python
import math

import jax
import jax.numpy as jnp
from jax import lax
from jax.experimental import pallas as pl
from jax.experimental.pallas import tpu as pltpu
from jax.sharding import PartitionSpec as P

NEG = -1e30
AXES = ("section", "seq", "dp")


def layer_norm(rows, gain):
    mean = jnp.mean(rows, axis=-1, keepdims=True)
    centered = rows - mean
    var = jnp.mean(centered * centered, axis=-1, keepdims=True)
    return centered * lax.rsqrt(var + 1e-06) * gain


def slide_place(lengths_row, index):
    ends = jnp.cumsum(lengths_row, dtype=jnp.int32)
    after = index[:, None] >= ends[None, :]
    slide = jnp.sum(after.astype(jnp.int32), axis=1, dtype=jnp.int32)
    before = jnp.sum(jnp.where(after, lengths_row[None, :], 0), axis=1, dtype=jnp.int32)
    return (slide, index - before)


def attend_kernel(*refs, heads, masks):
    blocks, (w_ref, out_w_ref, emb_ref, code_ref, keep_ref, send_ref) = refs[:-6], refs[-6:]
    sec = lax.axis_index("section")
    core, side = sec % 2, sec // 2
    own = blocks[0].shape[0]
    keys = jnp.concatenate([block[...] for block in blocks], axis=0)
    count, rows = keys.shape[0], own * len(masks)
    q_code = jnp.transpose(code_ref[:, :rows])
    width = w_ref.shape[1]
    size = width // heads
    scale = math.log2(math.e) / math.sqrt(size)

    def project(x, which):
        return lax.dot_general(
            x, w_ref[which], (((1,), (1,)), ((), ())), preferred_element_type=jnp.float32
        ).astype(jnp.bfloat16)

    key, query, value = project(keys, 1), project(keys[:rows], 0), project(keys, 2)
    lane_head = lax.broadcasted_iota(jnp.int32, (rows, width), 1) // size
    diag = lax.broadcasted_iota(jnp.int32, (rows, count), 0) == lax.broadcasted_iota(
        jnp.int32, (rows, count), 1
    )
    att = jnp.zeros((rows, width), jnp.float32)
    for h in range(heads):
        scores = lax.dot_general(
            jnp.where(lane_head == h, query, jnp.zeros_like(query)),
            key,
            (((1,), (1,)), ((), ())),
            preferred_element_type=jnp.float32,
        )
        ok = (q_code[:, h : h + 1] == code_ref[heads + h : heads + h + 1, :]) | diag
        scores = jnp.where(ok, scores, NEG)
        top = jnp.max(scores, axis=1, keepdims=True)
        weight = jnp.exp2((scores - top) * scale)
        total = jnp.sum(weight, axis=1, keepdims=True)
        mixed = jnp.dot(weight.astype(jnp.bfloat16), value, preferred_element_type=jnp.float32)
        att = jnp.where(lane_head == h, mixed / total, att)
    part = jnp.dot(
        out_w_ref[...], jnp.transpose(att).astype(jnp.bfloat16), preferred_element_type=jnp.float32
    )
    emb = jnp.transpose(emb_ref[...])
    for block, mask in enumerate(masks):
        piece = part[:, block * own : (block + 1) * own]
        if block == 0:
            piece = piece + emb
        at = pl.ds(pl.multiple_of((mask ^ sec) * own, own), own)
        for j in range(part.shape[0] // width // 2):
            low = piece[2 * j * width : (2 * j + 1) * width]
            high = piece[(2 * j + 1) * width : (2 * j + 2) * width]
            keep_ref[j ^ side, :, at] = jnp.where(core == 0, low, high)
            send_ref[j ^ side, :, at] = jnp.where(core == 0, high, low).astype(send_ref.dtype)


def norm_kernel(gain_ref, *refs):
    out_ref, sec = refs[-1], lax.axis_index("section")
    parts = (len(refs) - 1) // 2
    tokens, width = refs[0].shape
    step = 64
    for pack in range(2):
        pieces = refs[pack * parts : (pack + 1) * parts]

        def rows(i, carry, pack=pack, pieces=pieces):
            at = pl.multiple_of(i * step, step)
            x = [piece[pl.ds(at, step), :].astype(jnp.float32) for piece in pieces]
            total = sum(jnp.sum(part, axis=1, keepdims=True) for part in x)
            x = [part - total / (width * parts) for part in x]
            square = sum(jnp.sum(part * part, axis=1, keepdims=True) for part in x)
            factor = lax.rsqrt(square / (width * parts) + 1e-06)
            to = pl.ds(pl.multiple_of(pack * tokens + i * step, step), step)
            for m, part in enumerate(x):
                out_ref[to, m * width : (m + 1) * width] = (part * factor * gain_ref[m ^ sec]).astype(
                    out_ref.dtype
                )
            return carry

        lax.fori_loop(0, tokens // step, rows, 0, unroll=2)


def gate_kernel(normed_ref, *refs, places):
    blocks, (out_ref, all_ref, sem) = refs[:-3], refs[-3:]
    rows = blocks[0].shape[1]
    copies = []
    for i, (block, at) in enumerate(zip(blocks, places(rows))):
        to = pl.ds(pl.multiple_of(at, rows), rows)
        copies.append(pltpu.make_async_copy(block, all_ref.at[:, to, :], sem.at[i]))
        copies[-1].start()
    for copy in copies:
        copy.wait()
    step = 256
    for i in range(normed_ref.shape[0] // step):
        x = normed_ref[i * step : (i + 1) * step, :]
        gate = jnp.dot(x, all_ref[0], preferred_element_type=jnp.float32)
        up = jnp.dot(x, all_ref[1], preferred_element_type=jnp.float32)
        out_ref[i * step : (i + 1) * step, :] = (gate * jax.nn.sigmoid(gate) * up).astype(
            out_ref.dtype
        )


def project_kernel(hidden_ref, *refs, places, parts):
    proj, blocks, (send_ref, keep_ref, all_ref, sem) = refs[:parts], refs[parts:-4], refs[-4:]
    rows = blocks[0].shape[1]
    copies = []
    for i, (block, at) in enumerate(zip(blocks, places(rows))):
        to = pl.ds(pl.multiple_of(at, rows), rows)
        copies.append(pltpu.make_async_copy(block.at[0], all_ref.at[to, :], sem.at[i]))
        copies[-1].start()
    for copy in copies:
        copy.wait()
    depth = proj[0].shape[1]
    folded = sum(
        jnp.dot(
            proj[m][...],
            all_ref[m * depth : (m + 1) * depth],
            preferred_element_type=jnp.float32,
        )
        for m in range(parts)
    ).astype(jnp.bfloat16)
    packs, sides, _, own, units = hidden_ref.shape
    core = lax.axis_index("section") % 2
    for target, which in ((send_ref, 1 - core), (keep_ref, core)):
        x = jnp.concatenate(
            [hidden_ref[p, j, which] for p in range(packs) for j in range(sides)], axis=0
        )
        x = lax.dot_general(
            x, folded, (((1,), (1,)), ((), ())), preferred_element_type=jnp.float32
        ).astype(target.dtype)
        for p in range(packs):
            for j in range(sides):
                i = p * sides + j
                target[p, j] = x[i * own : (i + 1) * own]


def build(n_sec, n_seq, n_dp):
    sizes = {"section": n_sec, "seq": n_seq, "dp": n_dp}

    def flip(x, **masks):
        names = tuple(a for a in AXES if masks.get(a))
        pairs = []
        total = math.prod(sizes[a] for a in names)
        for source in range(total):
            rest, coords = source, []
            for a in reversed(names):
                coords.append(rest % sizes[a])
                rest //= sizes[a]
            target = 0
            for a, c in zip(names, reversed(coords)):
                target = target * sizes[a] + (c ^ masks[a])
            pairs.append((source, target))
        return lax.ppermute(x, names if len(names) > 1 else names[0], pairs)

    def rotate(x, k):
        return lax.ppermute(x, "dp", [(i, (i + k) % n_dp) for i in range(n_dp)])

    def after(x, *others):
        return lax.optimization_barrier((x,) + others)[0]

    def absolute(blocks):
        stacked, sec = jnp.stack(blocks), lax.axis_index("section")
        return [lax.dynamic_index_in_dim(stacked, sec ^ j, 0, False) for j in range(n_sec)]

    def gather_section(x):
        across = flip(x, section=2)
        return [x, flip(after(x, across), section=1), across, flip(across, section=1)]

    def gather_rows(same, other, seq_at, dp_at):
        mats, rows, units = same.shape
        part = jnp.zeros((mats, n_dp * rows, units), same.dtype)
        for k in range(n_dp):
            block = rotate(other if k % 2 else same, k) if k else same
            part = lax.dynamic_update_slice(part, block, (0, ((dp_at - k) % n_dp) * rows, 0))
        whole = lax.all_gather(part, "seq", axis=1, tiled=True)
        return jnp.concatenate(absolute(jnp.split(whole, n_sec, axis=1)), axis=1)

    def row_of(y, k, rows):
        sec, seq_at, dp_at = (lax.axis_index(a) for a in AXES)
        block = (seq_at ^ y) * n_dp + (dp_at - k) % n_dp
        each = n_seq * n_dp // n_sec
        return ((block // each ^ sec) * each + block % each) * rows

    def per_device(
        tile_feats,
        tile_gain,
        w_gate,
        w_up,
        w_down,
        w_proj,
        slide_gain,
        w_qkv,
        w_out,
        lengths,
        seg_len,
        rate,
    ):
        sec = lax.axis_index("section")
        seq_at = lax.axis_index("seq")
        dp_at = lax.axis_index("dp")
        core, side, odd = sec % 2, sec // 2, dp_at % 2
        mine = tile_feats[0]
        tokens, feats = mine.shape
        own_rows = tokens // n_sec
        half = w_gate.shape[1] // 2

        def halves(x, which):
            return lax.dynamic_slice_in_dim(x, which * half, half, x.ndim - 1)

        pair = jnp.stack([w_gate, w_up])
        pair_same, pair_other = halves(pair, odd), halves(pair, 1 - odd)
        down = w_down.T[None]
        down_same, down_other = halves(down, odd), halves(down, 1 - odd)
        ordered = n_seq == 2 and n_dp == 4

        if n_seq == 2:
            masks = (0, 2, 1, 3)
            span = jnp.arange(own_rows, dtype=jnp.int32)
            k_idx = jnp.concatenate(
                [(seq_at ^ y) * tokens + (sec ^ m) * own_rows + span for y in (0, 1) for m in masks]
            )
            q_idx = k_idx[:tokens]
        else:
            k_idx = jnp.arange(n_seq * tokens, dtype=jnp.int32)
            q_idx = seq_at * tokens + jnp.arange(tokens, dtype=jnp.int32)
        count = k_idx.shape[0]
        local_heads = seg_len.shape[0]
        heads = sec * local_heads + jnp.arange(local_heads, dtype=jnp.int32)

        def codes(index):
            slide, pos = slide_place(lengths[0], index)
            block = slide[None, :] * count + pos[None, :] // seg_len[:, None]
            return block, pos[None, :] % rate[:, None] == (heads % rate)[:, None]

        k_block, picked = codes(k_idx)
        k_code = jnp.where(picked, k_block, -1)
        code = jnp.concatenate([k_block, k_code], axis=0)

        own_at = sec * own_rows
        vmem = pl.BlockSpec(memory_space=pltpu.VMEM)
        anywhere = pl.BlockSpec(memory_space=pl.ANY)
        whole_vmem = pltpu.CompilerParams(vmem_limit_bytes=58 * 2**20)

        def residual_of(blocks, proj_t):
            return sum(
                lax.dot_general(
                    lax.dynamic_slice_in_dim(block, own_at, own_rows, 0),
                    matrix,
                    (((1,), (1,)), ((), ())),
                    preferred_element_type=jnp.float32,
                )
                for block, matrix in zip(blocks, proj_t)
            )

        if ordered:
            g, d = {(0, 0): pair_same}, {(0, 0): down_same}
            beside = flip(mine, dp=1)
            mine_x = flip(mine, section=2)
            g[0, 2] = rotate(pair_same, 2)
            g[1, 0] = flip(pair_same, seq=1)
            d[1, 0] = flip(after(down_same, g[1, 0]), seq=1)
            mine_c = flip(after(mine, mine_x, g[0, 2]), section=1)
            mine_xc = flip(after(mine_x, g[0, 2]), section=1)
            beside_x = flip(beside, section=2)
            for k in (1, 3):
                g[0, k] = rotate(after(pair_other, g[0, 2], d[1, 0]), k)
            g[1, 2] = flip(g[0, 2], seq=1)
            beside_c = flip(after(beside, beside_x), section=1)
            beside_xc = flip(beside_x, section=1)
            proj = after(w_proj.T, beside)
            proj_x = flip(after(proj, beside_x, g[0, 2]), section=2)
            d[0, 2] = rotate(after(down_same, g[0, 1], g[1, 2], mine_c, mine_xc, code), 2)
            proj_c = flip(after(proj, proj_x), section=1)
            proj_xc = flip(proj_x, section=1)
            g[1, 1], g[1, 3] = flip(g[0, 1], seq=1), flip(g[0, 3], seq=1)
            normed = pl.pallas_call(
                norm_kernel,
                out_shape=jax.ShapeDtypeStruct((2 * tokens, feats * n_sec), jnp.bfloat16),
                in_specs=[vmem] * 9,
                out_specs=vmem,
                compiler_params=whole_vmem,
                cost_estimate=pl.CostEstimate(
                    flops=16 * tokens * feats * n_sec,
                    bytes_accessed=8 * tokens * feats * n_sec,
                    transcendentals=2 * tokens,
                ),
            )(
                tile_gain.reshape(n_sec, 1, feats),
                *(mine, mine_c, mine_x, mine_xc),
                *(beside, beside_c, beside_x, beside_xc),
            )
            proj = [proj, proj_c, proj_x, proj_xc]
            out_w = w_out.T
            for k in (1, 3):
                d[0, k] = rotate(after(down_other, d[0, 2], normed, proj_c, proj_xc, out_w), k)
            d[1, 2], d[1, 1], d[1, 3] = (flip(d[0, k], seq=1) for k in (2, 1, 3))

            order = list(g)

            def places(rows):
                return [row_of(y, k, rows) for y, k in order]

            normed = after(normed, d[0, 1], d[0, 3])
            hidden = pl.pallas_call(
                lambda *refs: gate_kernel(*refs, places=places),
                out_shape=jax.ShapeDtypeStruct((2 * tokens, half), jnp.bfloat16),
                in_specs=[vmem] + [anywhere] * len(order),
                out_specs=vmem,
                scratch_shapes=[
                    pltpu.VMEM((2, feats * n_sec, half), jnp.bfloat16),
                    pltpu.SemaphoreType.DMA((len(order),)),
                ],
                compiler_params=whole_vmem,
                cost_estimate=pl.CostEstimate(
                    flops=8 * tokens * feats * n_sec * half,
                    bytes_accessed=8 * 2**20,
                    transcendentals=2 * tokens * half,
                ),
            )(normed, *(g[at] for at in order))
            hidden = hidden.reshape(2, n_sec // 2, 2, own_rows, half)
            sums = (2, n_sec // 2, own_rows, w_proj.shape[1])
            send, kept = pl.pallas_call(
                lambda *refs: project_kernel(*refs, places=places, parts=n_sec),
                out_shape=[
                    jax.ShapeDtypeStruct(sums, jnp.bfloat16),
                    jax.ShapeDtypeStruct(sums, jnp.float32),
                ],
                in_specs=[vmem] * (1 + n_sec) + [anywhere] * len(order),
                out_specs=[vmem] * 2,
                scratch_shapes=[
                    pltpu.VMEM((feats * n_sec, half), jnp.bfloat16),
                    pltpu.SemaphoreType.DMA((len(order),)),
                ],
                compiler_params=whole_vmem,
                cost_estimate=pl.CostEstimate(
                    flops=2 * half * w_proj.shape[1] * (feats * n_sec + 2 * tokens),
                    bytes_accessed=8 * 2**20,
                    transcendentals=0,
                ),
            )(hidden, *proj, *(d[at] for at in order))
            tiles = [mine, mine_c, mine_x, mine_xc]
        else:
            gate_up = gather_rows(pair_same, pair_other, seq_at, dp_at)
            down_all = gather_rows(down_same, down_other, seq_at, dp_at)[0]
            blocks = gather_section(jnp.concatenate([mine, flip(mine, dp=1)], axis=0))
            proj = gather_section(w_proj.T)
            tiles = [block[:tokens] for block in blocks]
            rows = jnp.concatenate(blocks, axis=1).astype(jnp.float32)
            gain = jnp.concatenate(absolute(jnp.split(tile_gain, n_sec)))
            normed = layer_norm(rows, gain).astype(jnp.bfloat16)
            gate = jnp.dot(normed, gate_up[0], preferred_element_type=jnp.float32)
            up = jnp.dot(normed, gate_up[1], preferred_element_type=jnp.float32)
            hidden = (jax.nn.silu(gate) * up).astype(jnp.bfloat16)
            folded = jnp.dot(
                jnp.concatenate(proj, axis=1), down_all, preferred_element_type=jnp.float32
            ).astype(jnp.bfloat16)
            sums = jnp.dot(hidden, folded.T, preferred_element_type=jnp.float32)
            sums = sums.reshape(2, n_sec // 2, 2, own_rows, w_proj.shape[1])
            send = lax.dynamic_index_in_dim(sums, 1 - core, 2, False).astype(jnp.bfloat16)
            kept = lax.dynamic_index_in_dim(sums, core, 2, False)
            out_w = w_out.T

        kept = kept + flip(send, section=1).astype(jnp.float32)
        here = lax.dynamic_index_in_dim(kept, side, 1, False)
        there = lax.dynamic_index_in_dim(kept, 1 - side, 1, False).astype(jnp.bfloat16)
        from_x = flip(there[0], section=2)
        from_z = flip(here[1].astype(jnp.bfloat16), dp=1)
        from_xz = flip(there[1], section=2, dp=1)
        tiles = [after(tile, kept) for tile in tiles]
        emb = (
            residual_of(tiles, proj)
            + here[0]
            + from_x.astype(jnp.float32)
            + from_z.astype(jnp.float32)
            + from_xz.astype(jnp.float32)
        )
        slide_normed = layer_norm(emb, slide_gain).astype(jnp.bfloat16)

        if n_seq == 2:
            keys = [
                slide_normed,
                flip(slide_normed, section=2),
                flip(slide_normed, seq=1),
                flip(slide_normed, section=2, seq=1),
            ]
            others = [flip(block, section=1) for block in keys]
            keys = keys[:2] + others[:2] + keys[2:] + others[2:]
        else:
            keys = lax.all_gather(slide_normed, ("seq", "section"), axis=0, tiled=True)

        width = w_qkv.shape[2]
        qkv = jnp.swapaxes(w_qkv, 1, 2)
        if n_seq == 2:
            keep, send = pl.pallas_call(
                lambda *refs: attend_kernel(*refs, heads=local_heads, masks=masks),
                out_shape=[
                    jax.ShapeDtypeStruct((2, width, tokens), jnp.float32),
                    jax.ShapeDtypeStruct((2, width, tokens), jnp.bfloat16),
                ],
                in_specs=[vmem] * 12,
                out_specs=[vmem] * 2,
                compiler_params=pltpu.CompilerParams(vmem_limit_bytes=40 * 2**20),
                cost_estimate=pl.CostEstimate(
                    flops=2 * count * width * (3 * 768 + 2 * local_heads * tokens),
                    bytes_accessed=8 * 2**20,
                    transcendentals=local_heads * tokens * count,
                ),
            )(*keys, qkv, out_w, emb, code)
        else:

            def by_head(x, matrix):
                x = jnp.dot(x, matrix.T, preferred_element_type=jnp.float32)
                x = x.astype(jnp.bfloat16).reshape(x.shape[0], local_heads, width // local_heads)
                return x.transpose(1, 0, 2)

            def one_head(args):
                q, k, v, q_row, k_row = args
                scores = jnp.dot(q, k.T, preferred_element_type=jnp.float32)
                scores = scores / math.sqrt(width // local_heads)
                ok = (q_row[:, None] == k_row[None, :]) | (q_idx[:, None] == k_idx[None, :])
                weight = jax.nn.softmax(jnp.where(ok, scores, NEG), axis=-1)
                return jnp.dot(weight, v, preferred_element_type=jnp.float32)

            queries = lax.dynamic_slice_in_dim(keys, seq_at * tokens, tokens, 0)
            att = lax.map(
                one_head,
                (by_head(queries, qkv[0]), by_head(keys, qkv[1]), by_head(keys, qkv[2]))
                + (codes(q_idx)[0], k_code),
            )
            att = att.transpose(1, 0, 2).reshape(tokens, width).astype(jnp.bfloat16)
            parts = jnp.dot(att, w_out, preferred_element_type=jnp.float32)
            old = lax.dynamic_slice_in_dim(parts, sec * own_rows, own_rows, 0)
            parts = lax.dynamic_update_slice_in_dim(parts, old + emb, sec * own_rows, 0)
            parts = jnp.stack(absolute(jnp.split(parts.T, n_sec, axis=0)))
            keep, send = parts[0::2], parts[1::2].astype(jnp.bfloat16)

        kept = keep + flip(send, section=1).astype(jnp.float32)
        out = kept[0] + flip(kept[1].astype(jnp.bfloat16), section=2).astype(jnp.float32)
        return out.astype(jnp.bfloat16).T[None]

    return per_device


def solution(mesh):
    placed = (
        P("dp", "seq", "section"),
        P(),
        P(("seq", "dp"), "section"),
        P(("seq", "dp"), "section"),
        P("section", ("seq", "dp")),
        P("section", None),
        P(),
        P(None, None, "section"),
        P("section", None),
        P("dp", None),
        P("section"),
        P("section"),
    )
    shape = mesh.shape
    return jax.shard_map(
        build(shape["section"], shape["seq"], shape["dp"]),
        mesh=mesh,
        in_specs=placed,
        out_specs=P("dp", "seq", "section"),
        check_vma=False,
    )
```

```python
import math

import jax
import jax.numpy as jnp
from jax import lax
from jax.experimental import pallas as pl
from jax.experimental.pallas import tpu as pltpu
from jax.sharding import PartitionSpec as P

NEG = -1e30
AXES = ("section", "seq", "dp")


def layer_norm(rows, gain):
    mean = jnp.mean(rows, axis=-1, keepdims=True)
    centered = rows - mean
    var = jnp.mean(centered * centered, axis=-1, keepdims=True)
    return centered * lax.rsqrt(var + 1e-06) * gain


def slide_place(lengths_row, index):
    ends = jnp.cumsum(lengths_row, dtype=jnp.int32)
    after = index[:, None] >= ends[None, :]
    slide = jnp.sum(after.astype(jnp.int32), axis=1, dtype=jnp.int32)
    before = jnp.sum(jnp.where(after, lengths_row[None, :], 0), axis=1, dtype=jnp.int32)
    return (slide, index - before)


def attend_kernel(*refs, heads, masks):
    blocks, (w_ref, out_w_ref, emb_ref, code_ref, keep_ref, send_ref) = refs[:-6], refs[-6:]
    sec = lax.axis_index("section")
    core, side = sec % 2, sec // 2
    own = blocks[0].shape[0]
    keys = jnp.concatenate([block[...] for block in blocks], axis=0)
    count, rows = keys.shape[0], own * len(masks)
    q_code = jnp.transpose(code_ref[:, :rows])
    width = w_ref.shape[1]
    size = width // heads
    scale = math.log2(math.e) / math.sqrt(size)

    def project(x, which):
        return lax.dot_general(
            x, w_ref[which], (((1,), (1,)), ((), ())), preferred_element_type=jnp.float32
        ).astype(jnp.bfloat16)

    key, query, value = project(keys, 1), project(keys[:rows], 0), project(keys, 2)
    lane_head = lax.broadcasted_iota(jnp.int32, (rows, width), 1) // size
    diag = lax.broadcasted_iota(jnp.int32, (rows, count), 0) == lax.broadcasted_iota(
        jnp.int32, (rows, count), 1
    )
    att = jnp.zeros((rows, width), jnp.float32)
    for h in range(heads):
        scores = lax.dot_general(
            jnp.where(lane_head == h, query, jnp.zeros_like(query)),
            key,
            (((1,), (1,)), ((), ())),
            preferred_element_type=jnp.float32,
        )
        ok = (q_code[:, h : h + 1] == code_ref[heads + h : heads + h + 1, :]) | diag
        scores = jnp.where(ok, scores, NEG)
        top = jnp.max(scores, axis=1, keepdims=True)
        weight = jnp.exp2((scores - top) * scale)
        total = jnp.sum(weight, axis=1, keepdims=True)
        mixed = jnp.dot(weight.astype(jnp.bfloat16), value, preferred_element_type=jnp.float32)
        att = jnp.where(lane_head == h, mixed / total, att)
    part = jnp.dot(
        out_w_ref[...], jnp.transpose(att).astype(jnp.bfloat16), preferred_element_type=jnp.float32
    )
    emb = jnp.transpose(emb_ref[...])
    for block, mask in enumerate(masks):
        piece = part[:, block * own : (block + 1) * own]
        if block == 0:
            piece = piece + emb
        at = pl.ds(pl.multiple_of((mask ^ sec) * own, own), own)
        for j in range(part.shape[0] // width // 2):
            low = piece[2 * j * width : (2 * j + 1) * width]
            high = piece[(2 * j + 1) * width : (2 * j + 2) * width]
            keep_ref[j ^ side, :, at] = jnp.where(core == 0, low, high)
            send_ref[j ^ side, :, at] = jnp.where(core == 0, high, low).astype(send_ref.dtype)


def build(n_sec, n_seq, n_dp):
    sizes = {"section": n_sec, "seq": n_seq, "dp": n_dp}

    def flip(x, **masks):
        names = tuple(a for a in AXES if masks.get(a))
        pairs = []
        total = math.prod(sizes[a] for a in names)
        for source in range(total):
            rest, coords = source, []
            for a in reversed(names):
                coords.append(rest % sizes[a])
                rest //= sizes[a]
            target = 0
            for a, c in zip(names, reversed(coords)):
                target = target * sizes[a] + (c ^ masks[a])
            pairs.append((source, target))
        return lax.ppermute(x, names if len(names) > 1 else names[0], pairs)

    def rotate(x, k):
        return lax.ppermute(x, "dp", [(i, (i + k) % n_dp) for i in range(n_dp)])

    def after(x, *others):
        return lax.optimization_barrier((x,) + others)[0]

    def absolute(blocks):
        stacked, sec = jnp.stack(blocks), lax.axis_index("section")
        return [lax.dynamic_index_in_dim(stacked, sec ^ j, 0, False) for j in range(n_sec)]

    def gather_section(x):
        across = flip(x, section=2)
        return [x, flip(after(x, across), section=1), across, flip(across, section=1)]

    def gather_rows(same, other, seq_at, dp_at):
        mats, rows, units = same.shape
        part = jnp.zeros((mats, n_dp * rows, units), same.dtype)
        for k in range(n_dp):
            block = rotate(other if k % 2 else same, k) if k else same
            part = lax.dynamic_update_slice(part, block, (0, ((dp_at - k) % n_dp) * rows, 0))
        whole = lax.all_gather(part, "seq", axis=1, tiled=True)
        return jnp.concatenate(absolute(jnp.split(whole, n_sec, axis=1)), axis=1)

    def row_of(y, k, rows):
        sec, seq_at, dp_at = (lax.axis_index(a) for a in AXES)
        block = (seq_at ^ y) * n_dp + (dp_at - k) % n_dp
        each = n_seq * n_dp // n_sec
        return ((block // each ^ sec) * each + block % each) * rows

    def place_rows(blocks):
        first = blocks[0, 2]
        mats, rows, units = first.shape
        whole = after(jnp.zeros((mats, n_seq * n_dp * rows, units), first.dtype), first)
        for (y, k), block in blocks.items():
            whole = lax.dynamic_update_slice(whole, block, (0, row_of(y, k, rows), 0))
        return whole

    def per_device(
        tile_feats,
        tile_gain,
        w_gate,
        w_up,
        w_down,
        w_proj,
        slide_gain,
        w_qkv,
        w_out,
        lengths,
        seg_len,
        rate,
    ):
        sec = lax.axis_index("section")
        seq_at = lax.axis_index("seq")
        dp_at = lax.axis_index("dp")
        core, side, odd = sec % 2, sec // 2, dp_at % 2
        mine = tile_feats[0]
        tokens, feats = mine.shape
        own_rows = tokens // n_sec
        half = w_gate.shape[1] // 2

        def halves(x, which):
            return lax.dynamic_slice_in_dim(x, which * half, half, x.ndim - 1)

        pair = jnp.stack([w_gate, w_up])
        pair_same, pair_other = halves(pair, odd), halves(pair, 1 - odd)
        down = w_down.T[None]
        down_same, down_other = halves(down, odd), halves(down, 1 - odd)
        ordered = n_seq == 2 and n_dp == 4

        if n_seq == 2:
            masks = (0, 2, 1, 3)
            span = jnp.arange(own_rows, dtype=jnp.int32)
            k_idx = jnp.concatenate(
                [(seq_at ^ y) * tokens + (sec ^ m) * own_rows + span for y in (0, 1) for m in masks]
            )
            q_idx = k_idx[:tokens]
        else:
            k_idx = jnp.arange(n_seq * tokens, dtype=jnp.int32)
            q_idx = seq_at * tokens + jnp.arange(tokens, dtype=jnp.int32)
        count = k_idx.shape[0]
        local_heads = seg_len.shape[0]
        heads = sec * local_heads + jnp.arange(local_heads, dtype=jnp.int32)

        def codes(index):
            slide, pos = slide_place(lengths[0], index)
            block = slide[None, :] * count + pos[None, :] // seg_len[:, None]
            return block, pos[None, :] % rate[:, None] == (heads % rate)[:, None]

        k_block, picked = codes(k_idx)
        k_code = jnp.where(picked, k_block, -1)
        code = jnp.concatenate([k_block, k_code], axis=0)

        own_at = sec * own_rows
        gain = jnp.concatenate(absolute(jnp.split(tile_gain, n_sec)))
        out_w = w_out.T

        if ordered:
            g, d = {(0, 0): pair_same}, {(0, 0): down_same}
            beside = flip(mine, dp=1)
            mine_x = flip(mine, section=2)
            g[0, 2] = rotate(pair_same, 2)
            g[1, 0] = flip(pair_same, seq=1)
            d[1, 0] = flip(down_same, seq=1)
            beside_x = flip(beside, section=2)
            for k in (1, 3):
                g[0, k] = rotate(after(pair_other, g[0, 2], d[1, 0]), k)
            g[1, 2] = flip(g[0, 2], seq=1)
            across = after(jnp.concatenate([mine_x, beside_x], axis=0), g[0, 2])
            both = after(jnp.concatenate([mine, beside], axis=0), across)
            both_c, across_c = flip(both, section=1), flip(across, section=1)
            proj_x = flip(after(w_proj, across), section=2)
            d[0, 2] = rotate(after(down_same, g[0, 1], g[1, 2], both_c, across_c, code), 2)
            proj_c = flip(after(w_proj, proj_x, d[0, 2]), section=1)
            proj_xc = flip(after(proj_x, d[0, 2]), section=1)
            rows = jnp.concatenate([both, both_c, across, across_c], axis=1)
            normed = layer_norm(rows.astype(jnp.float32), gain).astype(jnp.bfloat16)
            g[1, 1], g[1, 3] = flip(g[0, 1], seq=1), flip(after(g[0, 3], normed), seq=1)
            gate_up = place_rows(g)
            for k in (1, 3):
                d[0, k] = rotate(after(down_other, d[0, 2], proj_c, proj_xc, out_w), k)
            normed = after(normed, d[0, 1], d[0, 3])
            proj = jnp.concatenate([w_proj, proj_c, proj_x, proj_xc], axis=0)
            for k in (2, 1, 3):
                d[1, k] = flip(d[0, k], seq=1)
        else:
            gate_up = gather_rows(pair_same, pair_other, seq_at, dp_at)
            down_all = gather_rows(down_same, down_other, seq_at, dp_at)[0]
            both = jnp.concatenate([mine, flip(mine, dp=1)], axis=0)
            rows = jnp.concatenate(gather_section(both), axis=1)
            normed = layer_norm(rows.astype(jnp.float32), gain).astype(jnp.bfloat16)
            proj = jnp.concatenate(gather_section(w_proj), axis=0)

        gate = jnp.dot(normed, gate_up[0], preferred_element_type=jnp.float32)
        up = jnp.dot(normed, gate_up[1], preferred_element_type=jnp.float32)
        hidden = (jax.nn.silu(gate) * up).astype(jnp.bfloat16)
        hidden = hidden.reshape(2, n_sec // 2, 2, own_rows, half)

        def fold(proj_rows, down_rows):
            return lax.dot_general(
                proj_rows, down_rows, (((0,), (0,)), ((), ())), preferred_element_type=jnp.float32
            )

        if ordered:
            late = [d.pop((1, 1)), d.pop((1, 3))]
            folded = fold(proj, after(place_rows(d)[0], hidden))
            for k, block in zip((1, 3), late):
                at = row_of(1, k, block.shape[1])
                folded = folded + fold(
                    lax.dynamic_slice_in_dim(proj, at, block.shape[1], 0), block[0]
                )
        else:
            folded = fold(proj, down_all)
        folded = folded.astype(jnp.bfloat16)

        def project(x):
            return lax.dot_general(
                x, folded, (((x.ndim - 1,), (1,)), ((), ())), preferred_element_type=jnp.float32
            )

        send = project(lax.dynamic_index_in_dim(hidden, 1 - core, 2, False)).astype(jnp.bfloat16)
        got = flip(send, section=1)
        kept = project(lax.dynamic_index_in_dim(hidden, core, 2, False)) + got.astype(jnp.float32)
        here = lax.dynamic_index_in_dim(kept, side, 1, False)
        there = lax.dynamic_index_in_dim(kept, 1 - side, 1, False).astype(jnp.bfloat16)
        from_x = flip(there[0], section=2)
        from_z = flip(here[1].astype(jnp.bfloat16), dp=1)
        from_xz = flip(there[1], section=2, dp=1)
        residual = jnp.dot(
            lax.dynamic_slice_in_dim(rows[:tokens], sec * own_rows, own_rows, 0),
            proj,
            preferred_element_type=jnp.float32,
        )
        emb = (
            residual
            + here[0]
            + from_x.astype(jnp.float32)
            + from_z.astype(jnp.float32)
            + from_xz.astype(jnp.float32)
        )
        slide_normed = layer_norm(emb, slide_gain).astype(jnp.bfloat16)

        vmem = pl.BlockSpec(memory_space=pltpu.VMEM)
        if n_seq == 2:
            keys = [
                slide_normed,
                flip(slide_normed, section=2),
                flip(slide_normed, seq=1),
                flip(slide_normed, section=2, seq=1),
            ]
            others = [flip(block, section=1) for block in keys]
            keys = keys[:2] + others[:2] + keys[2:] + others[2:]
        else:
            keys = lax.all_gather(slide_normed, ("seq", "section"), axis=0, tiled=True)

        width = w_qkv.shape[2]
        qkv = jnp.swapaxes(w_qkv, 1, 2)
        if n_seq == 2:
            keep, send = pl.pallas_call(
                lambda *refs: attend_kernel(*refs, heads=local_heads, masks=masks),
                out_shape=[
                    jax.ShapeDtypeStruct((2, width, tokens), jnp.float32),
                    jax.ShapeDtypeStruct((2, width, tokens), jnp.bfloat16),
                ],
                in_specs=[vmem] * 12,
                out_specs=[vmem] * 2,
                compiler_params=pltpu.CompilerParams(vmem_limit_bytes=28 * 2**20),
                cost_estimate=pl.CostEstimate(
                    flops=2 * count * width * (3 * 768 + 2 * local_heads * tokens),
                    bytes_accessed=8 * 2**20,
                    transcendentals=local_heads * tokens * count,
                ),
            )(*keys, qkv, out_w, emb, code)
        else:

            def by_head(x, matrix):
                x = jnp.dot(x, matrix.T, preferred_element_type=jnp.float32)
                x = x.astype(jnp.bfloat16).reshape(x.shape[0], local_heads, width // local_heads)
                return x.transpose(1, 0, 2)

            def one_head(args):
                q, k, v, q_row, k_row = args
                scores = jnp.dot(q, k.T, preferred_element_type=jnp.float32)
                scores = scores / math.sqrt(width // local_heads)
                ok = (q_row[:, None] == k_row[None, :]) | (q_idx[:, None] == k_idx[None, :])
                weight = jax.nn.softmax(jnp.where(ok, scores, NEG), axis=-1)
                return jnp.dot(weight, v, preferred_element_type=jnp.float32)

            queries = lax.dynamic_slice_in_dim(keys, seq_at * tokens, tokens, 0)
            att = lax.map(
                one_head,
                (by_head(queries, qkv[0]), by_head(keys, qkv[1]), by_head(keys, qkv[2]))
                + (codes(q_idx)[0], k_code),
            )
            att = att.transpose(1, 0, 2).reshape(tokens, width).astype(jnp.bfloat16)
            parts = jnp.dot(att, w_out, preferred_element_type=jnp.float32)
            old = lax.dynamic_slice_in_dim(parts, sec * own_rows, own_rows, 0)
            parts = lax.dynamic_update_slice_in_dim(parts, old + emb, sec * own_rows, 0)
            parts = jnp.stack(absolute(jnp.split(parts.T, n_sec, axis=0)))
            keep, send = parts[0::2], parts[1::2].astype(jnp.bfloat16)

        kept = keep + flip(send, section=1).astype(jnp.float32)
        out = kept[0] + flip(kept[1].astype(jnp.bfloat16), section=2).astype(jnp.float32)
        return out.astype(jnp.bfloat16).T[None]

    return per_device


def solution(mesh):
    placed = (
        P("dp", "seq", "section"),
        P(),
        P(("seq", "dp"), "section"),
        P(("seq", "dp"), "section"),
        P("section", ("seq", "dp")),
        P("section", None),
        P(),
        P(None, None, "section"),
        P("section", None),
        P("dp", None),
        P("section"),
        P("section"),
    )
    shape = mesh.shape
    return jax.shard_map(
        build(shape["section"], shape["seq"], shape["dp"]),
        mesh=mesh,
        in_specs=placed,
        out_specs=P("dp", "seq", "section"),
        check_vma=False,
    )
```

```python
import math

import jax
import jax.numpy as jnp
from jax import lax
from jax.experimental import pallas as pl
from jax.experimental.pallas import tpu as pltpu
from jax.sharding import PartitionSpec as P

NEG = -1e30
AXES = ("section", "seq", "dp")


def layer_norm(rows, gain):
    mean = jnp.mean(rows, axis=-1, keepdims=True)
    centered = rows - mean
    var = jnp.mean(centered * centered, axis=-1, keepdims=True)
    return centered * lax.rsqrt(var + 1e-06) * gain


def slide_place(lengths_row, index):
    ends = jnp.cumsum(lengths_row, dtype=jnp.int32)
    after = index[:, None] >= ends[None, :]
    slide = jnp.sum(after.astype(jnp.int32), axis=1, dtype=jnp.int32)
    before = jnp.sum(jnp.where(after, lengths_row[None, :], 0), axis=1, dtype=jnp.int32)
    return (slide, index - before)


def attend_kernel(*refs, heads, masks):
    blocks, (w_ref, out_w_ref, emb_ref, code_ref, keep_ref, send_ref) = refs[:-6], refs[-6:]
    sec = lax.axis_index("section")
    core, side = sec % 2, sec // 2
    own = blocks[0].shape[0]
    keys = jnp.concatenate([block[...] for block in blocks], axis=0)
    count, rows = keys.shape[0], own * len(masks)
    q_code = jnp.transpose(code_ref[:, :rows])
    width = w_ref.shape[1]
    size = width // heads
    scale = math.log2(math.e) / math.sqrt(size)

    def project(x, which):
        return lax.dot_general(
            x, w_ref[which], (((1,), (1,)), ((), ())), preferred_element_type=jnp.float32
        ).astype(jnp.bfloat16)

    key, query, value = project(keys, 1), project(keys[:rows], 0), project(keys, 2)
    lane_head = lax.broadcasted_iota(jnp.int32, (rows, width), 1) // size
    diag = lax.broadcasted_iota(jnp.int32, (rows, count), 0) == lax.broadcasted_iota(
        jnp.int32, (rows, count), 1
    )
    att = jnp.zeros((rows, width), jnp.float32)
    for h in range(heads):
        scores = lax.dot_general(
            jnp.where(lane_head == h, query, jnp.zeros_like(query)),
            key,
            (((1,), (1,)), ((), ())),
            preferred_element_type=jnp.float32,
        )
        ok = (q_code[:, h : h + 1] == code_ref[heads + h : heads + h + 1, :]) | diag
        scores = jnp.where(ok, scores, NEG)
        top = jnp.max(scores, axis=1, keepdims=True)
        weight = jnp.exp2((scores - top) * scale)
        total = jnp.sum(weight, axis=1, keepdims=True)
        mixed = jnp.dot(weight.astype(jnp.bfloat16), value, preferred_element_type=jnp.float32)
        att = jnp.where(lane_head == h, mixed / total, att)
    part = jnp.dot(
        out_w_ref[...], jnp.transpose(att).astype(jnp.bfloat16), preferred_element_type=jnp.float32
    )
    emb = jnp.transpose(emb_ref[...])
    for block, mask in enumerate(masks):
        piece = part[:, block * own : (block + 1) * own]
        if block == 0:
            piece = piece + emb
        at = pl.ds(pl.multiple_of((mask ^ sec) * own, own), own)
        for j in range(part.shape[0] // width // 2):
            low = piece[2 * j * width : (2 * j + 1) * width]
            high = piece[(2 * j + 1) * width : (2 * j + 2) * width]
            keep_ref[j ^ side, :, at] = jnp.where(core == 0, low, high)
            send_ref[j ^ side, :, at] = jnp.where(core == 0, high, low).astype(send_ref.dtype)


def build(n_sec, n_seq, n_dp):
    sizes = {"section": n_sec, "seq": n_seq, "dp": n_dp}

    def flip(x, **masks):
        names = tuple(a for a in AXES if masks.get(a))
        pairs = []
        total = math.prod(sizes[a] for a in names)
        for source in range(total):
            rest, coords = source, []
            for a in reversed(names):
                coords.append(rest % sizes[a])
                rest //= sizes[a]
            target = 0
            for a, c in zip(names, reversed(coords)):
                target = target * sizes[a] + (c ^ masks[a])
            pairs.append((source, target))
        return lax.ppermute(x, names if len(names) > 1 else names[0], pairs)

    def rotate(x, k):
        return lax.ppermute(x, "dp", [(i, (i + k) % n_dp) for i in range(n_dp)])

    def after(x, *others):
        return lax.optimization_barrier((x,) + others)[0]

    def absolute(blocks):
        stacked, sec = jnp.stack(blocks), lax.axis_index("section")
        return [lax.dynamic_index_in_dim(stacked, sec ^ j, 0, False) for j in range(n_sec)]

    def gather_section(x):
        across = flip(x, section=2)
        return [x, flip(after(x, across), section=1), across, flip(across, section=1)]

    def gather_rows(same, other, seq_at, dp_at):
        mats, rows, units = same.shape
        part = jnp.zeros((mats, n_dp * rows, units), same.dtype)
        for k in range(n_dp):
            block = rotate(other if k % 2 else same, k) if k else same
            part = lax.dynamic_update_slice(part, block, (0, ((dp_at - k) % n_dp) * rows, 0))
        whole = lax.all_gather(part, "seq", axis=1, tiled=True)
        return jnp.concatenate(absolute(jnp.split(whole, n_sec, axis=1)), axis=1)

    def row_of(y, k, rows):
        sec, seq_at, dp_at = (lax.axis_index(a) for a in AXES)
        block = (seq_at ^ y) * n_dp + (dp_at - k) % n_dp
        each = n_seq * n_dp // n_sec
        return ((block // each ^ sec) * each + block % each) * rows

    def place_rows(blocks):
        first = blocks[0, 2]
        mats, rows, units = first.shape
        whole = after(jnp.zeros((mats, n_seq * n_dp * rows, units), first.dtype), first)
        for (y, k), block in blocks.items():
            whole = lax.dynamic_update_slice(whole, block, (0, row_of(y, k, rows), 0))
        return whole

    def per_device(
        tile_feats,
        tile_gain,
        w_gate,
        w_up,
        w_down,
        w_proj,
        slide_gain,
        w_qkv,
        w_out,
        lengths,
        seg_len,
        rate,
    ):
        sec = lax.axis_index("section")
        seq_at = lax.axis_index("seq")
        dp_at = lax.axis_index("dp")
        core, side, odd = sec % 2, sec // 2, dp_at % 2
        mine = tile_feats[0]
        tokens, feats = mine.shape
        own_rows = tokens // n_sec
        half = w_gate.shape[1] // 2

        def halves(x, which):
            return lax.dynamic_slice_in_dim(x, which * half, half, x.ndim - 1)

        pair = jnp.stack([w_gate, w_up])
        pair_same, pair_other = halves(pair, odd), halves(pair, 1 - odd)
        down = w_down.T[None]
        down_same, down_other = halves(down, odd), halves(down, 1 - odd)
        ordered = n_seq == 2 and n_dp == 4

        if n_seq == 2:
            masks = (0, 2, 1, 3)
            span = jnp.arange(own_rows, dtype=jnp.int32)
            k_idx = jnp.concatenate(
                [(seq_at ^ y) * tokens + (sec ^ m) * own_rows + span for y in (0, 1) for m in masks]
            )
            q_idx = k_idx[:tokens]
        else:
            k_idx = jnp.arange(n_seq * tokens, dtype=jnp.int32)
            q_idx = seq_at * tokens + jnp.arange(tokens, dtype=jnp.int32)
        count = k_idx.shape[0]
        local_heads = seg_len.shape[0]
        heads = sec * local_heads + jnp.arange(local_heads, dtype=jnp.int32)

        def codes(index):
            slide, pos = slide_place(lengths[0], index)
            block = slide[None, :] * count + pos[None, :] // seg_len[:, None]
            return block, pos[None, :] % rate[:, None] == (heads % rate)[:, None]

        k_block, picked = codes(k_idx)
        k_code = jnp.where(picked, k_block, -1)
        code = jnp.concatenate([k_block, k_code], axis=0)

        own_at = sec * own_rows
        gain = jnp.concatenate(absolute(jnp.split(tile_gain, n_sec)))
        out_w = w_out.T

        if ordered:
            g, d = {(0, 0): pair_same}, {(0, 0): down_same}
            beside = flip(mine, dp=1)
            mine_x = flip(mine, section=2)
            g[0, 2] = rotate(pair_same, 2)
            g[1, 0] = flip(pair_same, seq=1)
            d[1, 0] = flip(down_same, seq=1)
            beside_x = flip(beside, section=2)
            for k in (1, 3):
                g[0, k] = rotate(after(pair_other, g[0, 2], d[1, 0]), k)
            g[1, 2] = flip(g[0, 2], seq=1)
            across = after(jnp.concatenate([mine_x, beside_x], axis=0), g[0, 2])
            both = after(jnp.concatenate([mine, beside], axis=0), across)
            both_c, across_c = flip(both, section=1), flip(across, section=1)
            proj_x = flip(after(w_proj, across), section=2)
            d[0, 2] = rotate(after(down_same, g[0, 1]), 2)
            rows = jnp.concatenate([both, both_c, across, across_c], axis=1)
            normed = layer_norm(rows.astype(jnp.float32), gain).astype(jnp.bfloat16)
            g[1, 1], g[1, 3] = flip(g[0, 1], seq=1), flip(g[0, 3], seq=1)
            gate_up = place_rows(g)
            for k in (1, 3):
                d[0, k] = rotate(after(down_other, d[0, 2], normed, code, out_w), k)
            proj_c = flip(after(w_proj, proj_x, d[0, 1]), section=1)
            proj_xc = flip(after(proj_x, d[0, 1]), section=1)
            proj = jnp.concatenate([w_proj, proj_c, proj_x, proj_xc], axis=0)
            for k in (2, 1, 3):
                d[1, k] = flip(d[0, k], seq=1)
        else:
            gate_up = gather_rows(pair_same, pair_other, seq_at, dp_at)
            down_all = gather_rows(down_same, down_other, seq_at, dp_at)[0]
            both = jnp.concatenate([mine, flip(mine, dp=1)], axis=0)
            rows = jnp.concatenate(gather_section(both), axis=1)
            normed = layer_norm(rows.astype(jnp.float32), gain).astype(jnp.bfloat16)
            proj = jnp.concatenate(gather_section(w_proj), axis=0)

        residual = jnp.dot(
            lax.dynamic_slice_in_dim(rows[:tokens], own_at, own_rows, 0),
            proj,
            preferred_element_type=jnp.float32,
        )
        normed = after(normed, residual)
        gate = jnp.dot(normed, gate_up[0], preferred_element_type=jnp.float32)
        up = jnp.dot(normed, gate_up[1], preferred_element_type=jnp.float32)
        hidden = (jax.nn.silu(gate) * up).astype(jnp.bfloat16)
        hidden = hidden.reshape(2, n_sec // 2, 2, own_rows, half)

        def fold(proj_rows, down_rows):
            return lax.dot_general(
                proj_rows, down_rows, (((0,), (0,)), ((), ())), preferred_element_type=jnp.float32
            )

        if ordered:
            late = [d.pop((1, 1)), d.pop((1, 3))]
            folded = fold(proj, after(place_rows(d)[0], hidden))
            for k, block in zip((1, 3), late):
                at = row_of(1, k, block.shape[1])
                folded = folded + fold(
                    lax.dynamic_slice_in_dim(proj, at, block.shape[1], 0), block[0]
                )
        else:
            folded = fold(proj, down_all)
        folded = folded.astype(jnp.bfloat16)

        def project(x):
            return lax.dot_general(
                x, folded, (((x.ndim - 1,), (1,)), ((), ())), preferred_element_type=jnp.float32
            )

        send = project(lax.dynamic_index_in_dim(hidden, 1 - core, 2, False)).astype(jnp.bfloat16)
        got = flip(send, section=1)
        kept = project(lax.dynamic_index_in_dim(hidden, core, 2, False)) + got.astype(jnp.float32)
        here = lax.dynamic_index_in_dim(kept, side, 1, False)
        there = lax.dynamic_index_in_dim(kept, 1 - side, 1, False).astype(jnp.bfloat16)
        from_x = flip(there[0], section=2)
        from_z = flip(here[1].astype(jnp.bfloat16), dp=1)
        from_xz = flip(there[1], section=2, dp=1)
        emb = (
            residual
            + here[0]
            + from_x.astype(jnp.float32)
            + from_z.astype(jnp.float32)
            + from_xz.astype(jnp.float32)
        )
        slide_normed = layer_norm(emb, slide_gain).astype(jnp.bfloat16)

        vmem = pl.BlockSpec(memory_space=pltpu.VMEM)
        if n_seq == 2:
            keys = [
                slide_normed,
                flip(slide_normed, section=2),
                flip(slide_normed, seq=1),
                flip(slide_normed, section=2, seq=1),
            ]
            others = [flip(block, section=1) for block in keys]
            keys = keys[:2] + others[:2] + keys[2:] + others[2:]
        else:
            keys = lax.all_gather(slide_normed, ("seq", "section"), axis=0, tiled=True)

        width = w_qkv.shape[2]
        qkv = jnp.swapaxes(w_qkv, 1, 2)
        if n_seq == 2:
            keep, send = pl.pallas_call(
                lambda *refs: attend_kernel(*refs, heads=local_heads, masks=masks),
                out_shape=[
                    jax.ShapeDtypeStruct((2, width, tokens), jnp.float32),
                    jax.ShapeDtypeStruct((2, width, tokens), jnp.bfloat16),
                ],
                in_specs=[vmem] * 12,
                out_specs=[vmem] * 2,
                compiler_params=pltpu.CompilerParams(vmem_limit_bytes=28 * 2**20),
                cost_estimate=pl.CostEstimate(
                    flops=2 * count * width * (3 * 768 + 2 * local_heads * tokens),
                    bytes_accessed=8 * 2**20,
                    transcendentals=local_heads * tokens * count,
                ),
            )(*keys, qkv, out_w, emb, code)
        else:

            def by_head(x, matrix):
                x = jnp.dot(x, matrix.T, preferred_element_type=jnp.float32)
                x = x.astype(jnp.bfloat16).reshape(x.shape[0], local_heads, width // local_heads)
                return x.transpose(1, 0, 2)

            def one_head(args):
                q, k, v, q_row, k_row = args
                scores = jnp.dot(q, k.T, preferred_element_type=jnp.float32)
                scores = scores / math.sqrt(width // local_heads)
                ok = (q_row[:, None] == k_row[None, :]) | (q_idx[:, None] == k_idx[None, :])
                weight = jax.nn.softmax(jnp.where(ok, scores, NEG), axis=-1)
                return jnp.dot(weight, v, preferred_element_type=jnp.float32)

            queries = lax.dynamic_slice_in_dim(keys, seq_at * tokens, tokens, 0)
            att = lax.map(
                one_head,
                (by_head(queries, qkv[0]), by_head(keys, qkv[1]), by_head(keys, qkv[2]))
                + (codes(q_idx)[0], k_code),
            )
            att = att.transpose(1, 0, 2).reshape(tokens, width).astype(jnp.bfloat16)
            parts = jnp.dot(att, w_out, preferred_element_type=jnp.float32)
            old = lax.dynamic_slice_in_dim(parts, sec * own_rows, own_rows, 0)
            parts = lax.dynamic_update_slice_in_dim(parts, old + emb, sec * own_rows, 0)
            parts = jnp.stack(absolute(jnp.split(parts.T, n_sec, axis=0)))
            keep, send = parts[0::2], parts[1::2].astype(jnp.bfloat16)

        kept = keep + flip(send, section=1).astype(jnp.float32)
        out = kept[0] + flip(kept[1].astype(jnp.bfloat16), section=2).astype(jnp.float32)
        return out.astype(jnp.bfloat16).T[None]

    return per_device


def solution(mesh):
    placed = (
        P("dp", "seq", "section"),
        P(),
        P(("seq", "dp"), "section"),
        P(("seq", "dp"), "section"),
        P("section", ("seq", "dp")),
        P("section", None),
        P(),
        P(None, None, "section"),
        P("section", None),
        P("dp", None),
        P("section"),
        P("section"),
    )
    shape = mesh.shape
    return jax.shard_map(
        build(shape["section"], shape["seq"], shape["dp"]),
        mesh=mesh,
        in_specs=placed,
        out_specs=P("dp", "seq", "section"),
        check_vma=False,
    )
```

```python
import math

import jax
import jax.numpy as jnp
from jax import lax
from jax.experimental import pallas as pl
from jax.experimental.pallas import tpu as pltpu
from jax.sharding import PartitionSpec as P

NEG = -1e30
AXES = ("section", "seq", "dp")


def layer_norm(rows, gain):
    mean = jnp.mean(rows, axis=-1, keepdims=True)
    centered = rows - mean
    var = jnp.mean(centered * centered, axis=-1, keepdims=True)
    return centered * lax.rsqrt(var + 1e-06) * gain


def slide_place(lengths_row, index):
    ends = jnp.cumsum(lengths_row, dtype=jnp.int32)
    after = index[:, None] >= ends[None, :]
    slide = jnp.sum(after.astype(jnp.int32), axis=1, dtype=jnp.int32)
    before = jnp.sum(jnp.where(after, lengths_row[None, :], 0), axis=1, dtype=jnp.int32)
    return (slide, index - before)


def attend_kernel(*refs, heads, masks):
    blocks, (w_ref, out_w_ref, emb_ref, code_ref, keep_ref, send_ref) = refs[:-6], refs[-6:]
    sec = lax.axis_index("section")
    core, side = sec % 2, sec // 2
    own = blocks[0].shape[0]
    keys = jnp.concatenate([block[...] for block in blocks], axis=0)
    count, rows = keys.shape[0], own * len(masks)
    q_code = jnp.transpose(code_ref[:, :rows])
    width = w_ref.shape[1]
    size = width // heads
    scale = math.log2(math.e) / math.sqrt(size)

    def project(x, which):
        return lax.dot_general(
            x, w_ref[which], (((1,), (1,)), ((), ())), preferred_element_type=jnp.float32
        ).astype(jnp.bfloat16)

    key, query, value = project(keys, 1), project(keys[:rows], 0), project(keys, 2)
    lane_head = lax.broadcasted_iota(jnp.int32, (rows, width), 1) // size
    diag = lax.broadcasted_iota(jnp.int32, (rows, count), 0) == lax.broadcasted_iota(
        jnp.int32, (rows, count), 1
    )
    att = jnp.zeros((rows, width), jnp.float32)
    for h in range(heads):
        scores = lax.dot_general(
            jnp.where(lane_head == h, query, jnp.zeros_like(query)),
            key,
            (((1,), (1,)), ((), ())),
            preferred_element_type=jnp.float32,
        )
        ok = (q_code[:, h : h + 1] == code_ref[heads + h : heads + h + 1, :]) | diag
        scores = jnp.where(ok, scores, NEG)
        top = jnp.max(scores, axis=1, keepdims=True)
        weight = jnp.exp2((scores - top) * scale)
        total = jnp.sum(weight, axis=1, keepdims=True)
        mixed = jnp.dot(weight.astype(jnp.bfloat16), value, preferred_element_type=jnp.float32)
        att = jnp.where(lane_head == h, mixed / total, att)
    part = jnp.dot(
        out_w_ref[...], jnp.transpose(att).astype(jnp.bfloat16), preferred_element_type=jnp.float32
    )
    emb = jnp.transpose(emb_ref[...])
    for block, mask in enumerate(masks):
        piece = part[:, block * own : (block + 1) * own]
        if block == 0:
            piece = piece + emb
        at = pl.ds(pl.multiple_of((mask ^ sec) * own, own), own)
        for j in range(part.shape[0] // width // 2):
            low = piece[2 * j * width : (2 * j + 1) * width]
            high = piece[(2 * j + 1) * width : (2 * j + 2) * width]
            keep_ref[j ^ side, :, at] = jnp.where(core == 0, low, high)
            send_ref[j ^ side, :, at] = jnp.where(core == 0, high, low).astype(send_ref.dtype)


def build(n_sec, n_seq, n_dp):
    sizes = {"section": n_sec, "seq": n_seq, "dp": n_dp}

    def flip(x, **masks):
        names = tuple(a for a in AXES if masks.get(a))
        pairs = []
        total = math.prod(sizes[a] for a in names)
        for source in range(total):
            rest, coords = source, []
            for a in reversed(names):
                coords.append(rest % sizes[a])
                rest //= sizes[a]
            target = 0
            for a, c in zip(names, reversed(coords)):
                target = target * sizes[a] + (c ^ masks[a])
            pairs.append((source, target))
        return lax.ppermute(x, names if len(names) > 1 else names[0], pairs)

    def rotate(x, k):
        return lax.ppermute(x, "dp", [(i, (i + k) % n_dp) for i in range(n_dp)])

    def after(x, *others):
        return lax.optimization_barrier((x,) + others)[0]

    def absolute(blocks):
        stacked, sec = jnp.stack(blocks), lax.axis_index("section")
        return [lax.dynamic_index_in_dim(stacked, sec ^ j, 0, False) for j in range(n_sec)]

    def gather_section(x):
        across = flip(x, section=2)
        return [x, flip(after(x, across), section=1), across, flip(across, section=1)]

    def gather_rows(same, other, seq_at, dp_at):
        mats, rows, units = same.shape
        part = jnp.zeros((mats, n_dp * rows, units), same.dtype)
        for k in range(n_dp):
            block = rotate(other if k % 2 else same, k) if k else same
            part = lax.dynamic_update_slice(part, block, (0, ((dp_at - k) % n_dp) * rows, 0))
        whole = lax.all_gather(part, "seq", axis=1, tiled=True)
        return jnp.concatenate(absolute(jnp.split(whole, n_sec, axis=1)), axis=1)

    def row_of(y, k, rows):
        sec, seq_at, dp_at = (lax.axis_index(a) for a in AXES)
        block = (seq_at ^ y) * n_dp + (dp_at - k) % n_dp
        each = n_seq * n_dp // n_sec
        return ((block // each ^ sec) * each + block % each) * rows

    def place_rows(blocks):
        first = blocks[0, 2]
        mats, rows, units = first.shape
        whole = after(jnp.zeros((mats, n_seq * n_dp * rows, units), first.dtype), first)
        for (y, k), block in blocks.items():
            whole = lax.dynamic_update_slice(whole, block, (0, row_of(y, k, rows), 0))
        return whole

    def per_device(
        tile_feats,
        tile_gain,
        w_gate,
        w_up,
        w_down,
        w_proj,
        slide_gain,
        w_qkv,
        w_out,
        lengths,
        seg_len,
        rate,
    ):
        sec = lax.axis_index("section")
        seq_at = lax.axis_index("seq")
        dp_at = lax.axis_index("dp")
        core, side, odd = sec % 2, sec // 2, dp_at % 2
        mine = tile_feats[0]
        tokens, feats = mine.shape
        own_rows = tokens // n_sec
        half = w_gate.shape[1] // 2

        def halves(x, which):
            return lax.dynamic_slice_in_dim(x, which * half, half, x.ndim - 1)

        pair = jnp.stack([w_gate, w_up])
        pair_same, pair_other = halves(pair, odd), halves(pair, 1 - odd)
        down = w_down.T[None]
        down_same, down_other = halves(down, odd), halves(down, 1 - odd)
        ordered = n_seq == 2 and n_dp == 4

        if n_seq == 2:
            masks = (0, 2, 1, 3)
            span = jnp.arange(own_rows, dtype=jnp.int32)
            k_idx = jnp.concatenate(
                [(seq_at ^ y) * tokens + (sec ^ m) * own_rows + span for y in (0, 1) for m in masks]
            )
            q_idx = k_idx[:tokens]
        else:
            k_idx = jnp.arange(n_seq * tokens, dtype=jnp.int32)
            q_idx = seq_at * tokens + jnp.arange(tokens, dtype=jnp.int32)
        count = k_idx.shape[0]
        local_heads = seg_len.shape[0]
        heads = sec * local_heads + jnp.arange(local_heads, dtype=jnp.int32)

        def codes(index):
            slide, pos = slide_place(lengths[0], index)
            block = slide[None, :] * count + pos[None, :] // seg_len[:, None]
            return block, pos[None, :] % rate[:, None] == (heads % rate)[:, None]

        k_block, picked = codes(k_idx)
        k_code = jnp.where(picked, k_block, -1)
        code = jnp.concatenate([k_block, k_code], axis=0)

        own_at = sec * own_rows
        gain = jnp.concatenate(absolute(jnp.split(tile_gain, n_sec)))
        out_w = w_out.T

        if ordered:
            g, d = {(0, 0): pair_same}, {(0, 0): down_same}
            beside = flip(mine, dp=1)
            mine_x = flip(mine, section=2)
            g[0, 2] = rotate(pair_same, 2)
            g[1, 0] = flip(pair_same, seq=1)
            d[1, 0] = flip(down_same, seq=1)
            proj_x = flip(after(w_proj, mine_x), section=2)
            g[0, 1] = rotate(after(pair_other, g[0, 2], g[1, 0], d[1, 0], mine_x), 1)
            beside_x = flip(after(beside, g[0, 2]), section=2)
            g[1, 2] = flip(g[0, 2], seq=1)
            g[0, 3] = rotate(after(pair_other, g[0, 1], g[1, 2]), 3)
            across = jnp.concatenate([after(mine_x, g[0, 1]), beside_x], axis=0)
            both = after(jnp.concatenate([mine, beside], axis=0), across)
            both_c, across_c = flip(both, section=1), flip(across, section=1)
            rows = jnp.concatenate([both, both_c, across, across_c], axis=1)
            normed = layer_norm(rows.astype(jnp.float32), gain).astype(jnp.bfloat16)
            g[1, 1] = flip(g[0, 1], seq=1)
            g[1, 3] = flip(g[0, 3], seq=1)
            gate_up = place_rows(g)
            for k in (1, 3):
                d[0, k] = rotate(after(down_other, g[0, 3], g[1, 1], both_c, across_c, code, out_w), k)
            d[0, 2] = rotate(after(down_same, d[0, 1], d[0, 3], g[1, 3], normed), 2)
            proj_c = flip(after(w_proj, proj_x, both_c), section=1)
            proj_xc = flip(after(proj_x, across_c), section=1)
            proj = jnp.concatenate([w_proj, proj_c, proj_x, proj_xc], axis=0)
            d[1, 1], d[1, 3] = flip(d[0, 1], seq=1), flip(d[0, 3], seq=1)
        else:
            gate_up = gather_rows(pair_same, pair_other, seq_at, dp_at)
            down_all = gather_rows(down_same, down_other, seq_at, dp_at)[0]
            both = jnp.concatenate([mine, flip(mine, dp=1)], axis=0)
            rows = jnp.concatenate(gather_section(both), axis=1)
            normed = layer_norm(rows.astype(jnp.float32), gain).astype(jnp.bfloat16)
            proj = jnp.concatenate(gather_section(w_proj), axis=0)

        residual = jnp.dot(
            lax.dynamic_slice_in_dim(rows[:tokens], own_at, own_rows, 0),
            proj,
            preferred_element_type=jnp.float32,
        )
        normed = after(normed, residual)
        gate = jnp.dot(normed, gate_up[0], preferred_element_type=jnp.float32)
        up = jnp.dot(normed, gate_up[1], preferred_element_type=jnp.float32)
        hidden = (jax.nn.silu(gate) * up).astype(jnp.bfloat16)
        hidden = hidden.reshape(2, n_sec // 2, 2, own_rows, half)

        def fold(proj_rows, down_rows):
            return lax.dot_general(
                proj_rows, down_rows, (((0,), (0,)), ((), ())), preferred_element_type=jnp.float32
            )

        if ordered:
            late = flip(after(d[0, 2], d[1, 1], d[1, 3], hidden), seq=1)[0]
            folded = fold(proj, after(place_rows(d)[0], hidden))
            at = row_of(1, 2, late.shape[0])
            folded = folded + fold(
                lax.dynamic_slice_in_dim(proj, at, late.shape[0], 0), late
            )
        else:
            folded = fold(proj, down_all)
        folded = folded.astype(jnp.bfloat16)

        def project(x):
            return lax.dot_general(
                x, folded, (((x.ndim - 1,), (1,)), ((), ())), preferred_element_type=jnp.float32
            )

        send = project(lax.dynamic_index_in_dim(hidden, 1 - core, 2, False)).astype(jnp.bfloat16)
        got = flip(send, section=1)
        kept = after(project(lax.dynamic_index_in_dim(hidden, core, 2, False)), send)
        kept = kept + got.astype(jnp.float32)
        here = lax.dynamic_index_in_dim(kept, side, 1, False)
        there = lax.dynamic_index_in_dim(kept, 1 - side, 1, False).astype(jnp.bfloat16)
        from_x = flip(there[0], section=2)
        from_z = flip(here[1].astype(jnp.bfloat16), dp=1)
        from_xz = flip(there[1], section=2, dp=1)
        emb = (
            residual
            + here[0]
            + from_x.astype(jnp.float32)
            + from_z.astype(jnp.float32)
            + from_xz.astype(jnp.float32)
        )
        slide_normed = layer_norm(emb, slide_gain).astype(jnp.bfloat16)

        vmem = pl.BlockSpec(memory_space=pltpu.VMEM)
        if n_seq == 2:
            keys = [
                slide_normed,
                flip(slide_normed, section=2),
                flip(slide_normed, seq=1),
                flip(slide_normed, section=2, seq=1),
            ]
            others = [flip(block, section=1) for block in keys]
            keys = keys[:2] + others[:2] + keys[2:] + others[2:]
        else:
            keys = lax.all_gather(slide_normed, ("seq", "section"), axis=0, tiled=True)

        width = w_qkv.shape[2]
        qkv = jnp.swapaxes(w_qkv, 1, 2)
        if n_seq == 2:
            keep, send = pl.pallas_call(
                lambda *refs: attend_kernel(*refs, heads=local_heads, masks=masks),
                out_shape=[
                    jax.ShapeDtypeStruct((2, width, tokens), jnp.float32),
                    jax.ShapeDtypeStruct((2, width, tokens), jnp.bfloat16),
                ],
                in_specs=[vmem] * 12,
                out_specs=[vmem] * 2,
                compiler_params=pltpu.CompilerParams(vmem_limit_bytes=28 * 2**20),
                cost_estimate=pl.CostEstimate(
                    flops=2 * count * width * (3 * 768 + 2 * local_heads * tokens),
                    bytes_accessed=8 * 2**20,
                    transcendentals=local_heads * tokens * count,
                ),
            )(*keys, qkv, out_w, emb, code)
        else:

            def by_head(x, matrix):
                x = jnp.dot(x, matrix.T, preferred_element_type=jnp.float32)
                x = x.astype(jnp.bfloat16).reshape(x.shape[0], local_heads, width // local_heads)
                return x.transpose(1, 0, 2)

            def one_head(args):
                q, k, v, q_row, k_row = args
                scores = jnp.dot(q, k.T, preferred_element_type=jnp.float32)
                scores = scores / math.sqrt(width // local_heads)
                ok = (q_row[:, None] == k_row[None, :]) | (q_idx[:, None] == k_idx[None, :])
                weight = jax.nn.softmax(jnp.where(ok, scores, NEG), axis=-1)
                return jnp.dot(weight, v, preferred_element_type=jnp.float32)

            queries = lax.dynamic_slice_in_dim(keys, seq_at * tokens, tokens, 0)
            att = lax.map(
                one_head,
                (by_head(queries, qkv[0]), by_head(keys, qkv[1]), by_head(keys, qkv[2]))
                + (codes(q_idx)[0], k_code),
            )
            att = att.transpose(1, 0, 2).reshape(tokens, width).astype(jnp.bfloat16)
            parts = jnp.dot(att, w_out, preferred_element_type=jnp.float32)
            old = lax.dynamic_slice_in_dim(parts, sec * own_rows, own_rows, 0)
            parts = lax.dynamic_update_slice_in_dim(parts, old + emb, sec * own_rows, 0)
            parts = jnp.stack(absolute(jnp.split(parts.T, n_sec, axis=0)))
            keep, send = parts[0::2], parts[1::2].astype(jnp.bfloat16)

        kept = keep + flip(send, section=1).astype(jnp.float32)
        out = kept[0] + flip(kept[1].astype(jnp.bfloat16), section=2).astype(jnp.float32)
        return out.astype(jnp.bfloat16).T[None]

    return per_device


def solution(mesh):
    placed = (
        P("dp", "seq", "section"),
        P(),
        P(("seq", "dp"), "section"),
        P(("seq", "dp"), "section"),
        P("section", ("seq", "dp")),
        P("section", None),
        P(),
        P(None, None, "section"),
        P("section", None),
        P("dp", None),
        P("section"),
        P("section"),
    )
    shape = mesh.shape
    return jax.shard_map(
        build(shape["section"], shape["seq"], shape["dp"]),
        mesh=mesh,
        in_specs=placed,
        out_specs=P("dp", "seq", "section"),
        check_vma=False,
    )
```

```python
import math

import jax
import jax.numpy as jnp
from jax import lax
from jax.experimental import pallas as pl
from jax.experimental.pallas import tpu as pltpu
from jax.sharding import PartitionSpec as P

NEG = -1e30
AXES = ("section", "seq", "dp")


def layer_norm(rows, gain):
    mean = jnp.mean(rows, axis=-1, keepdims=True)
    centered = rows - mean
    var = jnp.mean(centered * centered, axis=-1, keepdims=True)
    return centered * lax.rsqrt(var + 1e-06) * gain


def slide_place(lengths_row, index):
    ends = jnp.cumsum(lengths_row, dtype=jnp.int32)
    after = index[:, None] >= ends[None, :]
    slide = jnp.sum(after.astype(jnp.int32), axis=1, dtype=jnp.int32)
    before = jnp.sum(jnp.where(after, lengths_row[None, :], 0), axis=1, dtype=jnp.int32)
    return (slide, index - before)


def attend_kernel(*refs, heads, masks):
    blocks, (w_ref, out_w_ref, emb_ref, code_ref, keep_ref, send_ref) = refs[:-6], refs[-6:]
    sec = lax.axis_index("section")
    core, side = sec % 2, sec // 2
    own = blocks[0].shape[0]
    keys = jnp.concatenate([block[...] for block in blocks], axis=0)
    count, rows = keys.shape[0], own * len(masks)
    q_code = jnp.transpose(code_ref[:, :rows])
    width = w_ref.shape[1]
    size = width // heads
    scale = math.log2(math.e) / math.sqrt(size)

    def project(x, which):
        return lax.dot_general(
            x, w_ref[which], (((1,), (1,)), ((), ())), preferred_element_type=jnp.float32
        ).astype(jnp.bfloat16)

    key, query, value = project(keys, 1), project(keys[:rows], 0), project(keys, 2)
    lane_head = lax.broadcasted_iota(jnp.int32, (rows, width), 1) // size
    diag = lax.broadcasted_iota(jnp.int32, (rows, count), 0) == lax.broadcasted_iota(
        jnp.int32, (rows, count), 1
    )
    att = jnp.zeros((rows, width), jnp.float32)
    for h in range(heads):
        scores = lax.dot_general(
            jnp.where(lane_head == h, query, jnp.zeros_like(query)),
            key,
            (((1,), (1,)), ((), ())),
            preferred_element_type=jnp.float32,
        )
        ok = (q_code[:, h : h + 1] == code_ref[heads + h : heads + h + 1, :]) | diag
        scores = jnp.where(ok, scores, NEG)
        top = jnp.max(scores, axis=1, keepdims=True)
        weight = jnp.exp2((scores - top) * scale)
        total = jnp.sum(weight, axis=1, keepdims=True)
        mixed = jnp.dot(weight.astype(jnp.bfloat16), value, preferred_element_type=jnp.float32)
        att = jnp.where(lane_head == h, mixed / total, att)
    part = jnp.dot(
        out_w_ref[...], jnp.transpose(att).astype(jnp.bfloat16), preferred_element_type=jnp.float32
    )
    emb = jnp.transpose(emb_ref[...])
    for block, mask in enumerate(masks):
        piece = part[:, block * own : (block + 1) * own]
        if block == 0:
            piece = piece + emb
        at = pl.ds(pl.multiple_of((mask ^ sec) * own, own), own)
        for j in range(part.shape[0] // width // 2):
            low = piece[2 * j * width : (2 * j + 1) * width]
            high = piece[(2 * j + 1) * width : (2 * j + 2) * width]
            keep_ref[j ^ side, :, at] = jnp.where(core == 0, low, high)
            send_ref[j ^ side, :, at] = jnp.where(core == 0, high, low).astype(send_ref.dtype)


def build(n_sec, n_seq, n_dp):
    sizes = {"section": n_sec, "seq": n_seq, "dp": n_dp}

    def flip(x, **masks):
        names = tuple(a for a in AXES if masks.get(a))
        pairs = []
        total = math.prod(sizes[a] for a in names)
        for source in range(total):
            rest, coords = source, []
            for a in reversed(names):
                coords.append(rest % sizes[a])
                rest //= sizes[a]
            target = 0
            for a, c in zip(names, reversed(coords)):
                target = target * sizes[a] + (c ^ masks[a])
            pairs.append((source, target))
        return lax.ppermute(x, names if len(names) > 1 else names[0], pairs)

    def rotate(x, k):
        return lax.ppermute(x, "dp", [(i, (i + k) % n_dp) for i in range(n_dp)])

    def after(x, *others):
        return lax.optimization_barrier((x,) + others)[0]

    def absolute(blocks):
        stacked, sec = jnp.stack(blocks), lax.axis_index("section")
        return [lax.dynamic_index_in_dim(stacked, sec ^ j, 0, False) for j in range(n_sec)]

    def gather_section(x):
        across = flip(x, section=2)
        return [x, flip(after(x, across), section=1), across, flip(across, section=1)]

    def gather_rows(same, other, seq_at, dp_at):
        mats, rows, units = same.shape
        part = jnp.zeros((mats, n_dp * rows, units), same.dtype)
        for k in range(n_dp):
            block = rotate(other if k % 2 else same, k) if k else same
            part = lax.dynamic_update_slice(part, block, (0, ((dp_at - k) % n_dp) * rows, 0))
        whole = lax.all_gather(part, "seq", axis=1, tiled=True)
        return jnp.concatenate(absolute(jnp.split(whole, n_sec, axis=1)), axis=1)

    def row_of(y, k, rows):
        sec, seq_at, dp_at = (lax.axis_index(a) for a in AXES)
        block = (seq_at ^ y) * n_dp + (dp_at - k) % n_dp
        each = n_seq * n_dp // n_sec
        return ((block // each ^ sec) * each + block % each) * rows

    def place_rows(blocks):
        first = blocks[0, 2]
        mats, rows, units = first.shape
        whole = after(jnp.zeros((mats, n_seq * n_dp * rows, units), first.dtype), first)
        for (y, k), block in blocks.items():
            whole = lax.dynamic_update_slice(whole, block, (0, row_of(y, k, rows), 0))
        return whole

    def per_device(
        tile_feats,
        tile_gain,
        w_gate,
        w_up,
        w_down,
        w_proj,
        slide_gain,
        w_qkv,
        w_out,
        lengths,
        seg_len,
        rate,
    ):
        sec = lax.axis_index("section")
        seq_at = lax.axis_index("seq")
        dp_at = lax.axis_index("dp")
        core, side, odd = sec % 2, sec // 2, dp_at % 2
        mine = tile_feats[0]
        tokens, feats = mine.shape
        own_rows = tokens // n_sec
        half = w_gate.shape[1] // 2

        def halves(x, which):
            return lax.dynamic_slice_in_dim(x, which * half, half, x.ndim - 1)

        pair = jnp.stack([w_gate, w_up])
        pair_same, pair_other = halves(pair, odd), halves(pair, 1 - odd)
        down = w_down.T[None]
        down_same, down_other = halves(down, odd), halves(down, 1 - odd)
        ordered = n_seq == 2 and n_dp == 4

        if n_seq == 2:
            masks = (0, 2, 1, 3)
            span = jnp.arange(own_rows, dtype=jnp.int32)
            k_idx = jnp.concatenate(
                [(seq_at ^ y) * tokens + (sec ^ m) * own_rows + span for y in (0, 1) for m in masks]
            )
            q_idx = k_idx[:tokens]
        else:
            k_idx = jnp.arange(n_seq * tokens, dtype=jnp.int32)
            q_idx = seq_at * tokens + jnp.arange(tokens, dtype=jnp.int32)
        count = k_idx.shape[0]
        local_heads = seg_len.shape[0]
        heads = sec * local_heads + jnp.arange(local_heads, dtype=jnp.int32)

        def codes(index):
            slide, pos = slide_place(lengths[0], index)
            block = slide[None, :] * count + pos[None, :] // seg_len[:, None]
            return block, pos[None, :] % rate[:, None] == (heads % rate)[:, None]

        k_block, picked = codes(k_idx)
        k_code = jnp.where(picked, k_block, -1)
        code = jnp.concatenate([k_block, k_code], axis=0)

        own_at = sec * own_rows
        gain = jnp.concatenate(absolute(jnp.split(tile_gain, n_sec)))
        out_w = w_out.T

        if ordered:
            g, d = {(0, 0): pair_same}, {(0, 0): down_same}
            beside = flip(mine, dp=1)
            mine_x = flip(mine, section=2)
            g[0, 2] = rotate(pair_same, 2)
            g[1, 0] = flip(pair_same, seq=1)
            d[1, 0] = flip(after(down_same, mine_x), seq=1)
            proj_x = flip(after(w_proj, mine_x), section=2)
            beside_x = flip(after(beside, proj_x, g[0, 2]), section=2)
            for k in (1, 3):
                g[0, k] = rotate(after(pair_other, g[0, 2], g[1, 0], d[1, 0]), k)
            g[1, 2] = flip(g[0, 2], seq=1)
            across = after(jnp.concatenate([mine_x, beside_x], axis=0), g[0, 2])
            both = after(jnp.concatenate([mine, beside], axis=0), across)
            both_c, across_c = flip(both, section=1), flip(across, section=1)
            d[0, 2] = rotate(after(down_same, g[0, 1]), 2)
            rows = jnp.concatenate([both, both_c, across, across_c], axis=1)
            normed = layer_norm(rows.astype(jnp.float32), gain).astype(jnp.bfloat16)
            g[1, 1] = flip(g[0, 1], seq=1)
            g[1, 3] = flip(after(g[0, 3], both_c, across_c), seq=1)
            gate_up = place_rows(g)
            for k in (1, 3):
                d[0, k] = rotate(after(down_other, d[0, 2], both_c, across_c, code, out_w), k)
            proj_c = flip(after(w_proj, proj_x, d[0, 1]), section=1)
            proj_xc = flip(after(proj_x, d[0, 1]), section=1)
            proj = jnp.concatenate([w_proj, proj_c, proj_x, proj_xc], axis=0)
            d[1, 2] = flip(d[0, 2], seq=1)
            d[1, 1], d[1, 3] = flip(after(d[0, 1], normed), seq=1), flip(d[0, 3], seq=1)
        else:
            gate_up = gather_rows(pair_same, pair_other, seq_at, dp_at)
            down_all = gather_rows(down_same, down_other, seq_at, dp_at)[0]
            both = jnp.concatenate([mine, flip(mine, dp=1)], axis=0)
            rows = jnp.concatenate(gather_section(both), axis=1)
            normed = layer_norm(rows.astype(jnp.float32), gain).astype(jnp.bfloat16)
            proj = jnp.concatenate(gather_section(w_proj), axis=0)

        residual = jnp.dot(
            lax.dynamic_slice_in_dim(rows[:tokens], own_at, own_rows, 0),
            proj,
            preferred_element_type=jnp.float32,
        )
        normed = after(normed, residual)
        gate = jnp.dot(normed, gate_up[0], preferred_element_type=jnp.float32)
        up = jnp.dot(normed, gate_up[1], preferred_element_type=jnp.float32)
        hidden = (jax.nn.silu(gate) * up).astype(jnp.bfloat16)
        hidden = hidden.reshape(2, n_sec // 2, 2, own_rows, half)
        hidden = jnp.stack(
            [lax.dynamic_index_in_dim(hidden, c, 2, False) for c in (1 - core, core)]
        )

        def fold(proj_rows, down_rows):
            return lax.dot_general(
                proj_rows, down_rows, (((0,), (0,)), ((), ())), preferred_element_type=jnp.float32
            )

        if ordered:
            late = [d.pop((1, 1)), d.pop((1, 3))]
            folded = fold(proj, after(place_rows(d)[0], hidden))
            for k, block in zip((1, 3), late):
                at = row_of(1, k, block.shape[1])
                folded = folded + fold(
                    lax.dynamic_slice_in_dim(proj, at, block.shape[1], 0), block[0]
                )
        else:
            folded = fold(proj, down_all)
        folded = folded.astype(jnp.bfloat16)

        def project(x):
            return lax.dot_general(
                x, folded, (((x.ndim - 1,), (1,)), ((), ())), preferred_element_type=jnp.float32
            )

        sums = project(hidden)
        got = flip(sums[0].astype(jnp.bfloat16), section=1)
        kept = sums[1] + got.astype(jnp.float32)
        here = lax.dynamic_index_in_dim(kept, side, 1, False)
        there = lax.dynamic_index_in_dim(kept, 1 - side, 1, False).astype(jnp.bfloat16)
        from_x = flip(there[0], section=2)
        from_z = flip(here[1].astype(jnp.bfloat16), dp=1)
        from_xz = flip(there[1], section=2, dp=1)
        emb = (
            residual
            + here[0]
            + from_x.astype(jnp.float32)
            + from_z.astype(jnp.float32)
            + from_xz.astype(jnp.float32)
        )
        slide_normed = layer_norm(emb, slide_gain).astype(jnp.bfloat16)

        vmem = pl.BlockSpec(memory_space=pltpu.VMEM)
        if n_seq == 2:
            keys = [
                slide_normed,
                flip(slide_normed, section=2),
                flip(slide_normed, seq=1),
                flip(slide_normed, section=2, seq=1),
            ]
            others = [flip(block, section=1) for block in keys]
            keys = keys[:2] + others[:2] + keys[2:] + others[2:]
        else:
            keys = lax.all_gather(slide_normed, ("seq", "section"), axis=0, tiled=True)

        width = w_qkv.shape[2]
        qkv = jnp.swapaxes(w_qkv, 1, 2)
        if n_seq == 2:
            keep, send = pl.pallas_call(
                lambda *refs: attend_kernel(*refs, heads=local_heads, masks=masks),
                out_shape=[
                    jax.ShapeDtypeStruct((2, width, tokens), jnp.float32),
                    jax.ShapeDtypeStruct((2, width, tokens), jnp.bfloat16),
                ],
                in_specs=[vmem] * 12,
                out_specs=[vmem] * 2,
                compiler_params=pltpu.CompilerParams(vmem_limit_bytes=28 * 2**20),
                cost_estimate=pl.CostEstimate(
                    flops=2 * count * width * (3 * 768 + 2 * local_heads * tokens),
                    bytes_accessed=8 * 2**20,
                    transcendentals=local_heads * tokens * count,
                ),
            )(*keys, qkv, out_w, emb, code)
        else:

            def by_head(x, matrix):
                x = jnp.dot(x, matrix.T, preferred_element_type=jnp.float32)
                x = x.astype(jnp.bfloat16).reshape(x.shape[0], local_heads, width // local_heads)
                return x.transpose(1, 0, 2)

            def one_head(args):
                q, k, v, q_row, k_row = args
                scores = jnp.dot(q, k.T, preferred_element_type=jnp.float32)
                scores = scores / math.sqrt(width // local_heads)
                ok = (q_row[:, None] == k_row[None, :]) | (q_idx[:, None] == k_idx[None, :])
                weight = jax.nn.softmax(jnp.where(ok, scores, NEG), axis=-1)
                return jnp.dot(weight, v, preferred_element_type=jnp.float32)

            queries = lax.dynamic_slice_in_dim(keys, seq_at * tokens, tokens, 0)
            att = lax.map(
                one_head,
                (by_head(queries, qkv[0]), by_head(keys, qkv[1]), by_head(keys, qkv[2]))
                + (codes(q_idx)[0], k_code),
            )
            att = att.transpose(1, 0, 2).reshape(tokens, width).astype(jnp.bfloat16)
            parts = jnp.dot(att, w_out, preferred_element_type=jnp.float32)
            old = lax.dynamic_slice_in_dim(parts, sec * own_rows, own_rows, 0)
            parts = lax.dynamic_update_slice_in_dim(parts, old + emb, sec * own_rows, 0)
            parts = jnp.stack(absolute(jnp.split(parts.T, n_sec, axis=0)))
            keep, send = parts[0::2], parts[1::2].astype(jnp.bfloat16)

        kept = keep + flip(send, section=1).astype(jnp.float32)
        out = kept[0] + flip(kept[1].astype(jnp.bfloat16), section=2).astype(jnp.float32)
        return out.astype(jnp.bfloat16).T[None]

    return per_device


def solution(mesh):
    placed = (
        P("dp", "seq", "section"),
        P(),
        P(("seq", "dp"), "section"),
        P(("seq", "dp"), "section"),
        P("section", ("seq", "dp")),
        P("section", None),
        P(),
        P(None, None, "section"),
        P("section", None),
        P("dp", None),
        P("section"),
        P("section"),
    )
    shape = mesh.shape
    return jax.shard_map(
        build(shape["section"], shape["seq"], shape["dp"]),
        mesh=mesh,
        in_specs=placed,
        out_specs=P("dp", "seq", "section"),
        check_vma=False,
    )
```

```python
import math

import jax
import jax.numpy as jnp
from jax import lax
from jax.experimental import pallas as pl
from jax.experimental.pallas import tpu as pltpu
from jax.sharding import PartitionSpec as P

NEG = -1e30
AXES = ("section", "seq", "dp")


def layer_norm(rows, gain):
    mean = jnp.mean(rows, axis=-1, keepdims=True)
    centered = rows - mean
    var = jnp.mean(centered * centered, axis=-1, keepdims=True)
    return centered * lax.rsqrt(var + 1e-06) * gain


def slide_place(lengths_row, index):
    ends = jnp.cumsum(lengths_row, dtype=jnp.int32)
    after = index[:, None] >= ends[None, :]
    slide = jnp.sum(after.astype(jnp.int32), axis=1, dtype=jnp.int32)
    before = jnp.sum(jnp.where(after, lengths_row[None, :], 0), axis=1, dtype=jnp.int32)
    return (slide, index - before)


def attend_kernel(*refs, heads, masks):
    blocks, (w_ref, out_w_ref, emb_ref, code_ref, keep_ref, send_ref) = refs[:-6], refs[-6:]
    sec = lax.axis_index("section")
    core, side = sec % 2, sec // 2
    own = blocks[0].shape[0]
    keys = jnp.concatenate([block[...] for block in blocks], axis=0)
    count, rows = keys.shape[0], own * len(masks)
    q_code = jnp.transpose(code_ref[:, :rows])
    width = w_ref.shape[1]
    size = width // heads
    scale = math.log2(math.e) / math.sqrt(size)

    def project(x, which):
        return lax.dot_general(
            x, w_ref[which], (((1,), (1,)), ((), ())), preferred_element_type=jnp.float32
        ).astype(jnp.bfloat16)

    key, query, value = project(keys, 1), project(keys[:rows], 0), project(keys, 2)
    lane_head = lax.broadcasted_iota(jnp.int32, (rows, width), 1) // size
    diag = lax.broadcasted_iota(jnp.int32, (rows, count), 0) == lax.broadcasted_iota(
        jnp.int32, (rows, count), 1
    )
    att = jnp.zeros((rows, width), jnp.float32)
    for h in range(heads):
        scores = lax.dot_general(
            jnp.where(lane_head == h, query, jnp.zeros_like(query)),
            key,
            (((1,), (1,)), ((), ())),
            preferred_element_type=jnp.float32,
        )
        ok = (q_code[:, h : h + 1] == code_ref[heads + h : heads + h + 1, :]) | diag
        scores = jnp.where(ok, scores, NEG)
        top = jnp.max(scores, axis=1, keepdims=True)
        weight = jnp.exp2((scores - top) * scale)
        total = jnp.sum(weight, axis=1, keepdims=True)
        mixed = jnp.dot(weight.astype(jnp.bfloat16), value, preferred_element_type=jnp.float32)
        att = jnp.where(lane_head == h, mixed / total, att)
    part = jnp.dot(
        out_w_ref[...], jnp.transpose(att).astype(jnp.bfloat16), preferred_element_type=jnp.float32
    )
    emb = jnp.transpose(emb_ref[...])
    for block, mask in enumerate(masks):
        piece = part[:, block * own : (block + 1) * own]
        if block == 0:
            piece = piece + emb
        at = pl.ds(pl.multiple_of((mask ^ sec) * own, own), own)
        for j in range(part.shape[0] // width // 2):
            low = piece[2 * j * width : (2 * j + 1) * width]
            high = piece[(2 * j + 1) * width : (2 * j + 2) * width]
            keep_ref[j ^ side, :, at] = jnp.where(core == 0, low, high)
            send_ref[j ^ side, :, at] = jnp.where(core == 0, high, low).astype(send_ref.dtype)


def build(n_sec, n_seq, n_dp):
    sizes = {"section": n_sec, "seq": n_seq, "dp": n_dp}

    def flip(x, **masks):
        names = tuple(a for a in AXES if masks.get(a))
        pairs = []
        total = math.prod(sizes[a] for a in names)
        for source in range(total):
            rest, coords = source, []
            for a in reversed(names):
                coords.append(rest % sizes[a])
                rest //= sizes[a]
            target = 0
            for a, c in zip(names, reversed(coords)):
                target = target * sizes[a] + (c ^ masks[a])
            pairs.append((source, target))
        return lax.ppermute(x, names if len(names) > 1 else names[0], pairs)

    def rotate(x, k):
        return lax.ppermute(x, "dp", [(i, (i + k) % n_dp) for i in range(n_dp)])

    def after(x, *others):
        return lax.optimization_barrier((x,) + others)[0]

    def absolute(blocks):
        stacked, sec = jnp.stack(blocks), lax.axis_index("section")
        return [lax.dynamic_index_in_dim(stacked, sec ^ j, 0, False) for j in range(n_sec)]

    def gather_section(x):
        across = flip(x, section=2)
        return [x, flip(after(x, across), section=1), across, flip(across, section=1)]

    def gather_rows(same, other, seq_at, dp_at):
        mats, rows, units = same.shape
        part = jnp.zeros((mats, n_dp * rows, units), same.dtype)
        for k in range(n_dp):
            block = rotate(other if k % 2 else same, k) if k else same
            part = lax.dynamic_update_slice(part, block, (0, ((dp_at - k) % n_dp) * rows, 0))
        whole = lax.all_gather(part, "seq", axis=1, tiled=True)
        return jnp.concatenate(absolute(jnp.split(whole, n_sec, axis=1)), axis=1)

    def row_of(y, k, rows):
        sec, seq_at, dp_at = (lax.axis_index(a) for a in AXES)
        block = (seq_at ^ y) * n_dp + (dp_at - k) % n_dp
        each = n_seq * n_dp // n_sec
        return ((block // each ^ sec) * each + block % each) * rows

    def place_rows(blocks):
        first = blocks[0, 2]
        mats, rows, units = first.shape
        whole = after(jnp.zeros((mats, n_seq * n_dp * rows, units), first.dtype), first)
        for (y, k), block in blocks.items():
            whole = lax.dynamic_update_slice(whole, block, (0, row_of(y, k, rows), 0))
        return whole

    def per_device(
        tile_feats,
        tile_gain,
        w_gate,
        w_up,
        w_down,
        w_proj,
        slide_gain,
        w_qkv,
        w_out,
        lengths,
        seg_len,
        rate,
    ):
        sec = lax.axis_index("section")
        seq_at = lax.axis_index("seq")
        dp_at = lax.axis_index("dp")
        core, side, odd = sec % 2, sec // 2, dp_at % 2
        mine = tile_feats[0]
        tokens, feats = mine.shape
        own_rows = tokens // n_sec
        half = w_gate.shape[1] // 2

        def halves(x, which):
            return lax.dynamic_slice_in_dim(x, which * half, half, x.ndim - 1)

        pair = jnp.stack([w_gate, w_up])
        pair_same, pair_other = halves(pair, odd), halves(pair, 1 - odd)
        down = w_down.T[None]
        down_same, down_other = halves(down, odd), halves(down, 1 - odd)
        ordered = n_seq == 2 and n_dp == 4

        if n_seq == 2:
            masks = (0, 2, 1, 3)
            span = jnp.arange(own_rows, dtype=jnp.int32)
            k_idx = jnp.concatenate(
                [(seq_at ^ y) * tokens + (sec ^ m) * own_rows + span for y in (0, 1) for m in masks]
            )
            q_idx = k_idx[:tokens]
        else:
            k_idx = jnp.arange(n_seq * tokens, dtype=jnp.int32)
            q_idx = seq_at * tokens + jnp.arange(tokens, dtype=jnp.int32)
        count = k_idx.shape[0]
        local_heads = seg_len.shape[0]
        heads = sec * local_heads + jnp.arange(local_heads, dtype=jnp.int32)

        def codes(index):
            slide, pos = slide_place(lengths[0], index)
            block = slide[None, :] * count + pos[None, :] // seg_len[:, None]
            return block, pos[None, :] % rate[:, None] == (heads % rate)[:, None]

        k_block, picked = codes(k_idx)
        k_code = jnp.where(picked, k_block, -1)
        code = jnp.concatenate([k_block, k_code], axis=0)

        own_at = sec * own_rows
        gain = jnp.concatenate(absolute(jnp.split(tile_gain, n_sec)))
        out_w = w_out.T

        if ordered:
            g, d = {(0, 0): pair_same}, {(0, 0): down_same}
            beside = flip(mine, dp=1)
            mine_x = flip(mine, section=2)
            g[0, 2] = rotate(pair_same, 2)
            g[1, 0] = flip(pair_same, seq=1)
            d[1, 0] = flip(after(down_same, mine_x), seq=1)
            proj_x = flip(after(w_proj, mine_x), section=2)
            beside_x = flip(after(beside, g[0, 2]), section=2)
            for k in (1, 3):
                g[0, k] = rotate(after(pair_other, g[0, 2], g[1, 0], d[1, 0]), k)
            g[1, 2] = flip(g[0, 2], seq=1)
            across = after(jnp.concatenate([mine_x, beside_x], axis=0), g[0, 2])
            both = after(jnp.concatenate([mine, beside], axis=0), across)
            both_c, across_c = flip(both, section=1), flip(across, section=1)
            d[0, 2] = rotate(after(down_same, g[0, 1], across), 2)
            rows = jnp.concatenate([both, both_c, across, across_c], axis=1)
            normed = layer_norm(rows.astype(jnp.float32), gain).astype(jnp.bfloat16)
            g[1, 1] = flip(g[0, 1], seq=1)
            g[1, 3] = flip(after(g[0, 3], both_c, across_c), seq=1)
            gate_up = place_rows(g)
            for k in (1, 3):
                d[0, k] = rotate(after(down_other, d[0, 2], both_c, across_c, code, out_w), k)
            proj_c = flip(after(w_proj, proj_x, d[0, 1]), section=1)
            proj_xc = flip(after(proj_x, d[0, 1]), section=1)
            proj = jnp.concatenate([w_proj, proj_c, proj_x, proj_xc], axis=0)
            d[1, 2] = flip(d[0, 2], seq=1)
            d[1, 1], d[1, 3] = flip(after(d[0, 1], normed), seq=1), flip(d[0, 3], seq=1)
        else:
            gate_up = gather_rows(pair_same, pair_other, seq_at, dp_at)
            down_all = gather_rows(down_same, down_other, seq_at, dp_at)[0]
            both = jnp.concatenate([mine, flip(mine, dp=1)], axis=0)
            rows = jnp.concatenate(gather_section(both), axis=1)
            normed = layer_norm(rows.astype(jnp.float32), gain).astype(jnp.bfloat16)
            proj = jnp.concatenate(gather_section(w_proj), axis=0)

        residual = jnp.dot(
            lax.dynamic_slice_in_dim(rows[:tokens], own_at, own_rows, 0),
            proj,
            preferred_element_type=jnp.float32,
        )
        normed = after(normed, residual)
        gate = jnp.dot(normed, gate_up[0], preferred_element_type=jnp.float32)
        up = jnp.dot(normed, gate_up[1], preferred_element_type=jnp.float32)
        hidden = (jax.nn.silu(gate) * up).astype(jnp.bfloat16)
        hidden = hidden.reshape(2, n_sec // 2, 2, own_rows, half)

        def fold(proj_rows, down_rows):
            return lax.dot_general(
                proj_rows, down_rows, (((0,), (0,)), ((), ())), preferred_element_type=jnp.float32
            )

        if ordered:
            late = [d.pop((1, 1)), d.pop((1, 3))]
            folded = fold(proj, after(place_rows(d)[0], hidden))
            for k, block in zip((1, 3), late):
                at = row_of(1, k, block.shape[1])
                folded = folded + fold(
                    lax.dynamic_slice_in_dim(proj, at, block.shape[1], 0), block[0]
                )
        else:
            folded = fold(proj, down_all)
        folded = folded.astype(jnp.bfloat16)

        def project(x):
            return lax.dot_general(
                x, folded, (((x.ndim - 1,), (1,)), ((), ())), preferred_element_type=jnp.float32
            )

        send = project(lax.dynamic_index_in_dim(hidden, 1 - core, 2, False)).astype(jnp.bfloat16)
        got = flip(send, section=1)
        kept = after(project(lax.dynamic_index_in_dim(hidden, core, 2, False)), send)
        kept = kept + got.astype(jnp.float32)
        here = lax.dynamic_index_in_dim(kept, side, 1, False)
        there = lax.dynamic_index_in_dim(kept, 1 - side, 1, False).astype(jnp.bfloat16)
        from_x = flip(there[0], section=2)
        from_z = flip(here[1].astype(jnp.bfloat16), dp=1)
        from_xz = flip(there[1], section=2, dp=1)
        emb = (
            residual
            + here[0]
            + from_x.astype(jnp.float32)
            + from_z.astype(jnp.float32)
            + from_xz.astype(jnp.float32)
        )
        slide_normed = layer_norm(emb, slide_gain).astype(jnp.bfloat16)

        vmem = pl.BlockSpec(memory_space=pltpu.VMEM)
        if n_seq == 2:
            keys = [
                slide_normed,
                flip(slide_normed, section=2),
                flip(slide_normed, seq=1),
                flip(slide_normed, section=2, seq=1),
            ]
            others = [flip(block, section=1) for block in keys]
            keys = keys[:2] + others[:2] + keys[2:] + others[2:]
        else:
            keys = lax.all_gather(slide_normed, ("seq", "section"), axis=0, tiled=True)

        width = w_qkv.shape[2]
        qkv = jnp.swapaxes(w_qkv, 1, 2)
        if n_seq == 2:
            keep, send = pl.pallas_call(
                lambda *refs: attend_kernel(*refs, heads=local_heads, masks=masks),
                out_shape=[
                    jax.ShapeDtypeStruct((2, width, tokens), jnp.float32),
                    jax.ShapeDtypeStruct((2, width, tokens), jnp.bfloat16),
                ],
                in_specs=[vmem] * 12,
                out_specs=[vmem] * 2,
                compiler_params=pltpu.CompilerParams(vmem_limit_bytes=16 * 2**20),
                cost_estimate=pl.CostEstimate(
                    flops=2 * count * width * (3 * 768 + 2 * local_heads * tokens),
                    bytes_accessed=8 * 2**20,
                    transcendentals=local_heads * tokens * count,
                ),
            )(*keys, qkv, out_w, emb, code)
        else:

            def by_head(x, matrix):
                x = jnp.dot(x, matrix.T, preferred_element_type=jnp.float32)
                x = x.astype(jnp.bfloat16).reshape(x.shape[0], local_heads, width // local_heads)
                return x.transpose(1, 0, 2)

            def one_head(args):
                q, k, v, q_row, k_row = args
                scores = jnp.dot(q, k.T, preferred_element_type=jnp.float32)
                scores = scores / math.sqrt(width // local_heads)
                ok = (q_row[:, None] == k_row[None, :]) | (q_idx[:, None] == k_idx[None, :])
                weight = jax.nn.softmax(jnp.where(ok, scores, NEG), axis=-1)
                return jnp.dot(weight, v, preferred_element_type=jnp.float32)

            queries = lax.dynamic_slice_in_dim(keys, seq_at * tokens, tokens, 0)
            att = lax.map(
                one_head,
                (by_head(queries, qkv[0]), by_head(keys, qkv[1]), by_head(keys, qkv[2]))
                + (codes(q_idx)[0], k_code),
            )
            att = att.transpose(1, 0, 2).reshape(tokens, width).astype(jnp.bfloat16)
            parts = jnp.dot(att, w_out, preferred_element_type=jnp.float32)
            old = lax.dynamic_slice_in_dim(parts, sec * own_rows, own_rows, 0)
            parts = lax.dynamic_update_slice_in_dim(parts, old + emb, sec * own_rows, 0)
            parts = jnp.stack(absolute(jnp.split(parts.T, n_sec, axis=0)))
            keep, send = parts[0::2], parts[1::2].astype(jnp.bfloat16)

        kept = keep + flip(send, section=1).astype(jnp.float32)
        out = kept[0] + flip(kept[1].astype(jnp.bfloat16), section=2).astype(jnp.float32)
        return out.astype(jnp.bfloat16).T[None]

    return per_device


def solution(mesh):
    placed = (
        P("dp", "seq", "section"),
        P(),
        P(("seq", "dp"), "section"),
        P(("seq", "dp"), "section"),
        P("section", ("seq", "dp")),
        P("section", None),
        P(),
        P(None, None, "section"),
        P("section", None),
        P("dp", None),
        P("section"),
        P("section"),
    )
    shape = mesh.shape
    return jax.shard_map(
        build(shape["section"], shape["seq"], shape["dp"]),
        mesh=mesh,
        in_specs=placed,
        out_specs=P("dp", "seq", "section"),
        check_vma=False,
    )
```

```python
import math

import jax
import jax.numpy as jnp
from jax import lax
from jax.experimental import pallas as pl
from jax.experimental.pallas import tpu as pltpu
from jax.sharding import PartitionSpec as P

NEG = -1e30
AXES = ("section", "seq", "dp")


def layer_norm(rows, gain):
    mean = jnp.mean(rows, axis=-1, keepdims=True)
    centered = rows - mean
    var = jnp.mean(centered * centered, axis=-1, keepdims=True)
    return centered * lax.rsqrt(var + 1e-06) * gain


def slide_place(lengths_row, index):
    ends = jnp.cumsum(lengths_row, dtype=jnp.int32)
    after = index[:, None] >= ends[None, :]
    slide = jnp.sum(after.astype(jnp.int32), axis=1, dtype=jnp.int32)
    before = jnp.sum(jnp.where(after, lengths_row[None, :], 0), axis=1, dtype=jnp.int32)
    return (slide, index - before)


def attend_kernel(*refs, heads, masks):
    blocks, (w_ref, out_w_ref, emb_ref, code_ref, keep_ref, send_ref) = refs[:-6], refs[-6:]
    sec = lax.axis_index("section")
    core, side = sec % 2, sec // 2
    own = blocks[0].shape[0]
    keys = jnp.concatenate([block[...] for block in blocks], axis=0)
    count, rows = keys.shape[0], own * len(masks)
    q_code = jnp.transpose(code_ref[:, :rows])
    width = w_ref.shape[1]
    size = width // heads
    scale = math.log2(math.e) / math.sqrt(size)

    def project(x, which):
        return lax.dot_general(
            x, w_ref[which], (((1,), (1,)), ((), ())), preferred_element_type=jnp.float32
        ).astype(jnp.bfloat16)

    key, query, value = project(keys, 1), project(keys[:rows], 0), project(keys, 2)
    lane_head = lax.broadcasted_iota(jnp.int32, (rows, width), 1) // size
    diag = lax.broadcasted_iota(jnp.int32, (rows, count), 0) == lax.broadcasted_iota(
        jnp.int32, (rows, count), 1
    )
    att = jnp.zeros((rows, width), jnp.float32)
    for h in range(heads):
        scores = lax.dot_general(
            jnp.where(lane_head == h, query, jnp.zeros_like(query)),
            key,
            (((1,), (1,)), ((), ())),
            preferred_element_type=jnp.float32,
        )
        ok = (q_code[:, h : h + 1] == code_ref[heads + h : heads + h + 1, :]) | diag
        scores = jnp.where(ok, scores, NEG)
        top = jnp.max(scores, axis=1, keepdims=True)
        weight = jnp.exp2((scores - top) * scale)
        total = jnp.sum(weight, axis=1, keepdims=True)
        mixed = jnp.dot(weight.astype(jnp.bfloat16), value, preferred_element_type=jnp.float32)
        att = jnp.where(lane_head == h, mixed / total, att)
    part = jnp.dot(
        out_w_ref[...], jnp.transpose(att).astype(jnp.bfloat16), preferred_element_type=jnp.float32
    )
    emb = jnp.transpose(emb_ref[...])
    for block, mask in enumerate(masks):
        piece = part[:, block * own : (block + 1) * own]
        if block == 0:
            piece = piece + emb
        at = pl.ds(pl.multiple_of((mask ^ sec) * own, own), own)
        for j in range(part.shape[0] // width // 2):
            low = piece[2 * j * width : (2 * j + 1) * width]
            high = piece[(2 * j + 1) * width : (2 * j + 2) * width]
            keep_ref[j ^ side, :, at] = jnp.where(core == 0, low, high)
            send_ref[j ^ side, :, at] = jnp.where(core == 0, high, low).astype(send_ref.dtype)


def build(n_sec, n_seq, n_dp):
    sizes = {"section": n_sec, "seq": n_seq, "dp": n_dp}

    def flip(x, **masks):
        names = tuple(a for a in AXES if masks.get(a))
        pairs = []
        total = math.prod(sizes[a] for a in names)
        for source in range(total):
            rest, coords = source, []
            for a in reversed(names):
                coords.append(rest % sizes[a])
                rest //= sizes[a]
            target = 0
            for a, c in zip(names, reversed(coords)):
                target = target * sizes[a] + (c ^ masks[a])
            pairs.append((source, target))
        return lax.ppermute(x, names if len(names) > 1 else names[0], pairs)

    def rotate(x, k):
        return lax.ppermute(x, "dp", [(i, (i + k) % n_dp) for i in range(n_dp)])

    def after(x, *others):
        return lax.optimization_barrier((x,) + others)[0]

    def absolute(blocks):
        stacked, sec = jnp.stack(blocks), lax.axis_index("section")
        return [lax.dynamic_index_in_dim(stacked, sec ^ j, 0, False) for j in range(n_sec)]

    def gather_section(x):
        across = flip(x, section=2)
        return [x, flip(after(x, across), section=1), across, flip(across, section=1)]

    def gather_rows(same, other, seq_at, dp_at):
        mats, rows, units = same.shape
        part = jnp.zeros((mats, n_dp * rows, units), same.dtype)
        for k in range(n_dp):
            block = rotate(other if k % 2 else same, k) if k else same
            part = lax.dynamic_update_slice(part, block, (0, ((dp_at - k) % n_dp) * rows, 0))
        whole = lax.all_gather(part, "seq", axis=1, tiled=True)
        return jnp.concatenate(absolute(jnp.split(whole, n_sec, axis=1)), axis=1)

    def row_of(y, k, rows):
        sec, seq_at, dp_at = (lax.axis_index(a) for a in AXES)
        block = (seq_at ^ y) * n_dp + (dp_at - k) % n_dp
        each = n_seq * n_dp // n_sec
        return ((block // each ^ sec) * each + block % each) * rows

    def place_rows(blocks):
        first = blocks[0, 2]
        mats, rows, units = first.shape
        whole = after(jnp.zeros((mats, n_seq * n_dp * rows, units), first.dtype), first)
        for (y, k), block in blocks.items():
            whole = lax.dynamic_update_slice(whole, block, (0, row_of(y, k, rows), 0))
        return whole

    def per_device(
        tile_feats,
        tile_gain,
        w_gate,
        w_up,
        w_down,
        w_proj,
        slide_gain,
        w_qkv,
        w_out,
        lengths,
        seg_len,
        rate,
    ):
        sec = lax.axis_index("section")
        seq_at = lax.axis_index("seq")
        dp_at = lax.axis_index("dp")
        core, side, odd = sec % 2, sec // 2, dp_at % 2
        mine = tile_feats[0]
        tokens, feats = mine.shape
        own_rows = tokens // n_sec
        half = w_gate.shape[1] // 2

        def halves(x, which):
            return lax.dynamic_slice_in_dim(x, which * half, half, x.ndim - 1)

        pair = jnp.stack([w_gate, w_up])
        pair_same, pair_other = halves(pair, odd), halves(pair, 1 - odd)
        down = w_down.T[None]
        down_same, down_other = halves(down, odd), halves(down, 1 - odd)
        ordered = n_seq == 2 and n_dp == 4

        if n_seq == 2:
            masks = (0, 2, 1, 3)
            span = jnp.arange(own_rows, dtype=jnp.int32)
            k_idx = jnp.concatenate(
                [(seq_at ^ y) * tokens + (sec ^ m) * own_rows + span for y in (0, 1) for m in masks]
            )
            q_idx = k_idx[:tokens]
        else:
            k_idx = jnp.arange(n_seq * tokens, dtype=jnp.int32)
            q_idx = seq_at * tokens + jnp.arange(tokens, dtype=jnp.int32)
        count = k_idx.shape[0]
        local_heads = seg_len.shape[0]
        heads = sec * local_heads + jnp.arange(local_heads, dtype=jnp.int32)

        def codes(index):
            slide, pos = slide_place(lengths[0], index)
            block = slide[None, :] * count + pos[None, :] // seg_len[:, None]
            return block, pos[None, :] % rate[:, None] == (heads % rate)[:, None]

        k_block, picked = codes(k_idx)
        k_code = jnp.where(picked, k_block, -1)
        code = jnp.concatenate([k_block, k_code], axis=0)

        own_at = sec * own_rows
        gain = jnp.concatenate(absolute(jnp.split(tile_gain, n_sec)))
        out_w = w_out.T

        if ordered:
            g, d = {(0, 0): pair_same}, {(0, 0): down_same}
            beside = flip(mine, dp=1)
            mine_x = flip(mine, section=2)
            g[0, 2] = rotate(pair_same, 2)
            g[1, 0] = flip(pair_same, seq=1)
            d[1, 0] = flip(after(down_same, mine_x), seq=1)
            proj_x = flip(after(w_proj, mine_x), section=2)
            beside_x = flip(after(beside, g[0, 2]), section=2)
            for k in (1, 3):
                g[0, k] = rotate(after(pair_other, g[0, 2], g[1, 0], d[1, 0]), k)
            g[1, 2] = flip(g[0, 2], seq=1)
            across = after(jnp.concatenate([mine_x, beside_x], axis=0), g[0, 2])
            both = after(jnp.concatenate([mine, beside], axis=0), across, g[1, 2], proj_x)
            both_c = flip(both, section=1)
            across_c = flip(after(across, g[1, 2], proj_x), section=1)
            far = rotate(after(down_same, g[0, 1], across), 2)
            rows = jnp.concatenate([both, both_c, across, across_c], axis=1)
            normed = layer_norm(rows.astype(jnp.float32), gain).astype(jnp.bfloat16)
            g[1, 1] = after(flip(g[0, 1], seq=1), normed)
            g[1, 3] = flip(after(g[0, 3], normed), seq=1)
            gate_up = place_rows(g)
            d[0, 2] = after(far, normed)
            for k in (1, 3):
                d[0, k] = rotate(after(down_other, d[0, 2], code, out_w), k)
            proj_c = flip(after(w_proj, proj_x, d[0, 1]), section=1)
            proj_xc = flip(after(proj_x, d[0, 1]), section=1)
            proj = jnp.concatenate([w_proj, proj_c, proj_x, proj_xc], axis=0)
            d[1, 2] = flip(d[0, 2], seq=1)
            d[1, 1], d[1, 3] = flip(d[0, 1], seq=1), flip(d[0, 3], seq=1)
        else:
            gate_up = gather_rows(pair_same, pair_other, seq_at, dp_at)
            down_all = gather_rows(down_same, down_other, seq_at, dp_at)[0]
            both = jnp.concatenate([mine, flip(mine, dp=1)], axis=0)
            rows = jnp.concatenate(gather_section(both), axis=1)
            normed = layer_norm(rows.astype(jnp.float32), gain).astype(jnp.bfloat16)
            proj = jnp.concatenate(gather_section(w_proj), axis=0)

        residual = jnp.dot(
            lax.dynamic_slice_in_dim(rows[:tokens], own_at, own_rows, 0),
            proj,
            preferred_element_type=jnp.float32,
        )
        normed = after(normed, residual)
        gate = jnp.dot(normed, gate_up[0], preferred_element_type=jnp.float32)
        up = jnp.dot(normed, gate_up[1], preferred_element_type=jnp.float32)
        hidden = (jax.nn.silu(gate) * up).astype(jnp.bfloat16)
        hidden = hidden.reshape(2, n_sec // 2, 2, own_rows, half)

        def fold(proj_rows, down_rows):
            return lax.dot_general(
                proj_rows, down_rows, (((0,), (0,)), ((), ())), preferred_element_type=jnp.float32
            )

        if ordered:
            late = [d.pop((1, 1)), d.pop((1, 3))]
            folded = fold(proj, after(place_rows(d)[0], hidden))
            for k, block in zip((1, 3), late):
                at = row_of(1, k, block.shape[1])
                folded = folded + fold(
                    lax.dynamic_slice_in_dim(proj, at, block.shape[1], 0), block[0]
                )
        else:
            folded = fold(proj, down_all)
        folded = folded.astype(jnp.bfloat16)

        def project(x):
            return lax.dot_general(
                x, folded, (((x.ndim - 1,), (1,)), ((), ())), preferred_element_type=jnp.float32
            )

        send = project(lax.dynamic_index_in_dim(hidden, 1 - core, 2, False)).astype(jnp.bfloat16)
        got = flip(send, section=1)
        kept = after(project(lax.dynamic_index_in_dim(hidden, core, 2, False)), send)
        kept = kept + got.astype(jnp.float32)
        here = lax.dynamic_index_in_dim(kept, side, 1, False)
        there = lax.dynamic_index_in_dim(kept, 1 - side, 1, False).astype(jnp.bfloat16)
        from_x = flip(there[0], section=2)
        from_z = flip(here[1].astype(jnp.bfloat16), dp=1)
        from_xz = flip(there[1], section=2, dp=1)
        emb = (
            residual
            + here[0]
            + from_x.astype(jnp.float32)
            + from_z.astype(jnp.float32)
            + from_xz.astype(jnp.float32)
        )
        slide_normed = layer_norm(emb, slide_gain).astype(jnp.bfloat16)

        vmem = pl.BlockSpec(memory_space=pltpu.VMEM)
        if n_seq == 2:
            keys = [
                slide_normed,
                flip(slide_normed, section=2),
                flip(slide_normed, seq=1),
                flip(slide_normed, section=2, seq=1),
            ]
            others = [flip(block, section=1) for block in keys]
            keys = keys[:2] + others[:2] + keys[2:] + others[2:]
        else:
            keys = lax.all_gather(slide_normed, ("seq", "section"), axis=0, tiled=True)

        width = w_qkv.shape[2]
        qkv = jnp.swapaxes(w_qkv, 1, 2)
        if n_seq == 2:
            keep, send = pl.pallas_call(
                lambda *refs: attend_kernel(*refs, heads=local_heads, masks=masks),
                out_shape=[
                    jax.ShapeDtypeStruct((2, width, tokens), jnp.float32),
                    jax.ShapeDtypeStruct((2, width, tokens), jnp.bfloat16),
                ],
                in_specs=[vmem] * 12,
                out_specs=[vmem] * 2,
                compiler_params=pltpu.CompilerParams(vmem_limit_bytes=16 * 2**20),
                cost_estimate=pl.CostEstimate(
                    flops=2 * count * width * (3 * 768 + 2 * local_heads * tokens),
                    bytes_accessed=8 * 2**20,
                    transcendentals=local_heads * tokens * count,
                ),
            )(*keys, qkv, out_w, emb, code)
        else:

            def by_head(x, matrix):
                x = jnp.dot(x, matrix.T, preferred_element_type=jnp.float32)
                x = x.astype(jnp.bfloat16).reshape(x.shape[0], local_heads, width // local_heads)
                return x.transpose(1, 0, 2)

            def one_head(args):
                q, k, v, q_row, k_row = args
                scores = jnp.dot(q, k.T, preferred_element_type=jnp.float32)
                scores = scores / math.sqrt(width // local_heads)
                ok = (q_row[:, None] == k_row[None, :]) | (q_idx[:, None] == k_idx[None, :])
                weight = jax.nn.softmax(jnp.where(ok, scores, NEG), axis=-1)
                return jnp.dot(weight, v, preferred_element_type=jnp.float32)

            queries = lax.dynamic_slice_in_dim(keys, seq_at * tokens, tokens, 0)
            att = lax.map(
                one_head,
                (by_head(queries, qkv[0]), by_head(keys, qkv[1]), by_head(keys, qkv[2]))
                + (codes(q_idx)[0], k_code),
            )
            att = att.transpose(1, 0, 2).reshape(tokens, width).astype(jnp.bfloat16)
            parts = jnp.dot(att, w_out, preferred_element_type=jnp.float32)
            old = lax.dynamic_slice_in_dim(parts, sec * own_rows, own_rows, 0)
            parts = lax.dynamic_update_slice_in_dim(parts, old + emb, sec * own_rows, 0)
            parts = jnp.stack(absolute(jnp.split(parts.T, n_sec, axis=0)))
            keep, send = parts[0::2], parts[1::2].astype(jnp.bfloat16)

        kept = keep + flip(send, section=1).astype(jnp.float32)
        out = kept[0] + flip(kept[1].astype(jnp.bfloat16), section=2).astype(jnp.float32)
        return out.astype(jnp.bfloat16).T[None]

    return per_device


def solution(mesh):
    placed = (
        P("dp", "seq", "section"),
        P(),
        P(("seq", "dp"), "section"),
        P(("seq", "dp"), "section"),
        P("section", ("seq", "dp")),
        P("section", None),
        P(),
        P(None, None, "section"),
        P("section", None),
        P("dp", None),
        P("section"),
        P("section"),
    )
    shape = mesh.shape
    return jax.shard_map(
        build(shape["section"], shape["seq"], shape["dp"]),
        mesh=mesh,
        in_specs=placed,
        out_specs=P("dp", "seq", "section"),
        check_vma=False,
    )
```

```python
import math

import jax
import jax.numpy as jnp
from jax import lax
from jax.experimental import pallas as pl
from jax.experimental.pallas import tpu as pltpu
from jax.sharding import PartitionSpec as P

NEG = -1e30
AXES = ("section", "seq", "dp")


def layer_norm(rows, gain):
    mean = jnp.mean(rows, axis=-1, keepdims=True)
    centered = rows - mean
    var = jnp.mean(centered * centered, axis=-1, keepdims=True)
    return centered * lax.rsqrt(var + 1e-06) * gain


def slide_place(lengths_row, index):
    ends = jnp.cumsum(lengths_row, dtype=jnp.int32)
    after = index[:, None] >= ends[None, :]
    slide = jnp.sum(after.astype(jnp.int32), axis=1, dtype=jnp.int32)
    before = jnp.sum(jnp.where(after, lengths_row[None, :], 0), axis=1, dtype=jnp.int32)
    return (slide, index - before)


def attend_kernel(*refs, heads, masks):
    blocks, (w_ref, out_w_ref, emb_ref, code_ref, keep_ref, send_ref) = refs[:-6], refs[-6:]
    sec = lax.axis_index("section")
    core, side = sec % 2, sec // 2
    own = blocks[0].shape[0]
    keys = jnp.concatenate([block[...] for block in blocks], axis=0)
    count, rows = keys.shape[0], own * len(masks)
    q_code = jnp.transpose(code_ref[:, :rows])
    width = w_ref.shape[1]
    size = width // heads
    scale = math.log2(math.e) / math.sqrt(size)

    def project(x, which):
        return lax.dot_general(
            x, w_ref[which], (((1,), (1,)), ((), ())), preferred_element_type=jnp.float32
        ).astype(jnp.bfloat16)

    key, query, value = project(keys, 1), project(keys[:rows], 0), project(keys, 2)
    lane_head = lax.broadcasted_iota(jnp.int32, (rows, width), 1) // size
    diag = lax.broadcasted_iota(jnp.int32, (rows, count), 0) == lax.broadcasted_iota(
        jnp.int32, (rows, count), 1
    )
    att = jnp.zeros((rows, width), jnp.float32)
    for h in range(heads):
        scores = lax.dot_general(
            jnp.where(lane_head == h, query, jnp.zeros_like(query)),
            key,
            (((1,), (1,)), ((), ())),
            preferred_element_type=jnp.float32,
        )
        ok = (q_code[:, h : h + 1] == code_ref[heads + h : heads + h + 1, :]) | diag
        scores = jnp.where(ok, scores, NEG)
        top = jnp.max(scores, axis=1, keepdims=True)
        weight = jnp.exp2((scores - top) * scale)
        total = jnp.sum(weight, axis=1, keepdims=True)
        mixed = jnp.dot(weight.astype(jnp.bfloat16), value, preferred_element_type=jnp.float32)
        att = jnp.where(lane_head == h, mixed / total, att)
    part = jnp.dot(
        out_w_ref[...], jnp.transpose(att).astype(jnp.bfloat16), preferred_element_type=jnp.float32
    )
    emb = jnp.transpose(emb_ref[...])
    for block, mask in enumerate(masks):
        piece = part[:, block * own : (block + 1) * own]
        if block == 0:
            piece = piece + emb
        at = pl.ds(pl.multiple_of((mask ^ sec) * own, own), own)
        for j in range(part.shape[0] // width // 2):
            low = piece[2 * j * width : (2 * j + 1) * width]
            high = piece[(2 * j + 1) * width : (2 * j + 2) * width]
            keep_ref[j ^ side, :, at] = jnp.where(core == 0, low, high)
            send_ref[j ^ side, :, at] = jnp.where(core == 0, high, low).astype(send_ref.dtype)


def build(n_sec, n_seq, n_dp):
    sizes = {"section": n_sec, "seq": n_seq, "dp": n_dp}

    def flip(x, **masks):
        names = tuple(a for a in AXES if masks.get(a))
        pairs = []
        total = math.prod(sizes[a] for a in names)
        for source in range(total):
            rest, coords = source, []
            for a in reversed(names):
                coords.append(rest % sizes[a])
                rest //= sizes[a]
            target = 0
            for a, c in zip(names, reversed(coords)):
                target = target * sizes[a] + (c ^ masks[a])
            pairs.append((source, target))
        return lax.ppermute(x, names if len(names) > 1 else names[0], pairs)

    def rotate(x, k):
        return lax.ppermute(x, "dp", [(i, (i + k) % n_dp) for i in range(n_dp)])

    def after(x, *others):
        return lax.optimization_barrier((x,) + others)[0]

    def absolute(blocks):
        stacked, sec = jnp.stack(blocks), lax.axis_index("section")
        return [lax.dynamic_index_in_dim(stacked, sec ^ j, 0, False) for j in range(n_sec)]

    def gather_section(x):
        across = flip(x, section=2)
        return [x, flip(after(x, across), section=1), across, flip(across, section=1)]

    def gather_rows(same, other, seq_at, dp_at):
        mats, rows, units = same.shape
        part = jnp.zeros((mats, n_dp * rows, units), same.dtype)
        for k in range(n_dp):
            block = rotate(other if k % 2 else same, k) if k else same
            part = lax.dynamic_update_slice(part, block, (0, ((dp_at - k) % n_dp) * rows, 0))
        whole = lax.all_gather(part, "seq", axis=1, tiled=True)
        return jnp.concatenate(absolute(jnp.split(whole, n_sec, axis=1)), axis=1)

    def row_of(y, k, rows):
        sec, seq_at, dp_at = (lax.axis_index(a) for a in AXES)
        block = (seq_at ^ y) * n_dp + (dp_at - k) % n_dp
        each = n_seq * n_dp // n_sec
        return ((block // each ^ sec) * each + block % each) * rows

    def place_rows(blocks):
        first = blocks[0, 2]
        mats, rows, units = first.shape
        whole = after(jnp.zeros((mats, n_seq * n_dp * rows, units), first.dtype), first)
        for (y, k), block in blocks.items():
            whole = lax.dynamic_update_slice(whole, block, (0, row_of(y, k, rows), 0))
        return whole

    def per_device(
        tile_feats,
        tile_gain,
        w_gate,
        w_up,
        w_down,
        w_proj,
        slide_gain,
        w_qkv,
        w_out,
        lengths,
        seg_len,
        rate,
    ):
        sec = lax.axis_index("section")
        seq_at = lax.axis_index("seq")
        dp_at = lax.axis_index("dp")
        core, side, odd = sec % 2, sec // 2, dp_at % 2
        mine = tile_feats[0]
        tokens, feats = mine.shape
        own_rows = tokens // n_sec
        half = w_gate.shape[1] // 2

        def halves(x, which):
            return lax.dynamic_slice_in_dim(x, which * half, half, x.ndim - 1)

        pair = jnp.stack([w_gate, w_up])
        pair_same, pair_other = halves(pair, odd), halves(pair, 1 - odd)
        down = w_down.T[None]
        down_same, down_other = halves(down, odd), halves(down, 1 - odd)
        ordered = n_seq == 2 and n_dp == 4

        if n_seq == 2:
            masks = (0, 2, 1, 3)
            span = jnp.arange(own_rows, dtype=jnp.int32)
            k_idx = jnp.concatenate(
                [(seq_at ^ y) * tokens + (sec ^ m) * own_rows + span for y in (0, 1) for m in masks]
            )
            q_idx = k_idx[:tokens]
        else:
            k_idx = jnp.arange(n_seq * tokens, dtype=jnp.int32)
            q_idx = seq_at * tokens + jnp.arange(tokens, dtype=jnp.int32)
        count = k_idx.shape[0]
        local_heads = seg_len.shape[0]
        heads = sec * local_heads + jnp.arange(local_heads, dtype=jnp.int32)

        def codes(index):
            slide, pos = slide_place(lengths[0], index)
            block = slide[None, :] * count + pos[None, :] // seg_len[:, None]
            return block, pos[None, :] % rate[:, None] == (heads % rate)[:, None]

        k_block, picked = codes(k_idx)
        k_code = jnp.where(picked, k_block, -1)
        code = jnp.concatenate([k_block, k_code], axis=0)

        own_at = sec * own_rows
        gain = jnp.concatenate(absolute(jnp.split(tile_gain, n_sec)))
        out_w = w_out.T

        if ordered:
            g, d = {(0, 0): pair_same}, {(0, 0): down_same}
            beside = flip(mine, dp=1)
            mine_x = flip(mine, section=2)
            g[0, 2] = rotate(pair_same, 2)
            g[1, 0] = flip(pair_same, seq=1)
            d[1, 0] = flip(down_same, seq=1)
            beside_x = flip(beside, section=2)
            for k in (1, 3):
                g[0, k] = rotate(after(pair_other, g[0, 2], d[1, 0], g[1, 0], mine_x), k)
            g[1, 2] = flip(g[0, 2], seq=1)
            across = after(jnp.concatenate([mine_x, beside_x], axis=0), g[0, 2], g[1, 2])
            both = after(jnp.concatenate([mine, beside], axis=0), across)
            both_c, across_c = flip(both, section=1), flip(across, section=1)
            proj_x = flip(after(w_proj, across), section=2)
            far = rotate(after(down_same, g[0, 1]), 2)
            rows = jnp.concatenate([both, both_c, across, across_c], axis=1)
            normed = layer_norm(rows.astype(jnp.float32), gain).astype(jnp.bfloat16)
            g[1, 1], g[1, 3] = flip(g[0, 1], seq=1), flip(g[0, 3], seq=1)
            gate_up = place_rows(g)
            d[0, 2] = after(far, normed)
            for k in (1, 3):
                d[0, k] = rotate(after(down_other, d[0, 2], code, out_w), k)
            proj_c = flip(after(w_proj, proj_x, d[0, 1]), section=1)
            proj_xc = flip(after(proj_x, d[0, 1]), section=1)
            proj = jnp.concatenate([w_proj, proj_c, proj_x, proj_xc], axis=0)
            for k in (2, 1, 3):
                d[1, k] = flip(d[0, k], seq=1)
        else:
            gate_up = gather_rows(pair_same, pair_other, seq_at, dp_at)
            down_all = gather_rows(down_same, down_other, seq_at, dp_at)[0]
            both = jnp.concatenate([mine, flip(mine, dp=1)], axis=0)
            rows = jnp.concatenate(gather_section(both), axis=1)
            normed = layer_norm(rows.astype(jnp.float32), gain).astype(jnp.bfloat16)
            proj = jnp.concatenate(gather_section(w_proj), axis=0)

        residual = jnp.dot(
            lax.dynamic_slice_in_dim(rows[:tokens], own_at, own_rows, 0),
            proj,
            preferred_element_type=jnp.float32,
        )
        normed = after(normed, residual)
        gate = jnp.dot(normed, gate_up[0], preferred_element_type=jnp.float32)
        up = jnp.dot(normed, gate_up[1], preferred_element_type=jnp.float32)
        hidden = (jax.nn.silu(gate) * up).astype(jnp.bfloat16)
        hidden = hidden.reshape(2, n_sec // 2, 2, own_rows, half)

        def fold(proj_rows, down_rows):
            return lax.dot_general(
                proj_rows, down_rows, (((0,), (0,)), ((), ())), preferred_element_type=jnp.float32
            )

        if ordered:
            late = [d.pop((1, 1)), d.pop((1, 3))]
            folded = fold(proj, after(place_rows(d)[0], hidden))
            for k, block in zip((1, 3), late):
                at = row_of(1, k, block.shape[1])
                folded = folded + fold(
                    lax.dynamic_slice_in_dim(proj, at, block.shape[1], 0), block[0]
                )
        else:
            folded = fold(proj, down_all)
        folded = folded.astype(jnp.bfloat16)

        def project(x):
            return lax.dot_general(
                x, folded, (((x.ndim - 1,), (1,)), ((), ())), preferred_element_type=jnp.float32
            )

        send = project(lax.dynamic_index_in_dim(hidden, 1 - core, 2, False)).astype(jnp.bfloat16)
        got = flip(send, section=1)
        kept = after(project(lax.dynamic_index_in_dim(hidden, core, 2, False)), send)
        kept = kept + got.astype(jnp.float32)
        here = lax.dynamic_index_in_dim(kept, side, 1, False)
        there = lax.dynamic_index_in_dim(kept, 1 - side, 1, False).astype(jnp.bfloat16)
        from_x = flip(there[0], section=2)
        from_z = flip(here[1].astype(jnp.bfloat16), dp=1)
        from_xz = flip(there[1], section=2, dp=1)
        emb = (
            residual
            + here[0]
            + from_x.astype(jnp.float32)
            + from_z.astype(jnp.float32)
            + from_xz.astype(jnp.float32)
        )
        slide_normed = layer_norm(emb, slide_gain).astype(jnp.bfloat16)

        vmem = pl.BlockSpec(memory_space=pltpu.VMEM)
        if n_seq == 2:
            keys = [
                slide_normed,
                flip(slide_normed, section=2),
                flip(slide_normed, seq=1),
                flip(slide_normed, section=2, seq=1),
            ]
            others = [flip(block, section=1) for block in keys]
            keys = keys[:2] + others[:2] + keys[2:] + others[2:]
        else:
            keys = lax.all_gather(slide_normed, ("seq", "section"), axis=0, tiled=True)

        width = w_qkv.shape[2]
        qkv = jnp.swapaxes(w_qkv, 1, 2)
        if n_seq == 2:
            keep, send = pl.pallas_call(
                lambda *refs: attend_kernel(*refs, heads=local_heads, masks=masks),
                out_shape=[
                    jax.ShapeDtypeStruct((2, width, tokens), jnp.float32),
                    jax.ShapeDtypeStruct((2, width, tokens), jnp.bfloat16),
                ],
                in_specs=[vmem] * 12,
                out_specs=[vmem] * 2,
                compiler_params=pltpu.CompilerParams(vmem_limit_bytes=16 * 2**20),
                cost_estimate=pl.CostEstimate(
                    flops=2 * count * width * (3 * 768 + 2 * local_heads * tokens),
                    bytes_accessed=8 * 2**20,
                    transcendentals=local_heads * tokens * count,
                ),
            )(*keys, qkv, out_w, emb, code)
        else:

            def by_head(x, matrix):
                x = jnp.dot(x, matrix.T, preferred_element_type=jnp.float32)
                x = x.astype(jnp.bfloat16).reshape(x.shape[0], local_heads, width // local_heads)
                return x.transpose(1, 0, 2)

            def one_head(args):
                q, k, v, q_row, k_row = args
                scores = jnp.dot(q, k.T, preferred_element_type=jnp.float32)
                scores = scores / math.sqrt(width // local_heads)
                ok = (q_row[:, None] == k_row[None, :]) | (q_idx[:, None] == k_idx[None, :])
                weight = jax.nn.softmax(jnp.where(ok, scores, NEG), axis=-1)
                return jnp.dot(weight, v, preferred_element_type=jnp.float32)

            queries = lax.dynamic_slice_in_dim(keys, seq_at * tokens, tokens, 0)
            att = lax.map(
                one_head,
                (by_head(queries, qkv[0]), by_head(keys, qkv[1]), by_head(keys, qkv[2]))
                + (codes(q_idx)[0], k_code),
            )
            att = att.transpose(1, 0, 2).reshape(tokens, width).astype(jnp.bfloat16)
            parts = jnp.dot(att, w_out, preferred_element_type=jnp.float32)
            old = lax.dynamic_slice_in_dim(parts, sec * own_rows, own_rows, 0)
            parts = lax.dynamic_update_slice_in_dim(parts, old + emb, sec * own_rows, 0)
            parts = jnp.stack(absolute(jnp.split(parts.T, n_sec, axis=0)))
            keep, send = parts[0::2], parts[1::2].astype(jnp.bfloat16)

        kept = keep + flip(send, section=1).astype(jnp.float32)
        out = kept[0] + flip(kept[1].astype(jnp.bfloat16), section=2).astype(jnp.float32)
        return out.astype(jnp.bfloat16).T[None]

    return per_device


def solution(mesh):
    placed = (
        P("dp", "seq", "section"),
        P(),
        P(("seq", "dp"), "section"),
        P(("seq", "dp"), "section"),
        P("section", ("seq", "dp")),
        P("section", None),
        P(),
        P(None, None, "section"),
        P("section", None),
        P("dp", None),
        P("section"),
        P("section"),
    )
    shape = mesh.shape
    return jax.shard_map(
        build(shape["section"], shape["seq"], shape["dp"]),
        mesh=mesh,
        in_specs=placed,
        out_specs=P("dp", "seq", "section"),
        check_vma=False,
    )
```

```python
import math

import jax
import jax.numpy as jnp
from jax import lax
from jax.experimental import pallas as pl
from jax.experimental.pallas import tpu as pltpu
from jax.sharding import PartitionSpec as P

NEG = -1e30
AXES = ("section", "seq", "dp")


def layer_norm(rows, gain):
    mean = jnp.mean(rows, axis=-1, keepdims=True)
    centered = rows - mean
    var = jnp.mean(centered * centered, axis=-1, keepdims=True)
    return centered * lax.rsqrt(var + 1e-06) * gain


def slide_place(lengths_row, index):
    ends = jnp.cumsum(lengths_row, dtype=jnp.int32)
    after = index[:, None] >= ends[None, :]
    slide = jnp.sum(after.astype(jnp.int32), axis=1, dtype=jnp.int32)
    before = jnp.sum(jnp.where(after, lengths_row[None, :], 0), axis=1, dtype=jnp.int32)
    return (slide, index - before)


def attend_kernel(*refs, heads, masks):
    blocks, (w_ref, out_w_ref, emb_ref, code_ref, keep_ref, send_ref) = refs[:-6], refs[-6:]
    sec = lax.axis_index("section")
    core, side = sec % 2, sec // 2
    own = blocks[0].shape[0]
    keys = jnp.concatenate([block[...] for block in blocks], axis=0)
    count, rows = keys.shape[0], own * len(masks)
    q_code = jnp.transpose(code_ref[:, :rows])
    width = w_ref.shape[1]
    size = width // heads
    scale = math.log2(math.e) / math.sqrt(size)

    def project(x, which):
        return lax.dot_general(
            x, w_ref[which], (((1,), (1,)), ((), ())), preferred_element_type=jnp.float32
        ).astype(jnp.bfloat16)

    key, query, value = project(keys, 1), project(keys[:rows], 0), project(keys, 2)
    lane_head = lax.broadcasted_iota(jnp.int32, (rows, width), 1) // size
    diag = lax.broadcasted_iota(jnp.int32, (rows, count), 0) == lax.broadcasted_iota(
        jnp.int32, (rows, count), 1
    )
    att = jnp.zeros((rows, width), jnp.float32)
    for h in range(heads):
        scores = lax.dot_general(
            jnp.where(lane_head == h, query, jnp.zeros_like(query)),
            key,
            (((1,), (1,)), ((), ())),
            preferred_element_type=jnp.float32,
        )
        ok = (q_code[:, h : h + 1] == code_ref[heads + h : heads + h + 1, :]) | diag
        scores = jnp.where(ok, scores, NEG)
        top = jnp.max(scores, axis=1, keepdims=True)
        weight = jnp.exp2((scores - top) * scale)
        total = jnp.sum(weight, axis=1, keepdims=True)
        mixed = jnp.dot(weight.astype(jnp.bfloat16), value, preferred_element_type=jnp.float32)
        att = jnp.where(lane_head == h, mixed / total, att)
    part = jnp.dot(
        out_w_ref[...], jnp.transpose(att).astype(jnp.bfloat16), preferred_element_type=jnp.float32
    )
    emb = jnp.transpose(emb_ref[...])
    for block, mask in enumerate(masks):
        piece = part[:, block * own : (block + 1) * own]
        if block == 0:
            piece = piece + emb
        at = pl.ds(pl.multiple_of((mask ^ sec) * own, own), own)
        for j in range(part.shape[0] // width // 2):
            low = piece[2 * j * width : (2 * j + 1) * width]
            high = piece[(2 * j + 1) * width : (2 * j + 2) * width]
            keep_ref[j ^ side, :, at] = jnp.where(core == 0, low, high)
            send_ref[j ^ side, :, at] = jnp.where(core == 0, high, low).astype(send_ref.dtype)


def build(n_sec, n_seq, n_dp):
    sizes = {"section": n_sec, "seq": n_seq, "dp": n_dp}

    def flip(x, **masks):
        names = tuple(a for a in AXES if masks.get(a))
        pairs = []
        total = math.prod(sizes[a] for a in names)
        for source in range(total):
            rest, coords = source, []
            for a in reversed(names):
                coords.append(rest % sizes[a])
                rest //= sizes[a]
            target = 0
            for a, c in zip(names, reversed(coords)):
                target = target * sizes[a] + (c ^ masks[a])
            pairs.append((source, target))
        return lax.ppermute(x, names if len(names) > 1 else names[0], pairs)

    def rotate(x, k):
        return lax.ppermute(x, "dp", [(i, (i + k) % n_dp) for i in range(n_dp)])

    def after(x, *others):
        return lax.optimization_barrier((x,) + others)[0]

    def absolute(blocks):
        stacked, sec = jnp.stack(blocks), lax.axis_index("section")
        return [lax.dynamic_index_in_dim(stacked, sec ^ j, 0, False) for j in range(n_sec)]

    def gather_section(x):
        across = flip(x, section=2)
        return [x, flip(after(x, across), section=1), across, flip(across, section=1)]

    def gather_rows(same, other, seq_at, dp_at):
        mats, rows, units = same.shape
        part = jnp.zeros((mats, n_dp * rows, units), same.dtype)
        for k in range(n_dp):
            block = rotate(other if k % 2 else same, k) if k else same
            part = lax.dynamic_update_slice(part, block, (0, ((dp_at - k) % n_dp) * rows, 0))
        whole = lax.all_gather(part, "seq", axis=1, tiled=True)
        return jnp.concatenate(absolute(jnp.split(whole, n_sec, axis=1)), axis=1)

    def row_of(y, k, rows):
        sec, seq_at, dp_at = (lax.axis_index(a) for a in AXES)
        block = (seq_at ^ y) * n_dp + (dp_at - k) % n_dp
        each = n_seq * n_dp // n_sec
        return ((block // each ^ sec) * each + block % each) * rows

    def place_rows(blocks):
        first = blocks[0, 2]
        mats, rows, units = first.shape
        whole = after(jnp.zeros((mats, n_seq * n_dp * rows, units), first.dtype), first)
        for (y, k), block in blocks.items():
            whole = lax.dynamic_update_slice(whole, block, (0, row_of(y, k, rows), 0))
        return whole

    def per_device(
        tile_feats,
        tile_gain,
        w_gate,
        w_up,
        w_down,
        w_proj,
        slide_gain,
        w_qkv,
        w_out,
        lengths,
        seg_len,
        rate,
    ):
        sec = lax.axis_index("section")
        seq_at = lax.axis_index("seq")
        dp_at = lax.axis_index("dp")
        core, side, odd = sec % 2, sec // 2, dp_at % 2
        mine = tile_feats[0]
        tokens, feats = mine.shape
        own_rows = tokens // n_sec
        half = w_gate.shape[1] // 2

        def halves(x, which):
            return lax.dynamic_slice_in_dim(x, which * half, half, x.ndim - 1)

        pair = jnp.stack([w_gate, w_up])
        pair_same, pair_other = halves(pair, odd), halves(pair, 1 - odd)
        down = w_down.T[None]
        down_same, down_other = halves(down, odd), halves(down, 1 - odd)
        ordered = n_seq == 2 and n_dp == 4

        if n_seq == 2:
            masks = (0, 2, 1, 3)
            span = jnp.arange(own_rows, dtype=jnp.int32)
            k_idx = jnp.concatenate(
                [(seq_at ^ y) * tokens + (sec ^ m) * own_rows + span for y in (0, 1) for m in masks]
            )
            q_idx = k_idx[:tokens]
        else:
            k_idx = jnp.arange(n_seq * tokens, dtype=jnp.int32)
            q_idx = seq_at * tokens + jnp.arange(tokens, dtype=jnp.int32)
        count = k_idx.shape[0]
        local_heads = seg_len.shape[0]
        heads = sec * local_heads + jnp.arange(local_heads, dtype=jnp.int32)

        def codes(index):
            slide, pos = slide_place(lengths[0], index)
            block = slide[None, :] * count + pos[None, :] // seg_len[:, None]
            return block, pos[None, :] % rate[:, None] == (heads % rate)[:, None]

        k_block, picked = codes(k_idx)
        k_code = jnp.where(picked, k_block, -1)
        code = jnp.concatenate([k_block, k_code], axis=0)

        own_at = sec * own_rows
        gain = jnp.concatenate(absolute(jnp.split(tile_gain, n_sec)))
        out_w = w_out.T

        if ordered:
            g, d = {(0, 0): pair_same}, {(0, 0): down_same}
            beside = flip(mine, dp=1)
            mine_x = flip(mine, section=2)
            g[0, 2] = rotate(pair_same, 2)
            g[1, 0] = flip(pair_same, seq=1)
            d[1, 0] = flip(down_same, seq=1)
            beside_x = flip(beside, section=2)
            for k in (1, 3):
                g[0, k] = rotate(after(pair_other, g[0, 2], d[1, 0], g[1, 0], mine_x), k)
            g[1, 2] = flip(g[0, 2], seq=1)
            across = after(jnp.concatenate([mine_x, beside_x], axis=0), g[0, 2], g[1, 2])
            both = after(jnp.concatenate([mine, beside], axis=0), across)
            both_c, across_c = flip(both, section=1), flip(across, section=1)
            proj_x = flip(after(w_proj, both_c, across_c), section=2)
            far = rotate(after(down_same, g[0, 1]), 2)
            rows = jnp.concatenate([both, both_c, across, across_c], axis=1)
            normed = layer_norm(rows.astype(jnp.float32), gain).astype(jnp.bfloat16)
            g[1, 1], g[1, 3] = (after(flip(g[0, k], seq=1), normed) for k in (1, 3))
            gate_up = place_rows(g)
            d[0, 2] = after(far, normed)
            for k in (1, 3):
                d[0, k] = rotate(after(down_other, d[0, 2], code, out_w), k)
            proj_c = flip(after(w_proj, proj_x, d[0, 1]), section=1)
            proj_xc = flip(after(proj_x, d[0, 1]), section=1)
            proj = jnp.concatenate([w_proj, proj_c, proj_x, proj_xc], axis=0)
            for k in (2, 1, 3):
                d[1, k] = flip(d[0, k], seq=1)
        else:
            gate_up = gather_rows(pair_same, pair_other, seq_at, dp_at)
            down_all = gather_rows(down_same, down_other, seq_at, dp_at)[0]
            both = jnp.concatenate([mine, flip(mine, dp=1)], axis=0)
            rows = jnp.concatenate(gather_section(both), axis=1)
            normed = layer_norm(rows.astype(jnp.float32), gain).astype(jnp.bfloat16)
            proj = jnp.concatenate(gather_section(w_proj), axis=0)

        residual = jnp.dot(
            lax.dynamic_slice_in_dim(rows[:tokens], own_at, own_rows, 0),
            proj,
            preferred_element_type=jnp.float32,
        )
        normed = after(normed, residual)
        gate = jnp.dot(normed, gate_up[0], preferred_element_type=jnp.float32)
        up = jnp.dot(normed, gate_up[1], preferred_element_type=jnp.float32)
        hidden = (jax.nn.silu(gate) * up).astype(jnp.bfloat16)
        hidden = hidden.reshape(2, n_sec // 2, 2, own_rows, half)

        def fold(proj_rows, down_rows):
            return lax.dot_general(
                proj_rows, down_rows, (((0,), (0,)), ((), ())), preferred_element_type=jnp.float32
            )

        if ordered:
            late = [d.pop((1, 1)), d.pop((1, 3))]
            folded = fold(proj, after(place_rows(d)[0], hidden))
            for k, block in zip((1, 3), late):
                at = row_of(1, k, block.shape[1])
                folded = folded + fold(
                    lax.dynamic_slice_in_dim(proj, at, block.shape[1], 0), block[0]
                )
        else:
            folded = fold(proj, down_all)
        folded = folded.astype(jnp.bfloat16)

        def project(x):
            return lax.dot_general(
                x, folded, (((x.ndim - 1,), (1,)), ((), ())), preferred_element_type=jnp.float32
            )

        send = project(lax.dynamic_index_in_dim(hidden, 1 - core, 2, False)).astype(jnp.bfloat16)
        got = flip(send, section=1)
        kept = after(project(lax.dynamic_index_in_dim(hidden, core, 2, False)), send)
        kept = kept + got.astype(jnp.float32)
        here = lax.dynamic_index_in_dim(kept, side, 1, False)
        there = lax.dynamic_index_in_dim(kept, 1 - side, 1, False).astype(jnp.bfloat16)
        from_x = flip(there[0], section=2)
        from_z = flip(here[1].astype(jnp.bfloat16), dp=1)
        from_xz = flip(there[1], section=2, dp=1)
        emb = (
            residual
            + here[0]
            + from_x.astype(jnp.float32)
            + from_z.astype(jnp.float32)
            + from_xz.astype(jnp.float32)
        )
        slide_normed = layer_norm(emb, slide_gain).astype(jnp.bfloat16)

        vmem = pl.BlockSpec(memory_space=pltpu.VMEM)
        if n_seq == 2:
            keys = [
                slide_normed,
                flip(slide_normed, section=2),
                flip(slide_normed, seq=1),
                flip(slide_normed, section=2, seq=1),
            ]
            others = [flip(block, section=1) for block in keys]
            keys = keys[:2] + others[:2] + keys[2:] + others[2:]
        else:
            keys = lax.all_gather(slide_normed, ("seq", "section"), axis=0, tiled=True)

        width = w_qkv.shape[2]
        qkv = jnp.swapaxes(w_qkv, 1, 2)
        if n_seq == 2:
            keep, send = pl.pallas_call(
                lambda *refs: attend_kernel(*refs, heads=local_heads, masks=masks),
                out_shape=[
                    jax.ShapeDtypeStruct((2, width, tokens), jnp.float32),
                    jax.ShapeDtypeStruct((2, width, tokens), jnp.bfloat16),
                ],
                in_specs=[vmem] * 12,
                out_specs=[vmem] * 2,
                compiler_params=pltpu.CompilerParams(vmem_limit_bytes=16 * 2**20),
                cost_estimate=pl.CostEstimate(
                    flops=2 * count * width * (3 * 768 + 2 * local_heads * tokens),
                    bytes_accessed=8 * 2**20,
                    transcendentals=local_heads * tokens * count,
                ),
            )(*keys, qkv, out_w, emb, code)
        else:

            def by_head(x, matrix):
                x = jnp.dot(x, matrix.T, preferred_element_type=jnp.float32)
                x = x.astype(jnp.bfloat16).reshape(x.shape[0], local_heads, width // local_heads)
                return x.transpose(1, 0, 2)

            def one_head(args):
                q, k, v, q_row, k_row = args
                scores = jnp.dot(q, k.T, preferred_element_type=jnp.float32)
                scores = scores / math.sqrt(width // local_heads)
                ok = (q_row[:, None] == k_row[None, :]) | (q_idx[:, None] == k_idx[None, :])
                weight = jax.nn.softmax(jnp.where(ok, scores, NEG), axis=-1)
                return jnp.dot(weight, v, preferred_element_type=jnp.float32)

            queries = lax.dynamic_slice_in_dim(keys, seq_at * tokens, tokens, 0)
            att = lax.map(
                one_head,
                (by_head(queries, qkv[0]), by_head(keys, qkv[1]), by_head(keys, qkv[2]))
                + (codes(q_idx)[0], k_code),
            )
            att = att.transpose(1, 0, 2).reshape(tokens, width).astype(jnp.bfloat16)
            parts = jnp.dot(att, w_out, preferred_element_type=jnp.float32)
            old = lax.dynamic_slice_in_dim(parts, sec * own_rows, own_rows, 0)
            parts = lax.dynamic_update_slice_in_dim(parts, old + emb, sec * own_rows, 0)
            parts = jnp.stack(absolute(jnp.split(parts.T, n_sec, axis=0)))
            keep, send = parts[0::2], parts[1::2].astype(jnp.bfloat16)

        kept = keep + flip(send, section=1).astype(jnp.float32)
        out = kept[0] + flip(kept[1].astype(jnp.bfloat16), section=2).astype(jnp.float32)
        return out.astype(jnp.bfloat16).T[None]

    return per_device


def solution(mesh):
    placed = (
        P("dp", "seq", "section"),
        P(),
        P(("seq", "dp"), "section"),
        P(("seq", "dp"), "section"),
        P("section", ("seq", "dp")),
        P("section", None),
        P(),
        P(None, None, "section"),
        P("section", None),
        P("dp", None),
        P("section"),
        P("section"),
    )
    shape = mesh.shape
    return jax.shard_map(
        build(shape["section"], shape["seq"], shape["dp"]),
        mesh=mesh,
        in_specs=placed,
        out_specs=P("dp", "seq", "section"),
        check_vma=False,
    )
```

```python
import math

import jax
import jax.numpy as jnp
from jax import lax
from jax.experimental import pallas as pl
from jax.experimental.pallas import tpu as pltpu
from jax.sharding import PartitionSpec as P

NEG = -1e30
AXES = ("section", "seq", "dp")


def layer_norm(rows, gain):
    mean = jnp.mean(rows, axis=-1, keepdims=True)
    centered = rows - mean
    var = jnp.mean(centered * centered, axis=-1, keepdims=True)
    return centered * lax.rsqrt(var + 1e-06) * gain


def slide_place(lengths_row, index):
    ends = jnp.cumsum(lengths_row, dtype=jnp.int32)
    after = index[:, None] >= ends[None, :]
    slide = jnp.sum(after.astype(jnp.int32), axis=1, dtype=jnp.int32)
    before = jnp.sum(jnp.where(after, lengths_row[None, :], 0), axis=1, dtype=jnp.int32)
    return (slide, index - before)


def attend_kernel(*refs, heads, masks):
    blocks, (w_ref, out_w_ref, emb_ref, code_ref, keep_ref, send_ref) = refs[:-6], refs[-6:]
    sec = lax.axis_index("section")
    core, side = sec % 2, sec // 2
    own = blocks[0].shape[0]
    keys = jnp.concatenate([block[...] for block in blocks], axis=0)
    count, rows = keys.shape[0], own * len(masks)
    q_code = jnp.transpose(code_ref[:, :rows])
    width = w_ref.shape[1]
    size = width // heads
    scale = math.log2(math.e) / math.sqrt(size)

    def project(x, which):
        return lax.dot_general(
            x, w_ref[which], (((1,), (1,)), ((), ())), preferred_element_type=jnp.float32
        ).astype(jnp.bfloat16)

    key, query, value = project(keys, 1), project(keys[:rows], 0), project(keys, 2)
    lane_head = lax.broadcasted_iota(jnp.int32, (rows, width), 1) // size
    diag = lax.broadcasted_iota(jnp.int32, (rows, count), 0) == lax.broadcasted_iota(
        jnp.int32, (rows, count), 1
    )
    att = jnp.zeros((rows, width), jnp.float32)
    for h in range(heads):
        scores = lax.dot_general(
            jnp.where(lane_head == h, query, jnp.zeros_like(query)),
            key,
            (((1,), (1,)), ((), ())),
            preferred_element_type=jnp.float32,
        )
        ok = (q_code[:, h : h + 1] == code_ref[heads + h : heads + h + 1, :]) | diag
        scores = jnp.where(ok, scores, NEG)
        top = jnp.max(scores, axis=1, keepdims=True)
        weight = jnp.exp2((scores - top) * scale)
        total = jnp.sum(weight, axis=1, keepdims=True)
        mixed = jnp.dot(weight.astype(jnp.bfloat16), value, preferred_element_type=jnp.float32)
        att = jnp.where(lane_head == h, mixed / total, att)
    part = jnp.dot(
        out_w_ref[...], jnp.transpose(att).astype(jnp.bfloat16), preferred_element_type=jnp.float32
    )
    emb = jnp.transpose(emb_ref[...])
    for block, mask in enumerate(masks):
        piece = part[:, block * own : (block + 1) * own]
        if block == 0:
            piece = piece + emb
        at = pl.ds(pl.multiple_of((mask ^ sec) * own, own), own)
        for j in range(part.shape[0] // width // 2):
            low = piece[2 * j * width : (2 * j + 1) * width]
            high = piece[(2 * j + 1) * width : (2 * j + 2) * width]
            keep_ref[j ^ side, :, at] = jnp.where(core == 0, low, high)
            send_ref[j ^ side, :, at] = jnp.where(core == 0, high, low).astype(send_ref.dtype)


def build(n_sec, n_seq, n_dp):
    sizes = {"section": n_sec, "seq": n_seq, "dp": n_dp}

    def flip(x, **masks):
        names = tuple(a for a in AXES if masks.get(a))
        pairs = []
        total = math.prod(sizes[a] for a in names)
        for source in range(total):
            rest, coords = source, []
            for a in reversed(names):
                coords.append(rest % sizes[a])
                rest //= sizes[a]
            target = 0
            for a, c in zip(names, reversed(coords)):
                target = target * sizes[a] + (c ^ masks[a])
            pairs.append((source, target))
        return lax.ppermute(x, names if len(names) > 1 else names[0], pairs)

    def rotate(x, k):
        return lax.ppermute(x, "dp", [(i, (i + k) % n_dp) for i in range(n_dp)])

    def after(x, *others):
        return lax.optimization_barrier((x,) + others)[0]

    def absolute(blocks):
        stacked, sec = jnp.stack(blocks), lax.axis_index("section")
        return [lax.dynamic_index_in_dim(stacked, sec ^ j, 0, False) for j in range(n_sec)]

    def gather_section(x):
        across = flip(x, section=2)
        return [x, flip(after(x, across), section=1), across, flip(across, section=1)]

    def gather_rows(same, other, seq_at, dp_at):
        mats, rows, units = same.shape
        part = jnp.zeros((mats, n_dp * rows, units), same.dtype)
        for k in range(n_dp):
            block = rotate(other if k % 2 else same, k) if k else same
            part = lax.dynamic_update_slice(part, block, (0, ((dp_at - k) % n_dp) * rows, 0))
        whole = lax.all_gather(part, "seq", axis=1, tiled=True)
        return jnp.concatenate(absolute(jnp.split(whole, n_sec, axis=1)), axis=1)

    def row_of(y, k, rows):
        sec, seq_at, dp_at = (lax.axis_index(a) for a in AXES)
        block = (seq_at ^ y) * n_dp + (dp_at - k) % n_dp
        each = n_seq * n_dp // n_sec
        return ((block // each ^ sec) * each + block % each) * rows

    def place_rows(blocks):
        first = blocks[0, 2]
        mats, rows, units = first.shape
        whole = after(jnp.zeros((mats, n_seq * n_dp * rows, units), first.dtype), first)
        for (y, k), block in blocks.items():
            whole = lax.dynamic_update_slice(whole, block, (0, row_of(y, k, rows), 0))
        return whole

    def per_device(
        tile_feats,
        tile_gain,
        w_gate,
        w_up,
        w_down,
        w_proj,
        slide_gain,
        w_qkv,
        w_out,
        lengths,
        seg_len,
        rate,
    ):
        sec = lax.axis_index("section")
        seq_at = lax.axis_index("seq")
        dp_at = lax.axis_index("dp")
        core, side, odd = sec % 2, sec // 2, dp_at % 2
        mine = tile_feats[0]
        tokens, feats = mine.shape
        own_rows = tokens // n_sec
        half = w_gate.shape[1] // 2

        def halves(x, which):
            return lax.dynamic_slice_in_dim(x, which * half, half, x.ndim - 1)

        pair = jnp.stack([w_gate, w_up])
        pair_same, pair_other = halves(pair, odd), halves(pair, 1 - odd)
        down = w_down.T[None]
        down_same, down_other = halves(down, odd), halves(down, 1 - odd)
        ordered = n_seq == 2 and n_dp == 4

        if n_seq == 2:
            masks = (0, 2, 1, 3)
            span = jnp.arange(own_rows, dtype=jnp.int32)
            k_idx = jnp.concatenate(
                [(seq_at ^ y) * tokens + (sec ^ m) * own_rows + span for y in (0, 1) for m in masks]
            )
            q_idx = k_idx[:tokens]
        else:
            k_idx = jnp.arange(n_seq * tokens, dtype=jnp.int32)
            q_idx = seq_at * tokens + jnp.arange(tokens, dtype=jnp.int32)
        count = k_idx.shape[0]
        local_heads = seg_len.shape[0]
        heads = sec * local_heads + jnp.arange(local_heads, dtype=jnp.int32)

        def codes(index):
            slide, pos = slide_place(lengths[0], index)
            block = slide[None, :] * count + pos[None, :] // seg_len[:, None]
            return block, pos[None, :] % rate[:, None] == (heads % rate)[:, None]

        k_block, picked = codes(k_idx)
        k_code = jnp.where(picked, k_block, -1)
        code = jnp.concatenate([k_block, k_code], axis=0)

        own_at = sec * own_rows
        gain = jnp.concatenate(absolute(jnp.split(tile_gain, n_sec)))
        out_w = w_out.T

        if ordered:
            g, d = {(0, 0): pair_same}, {(0, 0): down_same}
            beside = flip(mine, dp=1)
            mine_x = flip(mine, section=2)
            g[0, 2] = rotate(pair_same, 2)
            g[1, 0] = flip(pair_same, seq=1)
            d[1, 0] = flip(down_same, seq=1)
            beside_x = flip(beside, section=2)
            proj_x = flip(after(w_proj, mine_x), section=2)
            for k in (1, 3):
                g[0, k] = rotate(after(pair_other, g[0, 2], d[1, 0], g[1, 0], mine_x), k)
            g[1, 2] = flip(g[0, 2], seq=1)
            across = after(jnp.concatenate([mine_x, beside_x], axis=0), g[0, 2], g[1, 2])
            both = after(jnp.concatenate([mine, beside], axis=0), across)
            both_c, across_c = flip(both, section=1), flip(across, section=1)
            far = rotate(after(down_same, g[0, 1]), 2)
            rows = jnp.concatenate([both, both_c, across, across_c], axis=1)
            normed = layer_norm(rows.astype(jnp.float32), gain).astype(jnp.bfloat16)
            g[1, 1], g[1, 3] = (after(flip(g[0, k], seq=1), normed) for k in (1, 3))
            gate_up = place_rows(g)
            d[0, 2] = after(far, normed)
            for k in (1, 3):
                d[0, k] = rotate(after(down_other, d[0, 2], code, out_w), k)
            proj_c = flip(after(w_proj, proj_x, d[0, 1]), section=1)
            proj_xc = flip(after(proj_x, d[0, 1]), section=1)
            proj = jnp.concatenate([w_proj, proj_c, proj_x, proj_xc], axis=0)
            for k in (2, 1, 3):
                d[1, k] = flip(d[0, k], seq=1)
        else:
            gate_up = gather_rows(pair_same, pair_other, seq_at, dp_at)
            down_all = gather_rows(down_same, down_other, seq_at, dp_at)[0]
            both = jnp.concatenate([mine, flip(mine, dp=1)], axis=0)
            rows = jnp.concatenate(gather_section(both), axis=1)
            normed = layer_norm(rows.astype(jnp.float32), gain).astype(jnp.bfloat16)
            proj = jnp.concatenate(gather_section(w_proj), axis=0)

        residual = jnp.dot(
            lax.dynamic_slice_in_dim(rows[:tokens], own_at, own_rows, 0),
            proj,
            preferred_element_type=jnp.float32,
        )
        gate = jnp.dot(normed, gate_up[0], preferred_element_type=jnp.float32)
        up = jnp.dot(normed, gate_up[1], preferred_element_type=jnp.float32)
        hidden = (jax.nn.silu(gate) * up).astype(jnp.bfloat16)
        hidden = hidden.reshape(2, n_sec // 2, 2, own_rows, half)

        def fold(proj_rows, down_rows):
            return lax.dot_general(
                proj_rows, down_rows, (((0,), (0,)), ((), ())), preferred_element_type=jnp.float32
            )

        if ordered:
            late = [d.pop((1, 1)), d.pop((1, 3))]
            proj = after(proj, residual)
            folded = fold(proj, after(place_rows(d)[0], hidden))
            for k, block in zip((1, 3), late):
                at = row_of(1, k, block.shape[1])
                folded = folded + fold(
                    lax.dynamic_slice_in_dim(proj, at, block.shape[1], 0), block[0]
                )
        else:
            folded = fold(proj, down_all)
        folded = folded.astype(jnp.bfloat16)

        def project(x):
            return lax.dot_general(
                x, folded, (((x.ndim - 1,), (1,)), ((), ())), preferred_element_type=jnp.float32
            )

        send = project(lax.dynamic_index_in_dim(hidden, 1 - core, 2, False)).astype(jnp.bfloat16)
        got = flip(send, section=1)
        kept = after(project(lax.dynamic_index_in_dim(hidden, core, 2, False)), send)
        kept = kept + got.astype(jnp.float32)
        here = lax.dynamic_index_in_dim(kept, side, 1, False)
        there = lax.dynamic_index_in_dim(kept, 1 - side, 1, False).astype(jnp.bfloat16)
        from_x = flip(there[0], section=2)
        from_z = flip(here[1].astype(jnp.bfloat16), dp=1)
        from_xz = flip(there[1], section=2, dp=1)
        emb = (
            residual
            + here[0]
            + from_x.astype(jnp.float32)
            + from_z.astype(jnp.float32)
            + from_xz.astype(jnp.float32)
        )
        slide_normed = layer_norm(emb, slide_gain).astype(jnp.bfloat16)

        vmem = pl.BlockSpec(memory_space=pltpu.VMEM)
        if n_seq == 2:
            keys = [
                slide_normed,
                flip(slide_normed, section=2),
                flip(slide_normed, seq=1),
                flip(slide_normed, section=2, seq=1),
            ]
            others = [flip(block, section=1) for block in keys]
            keys = keys[:2] + others[:2] + keys[2:] + others[2:]
        else:
            keys = lax.all_gather(slide_normed, ("seq", "section"), axis=0, tiled=True)

        width = w_qkv.shape[2]
        qkv = jnp.swapaxes(w_qkv, 1, 2)
        if n_seq == 2:
            keep, send = pl.pallas_call(
                lambda *refs: attend_kernel(*refs, heads=local_heads, masks=masks),
                out_shape=[
                    jax.ShapeDtypeStruct((2, width, tokens), jnp.float32),
                    jax.ShapeDtypeStruct((2, width, tokens), jnp.bfloat16),
                ],
                in_specs=[vmem] * 12,
                out_specs=[vmem] * 2,
                compiler_params=pltpu.CompilerParams(vmem_limit_bytes=16 * 2**20),
                cost_estimate=pl.CostEstimate(
                    flops=2 * count * width * (3 * 768 + 2 * local_heads * tokens),
                    bytes_accessed=8 * 2**20,
                    transcendentals=local_heads * tokens * count,
                ),
            )(*keys, qkv, out_w, emb, code)
        else:

            def by_head(x, matrix):
                x = jnp.dot(x, matrix.T, preferred_element_type=jnp.float32)
                x = x.astype(jnp.bfloat16).reshape(x.shape[0], local_heads, width // local_heads)
                return x.transpose(1, 0, 2)

            def one_head(args):
                q, k, v, q_row, k_row = args
                scores = jnp.dot(q, k.T, preferred_element_type=jnp.float32)
                scores = scores / math.sqrt(width // local_heads)
                ok = (q_row[:, None] == k_row[None, :]) | (q_idx[:, None] == k_idx[None, :])
                weight = jax.nn.softmax(jnp.where(ok, scores, NEG), axis=-1)
                return jnp.dot(weight, v, preferred_element_type=jnp.float32)

            queries = lax.dynamic_slice_in_dim(keys, seq_at * tokens, tokens, 0)
            att = lax.map(
                one_head,
                (by_head(queries, qkv[0]), by_head(keys, qkv[1]), by_head(keys, qkv[2]))
                + (codes(q_idx)[0], k_code),
            )
            att = att.transpose(1, 0, 2).reshape(tokens, width).astype(jnp.bfloat16)
            parts = jnp.dot(att, w_out, preferred_element_type=jnp.float32)
            old = lax.dynamic_slice_in_dim(parts, sec * own_rows, own_rows, 0)
            parts = lax.dynamic_update_slice_in_dim(parts, old + emb, sec * own_rows, 0)
            parts = jnp.stack(absolute(jnp.split(parts.T, n_sec, axis=0)))
            keep, send = parts[0::2], parts[1::2].astype(jnp.bfloat16)

        kept = keep + flip(send, section=1).astype(jnp.float32)
        out = kept[0] + flip(kept[1].astype(jnp.bfloat16), section=2).astype(jnp.float32)
        return out.astype(jnp.bfloat16).T[None]

    return per_device


def solution(mesh):
    placed = (
        P("dp", "seq", "section"),
        P(),
        P(("seq", "dp"), "section"),
        P(("seq", "dp"), "section"),
        P("section", ("seq", "dp")),
        P("section", None),
        P(),
        P(None, None, "section"),
        P("section", None),
        P("dp", None),
        P("section"),
        P("section"),
    )
    shape = mesh.shape
    return jax.shard_map(
        build(shape["section"], shape["seq"], shape["dp"]),
        mesh=mesh,
        in_specs=placed,
        out_specs=P("dp", "seq", "section"),
        check_vma=False,
    )
```

```python
import math

import jax
import jax.numpy as jnp
from jax import lax
from jax.experimental import pallas as pl
from jax.experimental.pallas import tpu as pltpu
from jax.sharding import PartitionSpec as P

NEG = -1e30
AXES = ("section", "seq", "dp")


def layer_norm(rows, gain):
    mean = jnp.mean(rows, axis=-1, keepdims=True)
    centered = rows - mean
    var = jnp.mean(centered * centered, axis=-1, keepdims=True)
    return centered * lax.rsqrt(var + 1e-06) * gain


def slide_place(lengths_row, index):
    ends = jnp.cumsum(lengths_row, dtype=jnp.int32)
    after = index[:, None] >= ends[None, :]
    slide = jnp.sum(after.astype(jnp.int32), axis=1, dtype=jnp.int32)
    before = jnp.sum(jnp.where(after, lengths_row[None, :], 0), axis=1, dtype=jnp.int32)
    return (slide, index - before)


def attend_kernel(*refs, heads, masks):
    blocks, (w_ref, out_w_ref, emb_ref, code_ref, keep_ref, send_ref) = refs[:-6], refs[-6:]
    sec = lax.axis_index("section")
    core, side = sec % 2, sec // 2
    own = blocks[0].shape[0]
    keys = jnp.concatenate([block[...] for block in blocks], axis=0)
    count, rows = keys.shape[0], own * len(masks)
    q_code = jnp.transpose(code_ref[:, :rows])
    width = w_ref.shape[1]
    size = width // heads
    scale = math.log2(math.e) / math.sqrt(size)

    def project(x, which):
        return lax.dot_general(
            x, w_ref[which], (((1,), (1,)), ((), ())), preferred_element_type=jnp.float32
        ).astype(jnp.bfloat16)

    key, query, value = project(keys, 1), project(keys[:rows], 0), project(keys, 2)
    lane_head = lax.broadcasted_iota(jnp.int32, (rows, width), 1) // size
    diag = lax.broadcasted_iota(jnp.int32, (rows, count), 0) == lax.broadcasted_iota(
        jnp.int32, (rows, count), 1
    )
    att = jnp.zeros((rows, width), jnp.float32)
    for h in range(heads):
        scores = lax.dot_general(
            jnp.where(lane_head == h, query, jnp.zeros_like(query)),
            key,
            (((1,), (1,)), ((), ())),
            preferred_element_type=jnp.float32,
        )
        ok = (q_code[:, h : h + 1] == code_ref[heads + h : heads + h + 1, :]) | diag
        scores = jnp.where(ok, scores, NEG)
        top = jnp.max(scores, axis=1, keepdims=True)
        weight = jnp.exp2((scores - top) * scale)
        total = jnp.sum(weight, axis=1, keepdims=True)
        mixed = jnp.dot(weight.astype(jnp.bfloat16), value, preferred_element_type=jnp.float32)
        att = jnp.where(lane_head == h, mixed / total, att)
    part = jnp.dot(
        out_w_ref[...], jnp.transpose(att).astype(jnp.bfloat16), preferred_element_type=jnp.float32
    )
    emb = jnp.transpose(emb_ref[...])
    for block, mask in enumerate(masks):
        piece = part[:, block * own : (block + 1) * own]
        if block == 0:
            piece = piece + emb
        at = pl.ds(pl.multiple_of((mask ^ sec) * own, own), own)
        for j in range(part.shape[0] // width // 2):
            low = piece[2 * j * width : (2 * j + 1) * width]
            high = piece[(2 * j + 1) * width : (2 * j + 2) * width]
            keep_ref[j ^ side, :, at] = jnp.where(core == 0, low, high)
            send_ref[j ^ side, :, at] = jnp.where(core == 0, high, low).astype(send_ref.dtype)


def build(n_sec, n_seq, n_dp):
    sizes = {"section": n_sec, "seq": n_seq, "dp": n_dp}

    def flip(x, **masks):
        names = tuple(a for a in AXES if masks.get(a))
        pairs = []
        total = math.prod(sizes[a] for a in names)
        for source in range(total):
            rest, coords = source, []
            for a in reversed(names):
                coords.append(rest % sizes[a])
                rest //= sizes[a]
            target = 0
            for a, c in zip(names, reversed(coords)):
                target = target * sizes[a] + (c ^ masks[a])
            pairs.append((source, target))
        return lax.ppermute(x, names if len(names) > 1 else names[0], pairs)

    def rotate(x, k):
        return lax.ppermute(x, "dp", [(i, (i + k) % n_dp) for i in range(n_dp)])

    def after(x, *others):
        return lax.optimization_barrier((x,) + others)[0]

    def absolute(blocks):
        stacked, sec = jnp.stack(blocks), lax.axis_index("section")
        return [lax.dynamic_index_in_dim(stacked, sec ^ j, 0, False) for j in range(n_sec)]

    def gather_section(x):
        across = flip(x, section=2)
        return [x, flip(after(x, across), section=1), across, flip(across, section=1)]

    def gather_rows(same, other, seq_at, dp_at):
        mats, rows, units = same.shape
        part = jnp.zeros((mats, n_dp * rows, units), same.dtype)
        for k in range(n_dp):
            block = rotate(other if k % 2 else same, k) if k else same
            part = lax.dynamic_update_slice(part, block, (0, ((dp_at - k) % n_dp) * rows, 0))
        whole = lax.all_gather(part, "seq", axis=1, tiled=True)
        return jnp.concatenate(absolute(jnp.split(whole, n_sec, axis=1)), axis=1)

    def row_of(y, k, rows):
        sec, seq_at, dp_at = (lax.axis_index(a) for a in AXES)
        block = (seq_at ^ y) * n_dp + (dp_at - k) % n_dp
        each = n_seq * n_dp // n_sec
        return ((block // each ^ sec) * each + block % each) * rows

    def place_rows(blocks):
        first = blocks[0, 2]
        mats, rows, units = first.shape
        whole = after(jnp.zeros((mats, n_seq * n_dp * rows, units), first.dtype), first)
        for (y, k), block in blocks.items():
            whole = lax.dynamic_update_slice(whole, block, (0, row_of(y, k, rows), 0))
        return whole

    def per_device(
        tile_feats,
        tile_gain,
        w_gate,
        w_up,
        w_down,
        w_proj,
        slide_gain,
        w_qkv,
        w_out,
        lengths,
        seg_len,
        rate,
    ):
        sec = lax.axis_index("section")
        seq_at = lax.axis_index("seq")
        dp_at = lax.axis_index("dp")
        core, side, odd = sec % 2, sec // 2, dp_at % 2
        mine = tile_feats[0]
        tokens, feats = mine.shape
        own_rows = tokens // n_sec
        half = w_gate.shape[1] // 2

        def halves(x, which):
            return lax.dynamic_slice_in_dim(x, which * half, half, x.ndim - 1)

        pair = jnp.stack([w_gate, w_up])
        pair_same, pair_other = halves(pair, odd), halves(pair, 1 - odd)
        down = w_down.T[None]
        down_same, down_other = halves(down, odd), halves(down, 1 - odd)
        ordered = n_seq == 2 and n_dp == 4

        if n_seq == 2:
            masks = (0, 2, 1, 3)
            span = jnp.arange(own_rows, dtype=jnp.int32)
            k_idx = jnp.concatenate(
                [(seq_at ^ y) * tokens + (sec ^ m) * own_rows + span for y in (0, 1) for m in masks]
            )
            q_idx = k_idx[:tokens]
        else:
            k_idx = jnp.arange(n_seq * tokens, dtype=jnp.int32)
            q_idx = seq_at * tokens + jnp.arange(tokens, dtype=jnp.int32)
        count = k_idx.shape[0]
        local_heads = seg_len.shape[0]
        heads = sec * local_heads + jnp.arange(local_heads, dtype=jnp.int32)

        def codes(index):
            slide, pos = slide_place(lengths[0], index)
            block = slide[None, :] * count + pos[None, :] // seg_len[:, None]
            return block, pos[None, :] % rate[:, None] == (heads % rate)[:, None]

        k_block, picked = codes(k_idx)
        k_code = jnp.where(picked, k_block, -1)
        code = jnp.concatenate([k_block, k_code], axis=0)

        own_at = sec * own_rows
        gain = jnp.concatenate(absolute(jnp.split(tile_gain, n_sec)))
        out_w = w_out.T

        if ordered:
            g, d = {(0, 0): pair_same}, {(0, 0): down_same}
            beside = flip(mine, dp=1)
            mine_x = flip(mine, section=2)
            g[0, 2] = rotate(pair_same, 2)
            g[1, 0] = flip(pair_same, seq=1)
            d[1, 0] = flip(down_same, seq=1)
            beside_x = flip(beside, section=2)
            proj_x = flip(after(w_proj, mine_x), section=2)
            for k in (1, 3):
                g[0, k] = rotate(after(pair_other, g[0, 2], d[1, 0], g[1, 0], mine_x), k)
            g[1, 2] = flip(g[0, 2], seq=1)
            across = after(jnp.concatenate([mine_x, beside_x], axis=0), g[0, 2], g[1, 2])
            both = after(jnp.concatenate([mine, beside], axis=0), across)
            both_c, across_c = flip(both, section=1), flip(across, section=1)
            far = rotate(after(down_same, g[0, 1]), 2)
            rows = jnp.concatenate([both, both_c, across, across_c], axis=1)
            normed = layer_norm(rows.astype(jnp.float32), gain).astype(jnp.bfloat16)
            g[1, 1], g[1, 3] = (after(flip(g[0, k], seq=1), normed) for k in (1, 3))
            gate_up = place_rows(g)
            d[0, 2] = after(far, normed)
            for k in (1, 3):
                d[0, k] = rotate(after(down_other, d[0, 2], code, out_w), k)
            proj_c = flip(after(w_proj, proj_x, d[0, 1]), section=1)
            proj_xc = flip(after(proj_x, d[0, 1]), section=1)
            proj = jnp.concatenate([w_proj, proj_c, proj_x, proj_xc], axis=0)
            for k in (2, 1, 3):
                d[1, k] = flip(d[0, k], seq=1)
        else:
            gate_up = gather_rows(pair_same, pair_other, seq_at, dp_at)
            down_all = gather_rows(down_same, down_other, seq_at, dp_at)[0]
            both = jnp.concatenate([mine, flip(mine, dp=1)], axis=0)
            rows = jnp.concatenate(gather_section(both), axis=1)
            normed = layer_norm(rows.astype(jnp.float32), gain).astype(jnp.bfloat16)
            proj = jnp.concatenate(gather_section(w_proj), axis=0)

        residual = jnp.dot(
            lax.dynamic_slice_in_dim(rows[:tokens], own_at, own_rows, 0),
            proj,
            preferred_element_type=jnp.float32,
        )
        normed = after(normed, residual)
        gate = jnp.dot(normed, gate_up[0], preferred_element_type=jnp.float32)
        up = jnp.dot(normed, gate_up[1], preferred_element_type=jnp.float32)
        hidden = (jax.nn.silu(gate) * up).astype(jnp.bfloat16)
        hidden = hidden.reshape(2, n_sec // 2, 2, own_rows, half)

        def fold(proj_rows, down_rows):
            return lax.dot_general(
                proj_rows, down_rows, (((0,), (0,)), ((), ())), preferred_element_type=jnp.float32
            )

        if ordered:
            late = [d.pop((1, 1)), d.pop((1, 3))]
            folded = fold(proj, after(place_rows(d)[0], hidden))
            for k, block in zip((1, 3), late):
                at = row_of(1, k, block.shape[1])
                folded = folded + fold(
                    lax.dynamic_slice_in_dim(proj, at, block.shape[1], 0), block[0]
                )
        else:
            folded = fold(proj, down_all)
        folded = folded.astype(jnp.bfloat16)

        def project(x):
            return lax.dot_general(
                x, folded, (((x.ndim - 1,), (1,)), ((), ())), preferred_element_type=jnp.float32
            )

        send = project(lax.dynamic_index_in_dim(hidden, 1 - core, 2, False)).astype(jnp.bfloat16)
        got = flip(send, section=1)
        kept = after(project(lax.dynamic_index_in_dim(hidden, core, 2, False)), send)
        kept = kept + got.astype(jnp.float32)
        here = lax.dynamic_index_in_dim(kept, side, 1, False)
        there = lax.dynamic_index_in_dim(kept, 1 - side, 1, False).astype(jnp.bfloat16)
        from_x = flip(there[0], section=2)
        from_z = flip(here[1].astype(jnp.bfloat16), dp=1)
        from_xz = flip(there[1], section=2, dp=1)
        emb = (
            residual
            + here[0]
            + from_x.astype(jnp.float32)
            + from_z.astype(jnp.float32)
            + from_xz.astype(jnp.float32)
        )
        slide_normed = layer_norm(emb, slide_gain).astype(jnp.bfloat16)

        vmem = pl.BlockSpec(memory_space=pltpu.VMEM)
        if n_seq == 2:
            keys = [
                slide_normed,
                flip(slide_normed, section=2),
                flip(slide_normed, seq=1),
                flip(slide_normed, section=2, seq=1),
            ]
            others = [flip(block, section=1) for block in keys]
            keys = keys[:2] + others[:2] + keys[2:] + others[2:]
        else:
            keys = lax.all_gather(slide_normed, ("seq", "section"), axis=0, tiled=True)

        width = w_qkv.shape[2]
        qkv = jnp.swapaxes(w_qkv, 1, 2)
        if n_seq == 2:
            keep, send = pl.pallas_call(
                lambda *refs: attend_kernel(*refs, heads=local_heads, masks=masks),
                out_shape=[
                    jax.ShapeDtypeStruct((2, width, tokens), jnp.float32),
                    jax.ShapeDtypeStruct((2, width, tokens), jnp.bfloat16),
                ],
                in_specs=[vmem] * 12,
                out_specs=[vmem] * 2,
                compiler_params=pltpu.CompilerParams(vmem_limit_bytes=16 * 2**20),
                cost_estimate=pl.CostEstimate(
                    flops=2 * count * width * (3 * 768 + 2 * local_heads * tokens),
                    bytes_accessed=8 * 2**20,
                    transcendentals=local_heads * tokens * count,
                ),
            )(*keys, qkv, out_w, emb, code)
        else:

            def by_head(x, matrix):
                x = jnp.dot(x, matrix.T, preferred_element_type=jnp.float32)
                x = x.astype(jnp.bfloat16).reshape(x.shape[0], local_heads, width // local_heads)
                return x.transpose(1, 0, 2)

            def one_head(args):
                q, k, v, q_row, k_row = args
                scores = jnp.dot(q, k.T, preferred_element_type=jnp.float32)
                scores = scores / math.sqrt(width // local_heads)
                ok = (q_row[:, None] == k_row[None, :]) | (q_idx[:, None] == k_idx[None, :])
                weight = jax.nn.softmax(jnp.where(ok, scores, NEG), axis=-1)
                return jnp.dot(weight, v, preferred_element_type=jnp.float32)

            queries = lax.dynamic_slice_in_dim(keys, seq_at * tokens, tokens, 0)
            att = lax.map(
                one_head,
                (by_head(queries, qkv[0]), by_head(keys, qkv[1]), by_head(keys, qkv[2]))
                + (codes(q_idx)[0], k_code),
            )
            att = att.transpose(1, 0, 2).reshape(tokens, width).astype(jnp.bfloat16)
            parts = jnp.dot(att, w_out, preferred_element_type=jnp.float32)
            old = lax.dynamic_slice_in_dim(parts, sec * own_rows, own_rows, 0)
            parts = lax.dynamic_update_slice_in_dim(parts, old + emb, sec * own_rows, 0)
            parts = jnp.stack(absolute(jnp.split(parts.T, n_sec, axis=0)))
            keep, send = parts[0::2], parts[1::2].astype(jnp.bfloat16)

        kept = keep + flip(send, section=1).astype(jnp.float32)
        out = kept[0] + flip(kept[1].astype(jnp.bfloat16), section=2).astype(jnp.float32)
        return out.astype(jnp.bfloat16).T[None]

    return per_device


def solution(mesh):
    placed = (
        P("dp", "seq", "section"),
        P(),
        P(("seq", "dp"), "section"),
        P(("seq", "dp"), "section"),
        P("section", ("seq", "dp")),
        P("section", None),
        P(),
        P(None, None, "section"),
        P("section", None),
        P("dp", None),
        P("section"),
        P("section"),
    )
    shape = mesh.shape
    return jax.shard_map(
        build(shape["section"], shape["seq"], shape["dp"]),
        mesh=mesh,
        in_specs=placed,
        out_specs=P("dp", "seq", "section"),
        check_vma=False,
    )
```

```python
import math

import jax
import jax.numpy as jnp
from jax import lax
from jax.experimental import pallas as pl
from jax.experimental.pallas import tpu as pltpu
from jax.sharding import PartitionSpec as P

NEG = -1e30
AXES = ("section", "seq", "dp")


def layer_norm(rows, gain):
    mean = jnp.mean(rows, axis=-1, keepdims=True)
    centered = rows - mean
    var = jnp.mean(centered * centered, axis=-1, keepdims=True)
    return centered * lax.rsqrt(var + 1e-06) * gain


def slide_place(lengths_row, index):
    ends = jnp.cumsum(lengths_row, dtype=jnp.int32)
    after = index[:, None] >= ends[None, :]
    slide = jnp.sum(after.astype(jnp.int32), axis=1, dtype=jnp.int32)
    before = jnp.sum(jnp.where(after, lengths_row[None, :], 0), axis=1, dtype=jnp.int32)
    return (slide, index - before)


def attend_kernel(*refs, heads, masks):
    blocks, (w_ref, out_w_ref, emb_ref, code_ref, keep_ref, send_ref) = refs[:-6], refs[-6:]
    sec = lax.axis_index("section")
    core, side = sec % 2, sec // 2
    own = blocks[0].shape[0]
    keys = jnp.concatenate([block[...] for block in blocks], axis=0)
    count, rows = keys.shape[0], own * len(masks)
    q_code = jnp.transpose(code_ref[:, :rows])
    width = w_ref.shape[1]
    size = width // heads
    scale = math.log2(math.e) / math.sqrt(size)

    def project(x, which):
        return lax.dot_general(
            x, w_ref[which], (((1,), (1,)), ((), ())), preferred_element_type=jnp.float32
        ).astype(jnp.bfloat16)

    key, query, value = project(keys, 1), project(keys[:rows], 0), project(keys, 2)
    lane_head = lax.broadcasted_iota(jnp.int32, (rows, width), 1) // size
    diag = lax.broadcasted_iota(jnp.int32, (rows, count), 0) == lax.broadcasted_iota(
        jnp.int32, (rows, count), 1
    )
    att = jnp.zeros((rows, width), jnp.float32)
    for h in range(heads):
        scores = lax.dot_general(
            jnp.where(lane_head == h, query, jnp.zeros_like(query)),
            key,
            (((1,), (1,)), ((), ())),
            preferred_element_type=jnp.float32,
        )
        ok = (q_code[:, h : h + 1] == code_ref[heads + h : heads + h + 1, :]) | diag
        scores = jnp.where(ok, scores, NEG)
        top = jnp.max(scores, axis=1, keepdims=True)
        weight = jnp.exp2((scores - top) * scale)
        total = jnp.sum(weight, axis=1, keepdims=True)
        mixed = jnp.dot(weight.astype(jnp.bfloat16), value, preferred_element_type=jnp.float32)
        att = jnp.where(lane_head == h, mixed / total, att)
    part = jnp.dot(
        out_w_ref[...], jnp.transpose(att).astype(jnp.bfloat16), preferred_element_type=jnp.float32
    )
    emb = jnp.transpose(emb_ref[...])
    for block, mask in enumerate(masks):
        piece = part[:, block * own : (block + 1) * own]
        if block == 0:
            piece = piece + emb
        at = pl.ds(pl.multiple_of((mask ^ sec) * own, own), own)
        for j in range(part.shape[0] // width // 2):
            low = piece[2 * j * width : (2 * j + 1) * width]
            high = piece[(2 * j + 1) * width : (2 * j + 2) * width]
            keep_ref[j ^ side, :, at] = jnp.where(core == 0, low, high)
            send_ref[j ^ side, :, at] = jnp.where(core == 0, high, low).astype(send_ref.dtype)


def build(n_sec, n_seq, n_dp):
    sizes = {"section": n_sec, "seq": n_seq, "dp": n_dp}

    def flip(x, **masks):
        names = tuple(a for a in AXES if masks.get(a))
        pairs = []
        total = math.prod(sizes[a] for a in names)
        for source in range(total):
            rest, coords = source, []
            for a in reversed(names):
                coords.append(rest % sizes[a])
                rest //= sizes[a]
            target = 0
            for a, c in zip(names, reversed(coords)):
                target = target * sizes[a] + (c ^ masks[a])
            pairs.append((source, target))
        return lax.ppermute(x, names if len(names) > 1 else names[0], pairs)

    def rotate(x, k):
        return lax.ppermute(x, "dp", [(i, (i + k) % n_dp) for i in range(n_dp)])

    def after(x, *others):
        return lax.optimization_barrier((x,) + others)[0]

    def absolute(blocks):
        stacked, sec = jnp.stack(blocks), lax.axis_index("section")
        return [lax.dynamic_index_in_dim(stacked, sec ^ j, 0, False) for j in range(n_sec)]

    def gather_section(x):
        across = flip(x, section=2)
        return [x, flip(after(x, across), section=1), across, flip(across, section=1)]

    def gather_rows(same, other, seq_at, dp_at):
        mats, rows, units = same.shape
        part = jnp.zeros((mats, n_dp * rows, units), same.dtype)
        for k in range(n_dp):
            block = rotate(other if k % 2 else same, k) if k else same
            part = lax.dynamic_update_slice(part, block, (0, ((dp_at - k) % n_dp) * rows, 0))
        whole = lax.all_gather(part, "seq", axis=1, tiled=True)
        return jnp.concatenate(absolute(jnp.split(whole, n_sec, axis=1)), axis=1)

    def row_of(y, k, rows):
        sec, seq_at, dp_at = (lax.axis_index(a) for a in AXES)
        block = (seq_at ^ y) * n_dp + (dp_at - k) % n_dp
        each = n_seq * n_dp // n_sec
        return ((block // each ^ sec) * each + block % each) * rows

    def place_rows(blocks):
        first = blocks[0, 2]
        mats, rows, units = first.shape
        whole = after(jnp.zeros((mats, n_seq * n_dp * rows, units), first.dtype), first)
        for (y, k), block in blocks.items():
            whole = lax.dynamic_update_slice(whole, block, (0, row_of(y, k, rows), 0))
        return whole

    def per_device(
        tile_feats,
        tile_gain,
        w_gate,
        w_up,
        w_down,
        w_proj,
        slide_gain,
        w_qkv,
        w_out,
        lengths,
        seg_len,
        rate,
    ):
        sec = lax.axis_index("section")
        seq_at = lax.axis_index("seq")
        dp_at = lax.axis_index("dp")
        core, side, odd = sec % 2, sec // 2, dp_at % 2
        mine = tile_feats[0]
        tokens, feats = mine.shape
        own_rows = tokens // n_sec
        half = w_gate.shape[1] // 2

        def halves(x, which):
            return lax.dynamic_slice_in_dim(x, which * half, half, x.ndim - 1)

        pair = jnp.stack([w_gate, w_up])
        pair_same, pair_other = halves(pair, odd), halves(pair, 1 - odd)
        down = w_down.T[None]
        down_same, down_other = halves(down, odd), halves(down, 1 - odd)
        ordered = n_seq == 2 and n_dp == 4

        if n_seq == 2:
            masks = (0, 2, 1, 3)
            span = jnp.arange(own_rows, dtype=jnp.int32)
            k_idx = jnp.concatenate(
                [(seq_at ^ y) * tokens + (sec ^ m) * own_rows + span for y in (0, 1) for m in masks]
            )
            q_idx = k_idx[:tokens]
        else:
            k_idx = jnp.arange(n_seq * tokens, dtype=jnp.int32)
            q_idx = seq_at * tokens + jnp.arange(tokens, dtype=jnp.int32)
        count = k_idx.shape[0]
        local_heads = seg_len.shape[0]
        heads = sec * local_heads + jnp.arange(local_heads, dtype=jnp.int32)

        def codes(index):
            slide, pos = slide_place(lengths[0], index)
            block = slide[None, :] * count + pos[None, :] // seg_len[:, None]
            return block, pos[None, :] % rate[:, None] == (heads % rate)[:, None]

        k_block, picked = codes(k_idx)
        k_code = jnp.where(picked, k_block, -1)
        code = jnp.concatenate([k_block, k_code], axis=0)

        own_at = sec * own_rows
        gain = jnp.concatenate(absolute(jnp.split(tile_gain, n_sec)))
        out_w = w_out.T

        if ordered:
            g, d = {(0, 0): pair_same}, {(0, 0): down_same}
            beside = flip(mine, dp=1)
            mine_x = flip(mine, section=2)
            g[0, 2] = rotate(pair_same, 2)
            g[1, 0] = flip(pair_same, seq=1)
            d[1, 0] = flip(down_same, seq=1)
            beside_x = flip(beside, section=2)
            proj_x = flip(after(w_proj, mine_x), section=2)
            for k in (1, 3):
                g[0, k] = rotate(after(pair_other, g[0, 2], d[1, 0], g[1, 0], mine_x), k)
            g[1, 2] = flip(g[0, 2], seq=1)
            across = after(jnp.concatenate([mine_x, beside_x], axis=0), g[0, 2], g[1, 2])
            both = after(jnp.concatenate([mine, beside], axis=0), across)
            both_c, across_c = flip(both, section=1), flip(across, section=1)
            far = rotate(after(down_same, g[0, 1]), 2)
            rows = jnp.concatenate([both, both_c, across, across_c], axis=1)
            normed = layer_norm(rows.astype(jnp.float32), gain).astype(jnp.bfloat16)
            g[1, 1] = after(flip(after(g[0, 1], both_c), seq=1), normed)
            d[0, 2] = after(far, normed)
            for k in (1, 3):
                d[0, k] = rotate(after(down_other, d[0, 2], code, out_w), k)
            g[1, 3] = after(flip(g[0, 3], seq=1), d[0, 1], d[0, 3])
            gate_up = place_rows(g)
            proj_c = flip(after(w_proj, proj_x, d[0, 1]), section=1)
            proj_xc = flip(after(proj_x, d[0, 1]), section=1)
            proj = jnp.concatenate([w_proj, proj_c, proj_x, proj_xc], axis=0)
            for k in (2, 1, 3):
                d[1, k] = flip(d[0, k], seq=1)
        else:
            gate_up = gather_rows(pair_same, pair_other, seq_at, dp_at)
            down_all = gather_rows(down_same, down_other, seq_at, dp_at)[0]
            both = jnp.concatenate([mine, flip(mine, dp=1)], axis=0)
            rows = jnp.concatenate(gather_section(both), axis=1)
            normed = layer_norm(rows.astype(jnp.float32), gain).astype(jnp.bfloat16)
            proj = jnp.concatenate(gather_section(w_proj), axis=0)

        residual = jnp.dot(
            lax.dynamic_slice_in_dim(rows[:tokens], own_at, own_rows, 0),
            proj,
            preferred_element_type=jnp.float32,
        )
        normed = after(normed, residual)
        gate = jnp.dot(normed, gate_up[0], preferred_element_type=jnp.float32)
        up = jnp.dot(normed, gate_up[1], preferred_element_type=jnp.float32)
        hidden = (jax.nn.silu(gate) * up).astype(jnp.bfloat16)
        hidden = hidden.reshape(2, n_sec // 2, 2, own_rows, half)

        def fold(proj_rows, down_rows):
            return lax.dot_general(
                proj_rows, down_rows, (((0,), (0,)), ((), ())), preferred_element_type=jnp.float32
            )

        if ordered:
            late = [d.pop((1, 1)), d.pop((1, 3))]
            folded = fold(proj, after(place_rows(d)[0], hidden))
            for k, block in zip((1, 3), late):
                at = row_of(1, k, block.shape[1])
                folded = folded + fold(
                    lax.dynamic_slice_in_dim(proj, at, block.shape[1], 0), block[0]
                )
        else:
            folded = fold(proj, down_all)
        folded = folded.astype(jnp.bfloat16)

        def project(x):
            return lax.dot_general(
                x, folded, (((x.ndim - 1,), (1,)), ((), ())), preferred_element_type=jnp.float32
            )

        send = project(lax.dynamic_index_in_dim(hidden, 1 - core, 2, False)).astype(jnp.bfloat16)
        got = flip(send, section=1)
        kept = after(project(lax.dynamic_index_in_dim(hidden, core, 2, False)), send)
        kept = kept + got.astype(jnp.float32)
        here = lax.dynamic_index_in_dim(kept, side, 1, False)
        there = lax.dynamic_index_in_dim(kept, 1 - side, 1, False).astype(jnp.bfloat16)
        from_x = flip(there[0], section=2)
        from_z = flip(here[1].astype(jnp.bfloat16), dp=1)
        from_xz = flip(there[1], section=2, dp=1)
        emb = (
            residual
            + here[0]
            + from_x.astype(jnp.float32)
            + from_z.astype(jnp.float32)
            + from_xz.astype(jnp.float32)
        )
        slide_normed = layer_norm(emb, slide_gain).astype(jnp.bfloat16)

        vmem = pl.BlockSpec(memory_space=pltpu.VMEM)
        if n_seq == 2:
            keys = [
                slide_normed,
                flip(slide_normed, section=2),
                flip(slide_normed, seq=1),
                flip(slide_normed, section=2, seq=1),
            ]
            others = [flip(block, section=1) for block in keys]
            keys = keys[:2] + others[:2] + keys[2:] + others[2:]
        else:
            keys = lax.all_gather(slide_normed, ("seq", "section"), axis=0, tiled=True)

        width = w_qkv.shape[2]
        qkv = jnp.swapaxes(w_qkv, 1, 2)
        if n_seq == 2:
            keep, send = pl.pallas_call(
                lambda *refs: attend_kernel(*refs, heads=local_heads, masks=masks),
                out_shape=[
                    jax.ShapeDtypeStruct((2, width, tokens), jnp.float32),
                    jax.ShapeDtypeStruct((2, width, tokens), jnp.bfloat16),
                ],
                in_specs=[vmem] * 12,
                out_specs=[vmem] * 2,
                compiler_params=pltpu.CompilerParams(vmem_limit_bytes=16 * 2**20),
                cost_estimate=pl.CostEstimate(
                    flops=2 * count * width * (3 * 768 + 2 * local_heads * tokens),
                    bytes_accessed=8 * 2**20,
                    transcendentals=local_heads * tokens * count,
                ),
            )(*keys, qkv, out_w, emb, code)
        else:

            def by_head(x, matrix):
                x = jnp.dot(x, matrix.T, preferred_element_type=jnp.float32)
                x = x.astype(jnp.bfloat16).reshape(x.shape[0], local_heads, width // local_heads)
                return x.transpose(1, 0, 2)

            def one_head(args):
                q, k, v, q_row, k_row = args
                scores = jnp.dot(q, k.T, preferred_element_type=jnp.float32)
                scores = scores / math.sqrt(width // local_heads)
                ok = (q_row[:, None] == k_row[None, :]) | (q_idx[:, None] == k_idx[None, :])
                weight = jax.nn.softmax(jnp.where(ok, scores, NEG), axis=-1)
                return jnp.dot(weight, v, preferred_element_type=jnp.float32)

            queries = lax.dynamic_slice_in_dim(keys, seq_at * tokens, tokens, 0)
            att = lax.map(
                one_head,
                (by_head(queries, qkv[0]), by_head(keys, qkv[1]), by_head(keys, qkv[2]))
                + (codes(q_idx)[0], k_code),
            )
            att = att.transpose(1, 0, 2).reshape(tokens, width).astype(jnp.bfloat16)
            parts = jnp.dot(att, w_out, preferred_element_type=jnp.float32)
            old = lax.dynamic_slice_in_dim(parts, sec * own_rows, own_rows, 0)
            parts = lax.dynamic_update_slice_in_dim(parts, old + emb, sec * own_rows, 0)
            parts = jnp.stack(absolute(jnp.split(parts.T, n_sec, axis=0)))
            keep, send = parts[0::2], parts[1::2].astype(jnp.bfloat16)

        kept = keep + flip(send, section=1).astype(jnp.float32)
        out = kept[0] + flip(kept[1].astype(jnp.bfloat16), section=2).astype(jnp.float32)
        return out.astype(jnp.bfloat16).T[None]

    return per_device


def solution(mesh):
    placed = (
        P("dp", "seq", "section"),
        P(),
        P(("seq", "dp"), "section"),
        P(("seq", "dp"), "section"),
        P("section", ("seq", "dp")),
        P("section", None),
        P(),
        P(None, None, "section"),
        P("section", None),
        P("dp", None),
        P("section"),
        P("section"),
    )
    shape = mesh.shape
    return jax.shard_map(
        build(shape["section"], shape["seq"], shape["dp"]),
        mesh=mesh,
        in_specs=placed,
        out_specs=P("dp", "seq", "section"),
        check_vma=False,
    )
```

```python
import math

import jax
import jax.numpy as jnp
from jax import lax
from jax.experimental import pallas as pl
from jax.experimental.pallas import tpu as pltpu
from jax.sharding import PartitionSpec as P

NEG = -1e30
AXES = ("section", "seq", "dp")


def layer_norm(rows, gain):
    mean = jnp.mean(rows, axis=-1, keepdims=True)
    centered = rows - mean
    var = jnp.mean(centered * centered, axis=-1, keepdims=True)
    return centered * lax.rsqrt(var + 1e-06) * gain


def slide_place(lengths_row, index):
    ends = jnp.cumsum(lengths_row, dtype=jnp.int32)
    after = index[:, None] >= ends[None, :]
    slide = jnp.sum(after.astype(jnp.int32), axis=1, dtype=jnp.int32)
    before = jnp.sum(jnp.where(after, lengths_row[None, :], 0), axis=1, dtype=jnp.int32)
    return (slide, index - before)


def attend_kernel(*refs, heads, masks):
    blocks, (w_ref, out_w_ref, emb_ref, code_ref, keep_ref, send_ref) = refs[:-6], refs[-6:]
    sec = lax.axis_index("section")
    core, side = sec % 2, sec // 2
    own = blocks[0].shape[0]
    keys = jnp.concatenate([block[...] for block in blocks], axis=0)
    count, rows = keys.shape[0], own * len(masks)
    q_code = jnp.transpose(code_ref[:, :rows])
    width = w_ref.shape[1]
    size = width // heads
    scale = math.log2(math.e) / math.sqrt(size)

    def project(x, which):
        return lax.dot_general(
            x, w_ref[which], (((1,), (1,)), ((), ())), preferred_element_type=jnp.float32
        ).astype(jnp.bfloat16)

    key, query, value = project(keys, 1), project(keys[:rows], 0), project(keys, 2)
    lane_head = lax.broadcasted_iota(jnp.int32, (rows, width), 1) // size
    diag = lax.broadcasted_iota(jnp.int32, (rows, count), 0) == lax.broadcasted_iota(
        jnp.int32, (rows, count), 1
    )
    att = jnp.zeros((rows, width), jnp.float32)
    for h in range(heads):
        scores = lax.dot_general(
            jnp.where(lane_head == h, query, jnp.zeros_like(query)),
            key,
            (((1,), (1,)), ((), ())),
            preferred_element_type=jnp.float32,
        )
        ok = (q_code[:, h : h + 1] == code_ref[heads + h : heads + h + 1, :]) | diag
        scores = jnp.where(ok, scores, NEG)
        top = jnp.max(scores, axis=1, keepdims=True)
        weight = jnp.exp2((scores - top) * scale)
        total = jnp.sum(weight, axis=1, keepdims=True)
        mixed = jnp.dot(weight.astype(jnp.bfloat16), value, preferred_element_type=jnp.float32)
        att = jnp.where(lane_head == h, mixed / total, att)
    part = jnp.dot(
        out_w_ref[...], jnp.transpose(att).astype(jnp.bfloat16), preferred_element_type=jnp.float32
    )
    emb = jnp.transpose(emb_ref[...])
    for block, mask in enumerate(masks):
        piece = part[:, block * own : (block + 1) * own]
        if block == 0:
            piece = piece + emb
        at = pl.ds(pl.multiple_of((mask ^ sec) * own, own), own)
        for j in range(part.shape[0] // width // 2):
            low = piece[2 * j * width : (2 * j + 1) * width]
            high = piece[(2 * j + 1) * width : (2 * j + 2) * width]
            keep_ref[j ^ side, :, at] = jnp.where(core == 0, low, high)
            send_ref[j ^ side, :, at] = jnp.where(core == 0, high, low).astype(send_ref.dtype)


def build(n_sec, n_seq, n_dp):
    sizes = {"section": n_sec, "seq": n_seq, "dp": n_dp}

    def flip(x, **masks):
        names = tuple(a for a in AXES if masks.get(a))
        pairs = []
        total = math.prod(sizes[a] for a in names)
        for source in range(total):
            rest, coords = source, []
            for a in reversed(names):
                coords.append(rest % sizes[a])
                rest //= sizes[a]
            target = 0
            for a, c in zip(names, reversed(coords)):
                target = target * sizes[a] + (c ^ masks[a])
            pairs.append((source, target))
        return lax.ppermute(x, names if len(names) > 1 else names[0], pairs)

    def rotate(x, k):
        return lax.ppermute(x, "dp", [(i, (i + k) % n_dp) for i in range(n_dp)])

    def after(x, *others):
        return lax.optimization_barrier((x,) + others)[0]

    def absolute(blocks):
        stacked, sec = jnp.stack(blocks), lax.axis_index("section")
        return [lax.dynamic_index_in_dim(stacked, sec ^ j, 0, False) for j in range(n_sec)]

    def gather_section(x):
        across = flip(x, section=2)
        return [x, flip(after(x, across), section=1), across, flip(across, section=1)]

    def gather_rows(same, other, seq_at, dp_at):
        mats, rows, units = same.shape
        part = jnp.zeros((mats, n_dp * rows, units), same.dtype)
        for k in range(n_dp):
            block = rotate(other if k % 2 else same, k) if k else same
            part = lax.dynamic_update_slice(part, block, (0, ((dp_at - k) % n_dp) * rows, 0))
        whole = lax.all_gather(part, "seq", axis=1, tiled=True)
        return jnp.concatenate(absolute(jnp.split(whole, n_sec, axis=1)), axis=1)

    def row_of(y, k, rows):
        sec, seq_at, dp_at = (lax.axis_index(a) for a in AXES)
        block = (seq_at ^ y) * n_dp + (dp_at - k) % n_dp
        each = n_seq * n_dp // n_sec
        return ((block // each ^ sec) * each + block % each) * rows

    def place_rows(blocks):
        first = blocks[0, 2]
        mats, rows, units = first.shape
        whole = after(jnp.zeros((mats, n_seq * n_dp * rows, units), first.dtype), first)
        for (y, k), block in blocks.items():
            whole = lax.dynamic_update_slice(whole, block, (0, row_of(y, k, rows), 0))
        return whole

    def per_device(
        tile_feats,
        tile_gain,
        w_gate,
        w_up,
        w_down,
        w_proj,
        slide_gain,
        w_qkv,
        w_out,
        lengths,
        seg_len,
        rate,
    ):
        sec = lax.axis_index("section")
        seq_at = lax.axis_index("seq")
        dp_at = lax.axis_index("dp")
        core, side, odd = sec % 2, sec // 2, dp_at % 2
        mine = tile_feats[0]
        tokens, feats = mine.shape
        own_rows = tokens // n_sec
        half = w_gate.shape[1] // 2

        def halves(x, which):
            return lax.dynamic_slice_in_dim(x, which * half, half, x.ndim - 1)

        pair = jnp.stack([w_gate, w_up])
        pair_same, pair_other = halves(pair, odd), halves(pair, 1 - odd)
        down = w_down.T[None]
        down_same, down_other = halves(down, odd), halves(down, 1 - odd)
        ordered = n_seq == 2 and n_dp == 4

        if n_seq == 2:
            masks = (0, 2, 1, 3)
            span = jnp.arange(own_rows, dtype=jnp.int32)
            k_idx = jnp.concatenate(
                [(seq_at ^ y) * tokens + (sec ^ m) * own_rows + span for y in (0, 1) for m in masks]
            )
            q_idx = k_idx[:tokens]
        else:
            k_idx = jnp.arange(n_seq * tokens, dtype=jnp.int32)
            q_idx = seq_at * tokens + jnp.arange(tokens, dtype=jnp.int32)
        count = k_idx.shape[0]
        local_heads = seg_len.shape[0]
        heads = sec * local_heads + jnp.arange(local_heads, dtype=jnp.int32)

        def codes(index):
            slide, pos = slide_place(lengths[0], index)
            block = slide[None, :] * count + pos[None, :] // seg_len[:, None]
            return block, pos[None, :] % rate[:, None] == (heads % rate)[:, None]

        k_block, picked = codes(k_idx)
        k_code = jnp.where(picked, k_block, -1)
        code = jnp.concatenate([k_block, k_code], axis=0)

        own_at = sec * own_rows
        gain = jnp.concatenate(absolute(jnp.split(tile_gain, n_sec)))
        out_w = w_out.T

        if ordered:
            g, d = {(0, 0): pair_same}, {(0, 0): down_same}
            beside = flip(mine, dp=1)
            mine_x = flip(mine, section=2)
            g[0, 2] = rotate(pair_same, 2)
            g[1, 0] = flip(pair_same, seq=1)
            d[1, 0] = flip(down_same, seq=1)
            beside_x = flip(beside, section=2)
            proj_x = flip(after(w_proj, mine_x), section=2)
            for k in (1, 3):
                g[0, k] = rotate(after(pair_other, g[0, 2], d[1, 0], g[1, 0], mine_x), k)
            g[1, 2] = flip(g[0, 2], seq=1)
            across = after(jnp.concatenate([mine_x, beside_x], axis=0), g[0, 2], g[1, 2])
            both = after(jnp.concatenate([mine, beside], axis=0), across)
            both_c, across_c = flip(both, section=1), flip(across, section=1)
            far = rotate(after(down_same, g[0, 1]), 2)
            rows = jnp.concatenate([both, both_c, across, across_c], axis=1)
            normed = layer_norm(rows.astype(jnp.float32), gain).astype(jnp.bfloat16)
            g[1, 1] = after(flip(g[0, 1], seq=1), normed)
            d[0, 2] = after(far, normed)
            for k in (1, 3):
                d[0, k] = rotate(after(down_other, d[0, 2], code, out_w), k)
            g[1, 3] = after(flip(g[0, 3], seq=1), d[0, 1], d[0, 3])
            gate_up = place_rows(g)
            proj_c = flip(after(w_proj, proj_x, d[0, 1]), section=1)
            proj_xc = flip(after(proj_x, d[0, 1]), section=1)
            proj = jnp.concatenate([w_proj, proj_c, proj_x, proj_xc], axis=0)
            for k in (2, 1, 3):
                d[1, k] = flip(d[0, k], seq=1)
        else:
            gate_up = gather_rows(pair_same, pair_other, seq_at, dp_at)
            down_all = gather_rows(down_same, down_other, seq_at, dp_at)[0]
            both = jnp.concatenate([mine, flip(mine, dp=1)], axis=0)
            rows = jnp.concatenate(gather_section(both), axis=1)
            normed = layer_norm(rows.astype(jnp.float32), gain).astype(jnp.bfloat16)
            proj = jnp.concatenate(gather_section(w_proj), axis=0)

        residual = jnp.dot(
            lax.dynamic_slice_in_dim(rows[:tokens], own_at, own_rows, 0),
            proj,
            preferred_element_type=jnp.float32,
        )
        normed = after(normed, residual)
        gate = jnp.dot(normed, gate_up[0], preferred_element_type=jnp.float32)
        up = jnp.dot(normed, gate_up[1], preferred_element_type=jnp.float32)
        hidden = (jax.nn.silu(gate) * up).astype(jnp.bfloat16)
        hidden = hidden.reshape(2, n_sec // 2, 2, own_rows, half)

        def fold(proj_rows, down_rows):
            return lax.dot_general(
                proj_rows, down_rows, (((0,), (0,)), ((), ())), preferred_element_type=jnp.float32
            )

        if ordered:
            late = [d.pop((1, 1)), d.pop((1, 3))]
            folded = fold(proj, after(place_rows(d)[0], hidden))
            for k, block in zip((1, 3), late):
                at = row_of(1, k, block.shape[1])
                folded = folded + fold(
                    lax.dynamic_slice_in_dim(proj, at, block.shape[1], 0), block[0]
                )
        else:
            folded = fold(proj, down_all)
        folded = folded.astype(jnp.bfloat16)

        def project(x):
            return lax.dot_general(
                x, folded, (((x.ndim - 1,), (1,)), ((), ())), preferred_element_type=jnp.float32
            )

        send = project(lax.dynamic_index_in_dim(hidden, 1 - core, 2, False)).astype(jnp.bfloat16)
        got = flip(send, section=1)
        kept = after(project(lax.dynamic_index_in_dim(hidden, core, 2, False)), send)
        kept = kept + got.astype(jnp.float32)
        here = lax.dynamic_index_in_dim(kept, side, 1, False)
        there = lax.dynamic_index_in_dim(kept, 1 - side, 1, False).astype(jnp.bfloat16)
        from_x = flip(there[0], section=2)
        from_z = flip(here[1].astype(jnp.bfloat16), dp=1)
        from_xz = flip(there[1], section=2, dp=1)
        emb = (
            residual
            + here[0]
            + from_x.astype(jnp.float32)
            + from_z.astype(jnp.float32)
            + from_xz.astype(jnp.float32)
        )
        slide_normed = layer_norm(emb, slide_gain).astype(jnp.bfloat16)

        vmem = pl.BlockSpec(memory_space=pltpu.VMEM)
        if n_seq == 2:
            keys = [
                slide_normed,
                flip(slide_normed, section=2),
                flip(slide_normed, seq=1),
                flip(slide_normed, section=2, seq=1),
            ]
            others = [flip(block, section=1) for block in keys]
            keys = keys[:2] + others[:2] + keys[2:] + others[2:]
        else:
            keys = lax.all_gather(slide_normed, ("seq", "section"), axis=0, tiled=True)

        width = w_qkv.shape[2]
        qkv = jnp.swapaxes(w_qkv, 1, 2)
        if n_seq == 2:
            keep, send = pl.pallas_call(
                lambda *refs: attend_kernel(*refs, heads=local_heads, masks=masks),
                out_shape=[
                    jax.ShapeDtypeStruct((2, width, tokens), jnp.float32),
                    jax.ShapeDtypeStruct((2, width, tokens), jnp.bfloat16),
                ],
                in_specs=[vmem] * 12,
                out_specs=[vmem] * 2,
                compiler_params=pltpu.CompilerParams(vmem_limit_bytes=16 * 2**20),
                cost_estimate=pl.CostEstimate(
                    flops=2 * count * width * (3 * 768 + 2 * local_heads * tokens),
                    bytes_accessed=8 * 2**20,
                    transcendentals=local_heads * tokens * count,
                ),
            )(*keys, qkv, out_w, emb, code)
        else:

            def by_head(x, matrix):
                x = jnp.dot(x, matrix.T, preferred_element_type=jnp.float32)
                x = x.astype(jnp.bfloat16).reshape(x.shape[0], local_heads, width // local_heads)
                return x.transpose(1, 0, 2)

            def one_head(args):
                q, k, v, q_row, k_row = args
                scores = jnp.dot(q, k.T, preferred_element_type=jnp.float32)
                scores = scores / math.sqrt(width // local_heads)
                ok = (q_row[:, None] == k_row[None, :]) | (q_idx[:, None] == k_idx[None, :])
                weight = jax.nn.softmax(jnp.where(ok, scores, NEG), axis=-1)
                return jnp.dot(weight, v, preferred_element_type=jnp.float32)

            queries = lax.dynamic_slice_in_dim(keys, seq_at * tokens, tokens, 0)
            att = lax.map(
                one_head,
                (by_head(queries, qkv[0]), by_head(keys, qkv[1]), by_head(keys, qkv[2]))
                + (codes(q_idx)[0], k_code),
            )
            att = att.transpose(1, 0, 2).reshape(tokens, width).astype(jnp.bfloat16)
            parts = jnp.dot(att, w_out, preferred_element_type=jnp.float32)
            old = lax.dynamic_slice_in_dim(parts, sec * own_rows, own_rows, 0)
            parts = lax.dynamic_update_slice_in_dim(parts, old + emb, sec * own_rows, 0)
            parts = jnp.stack(absolute(jnp.split(parts.T, n_sec, axis=0)))
            keep, send = parts[0::2], parts[1::2].astype(jnp.bfloat16)

        kept = keep + flip(send, section=1).astype(jnp.float32)
        out = kept[0] + flip(kept[1].astype(jnp.bfloat16), section=2).astype(jnp.float32)
        return out.astype(jnp.bfloat16).T[None]

    return per_device


def solution(mesh):
    placed = (
        P("dp", "seq", "section"),
        P(),
        P(("seq", "dp"), "section"),
        P(("seq", "dp"), "section"),
        P("section", ("seq", "dp")),
        P("section", None),
        P(),
        P(None, None, "section"),
        P("section", None),
        P("dp", None),
        P("section"),
        P("section"),
    )
    shape = mesh.shape
    return jax.shard_map(
        build(shape["section"], shape["seq"], shape["dp"]),
        mesh=mesh,
        in_specs=placed,
        out_specs=P("dp", "seq", "section"),
        check_vma=False,
    )
```

```python
import math

import jax
import jax.numpy as jnp
from jax import lax
from jax.experimental import pallas as pl
from jax.experimental.pallas import tpu as pltpu
from jax.sharding import PartitionSpec as P

NEG = -1e30
AXES = ("section", "seq", "dp")


def layer_norm(rows, gain):
    mean = jnp.mean(rows, axis=-1, keepdims=True)
    centered = rows - mean
    var = jnp.mean(centered * centered, axis=-1, keepdims=True)
    return centered * lax.rsqrt(var + 1e-06) * gain


def slide_place(lengths_row, index):
    ends = jnp.cumsum(lengths_row, dtype=jnp.int32)
    after = index[:, None] >= ends[None, :]
    slide = jnp.sum(after.astype(jnp.int32), axis=1, dtype=jnp.int32)
    before = jnp.sum(jnp.where(after, lengths_row[None, :], 0), axis=1, dtype=jnp.int32)
    return (slide, index - before)


def attend_kernel(*refs, heads, masks):
    blocks, (w_ref, out_w_ref, emb_ref, code_ref, keep_ref, send_ref) = refs[:-6], refs[-6:]
    sec = lax.axis_index("section")
    core, side = sec % 2, sec // 2
    own = blocks[0].shape[0]
    keys = jnp.concatenate([block[...] for block in blocks], axis=0)
    count, rows = keys.shape[0], own * len(masks)
    q_code = jnp.transpose(code_ref[:, :rows])
    width = w_ref.shape[1]
    size = width // heads
    scale = math.log2(math.e) / math.sqrt(size)

    def project(x, which):
        return lax.dot_general(
            x, w_ref[which], (((1,), (1,)), ((), ())), preferred_element_type=jnp.float32
        ).astype(jnp.bfloat16)

    key, query, value = project(keys, 1), project(keys[:rows], 0), project(keys, 2)
    lane_head = lax.broadcasted_iota(jnp.int32, (rows, width), 1) // size
    diag = lax.broadcasted_iota(jnp.int32, (rows, count), 0) == lax.broadcasted_iota(
        jnp.int32, (rows, count), 1
    )
    att = jnp.zeros((rows, width), jnp.float32)
    for h in range(heads):
        scores = lax.dot_general(
            jnp.where(lane_head == h, query, jnp.zeros_like(query)),
            key,
            (((1,), (1,)), ((), ())),
            preferred_element_type=jnp.float32,
        )
        ok = (q_code[:, h : h + 1] == code_ref[heads + h : heads + h + 1, :]) | diag
        scores = jnp.where(ok, scores, NEG)
        top = jnp.max(scores, axis=1, keepdims=True)
        weight = jnp.exp2((scores - top) * scale)
        total = jnp.sum(weight, axis=1, keepdims=True)
        mixed = jnp.dot(weight.astype(jnp.bfloat16), value, preferred_element_type=jnp.float32)
        att = jnp.where(lane_head == h, mixed / total, att)
    part = jnp.dot(
        out_w_ref[...], jnp.transpose(att).astype(jnp.bfloat16), preferred_element_type=jnp.float32
    )
    emb = jnp.transpose(emb_ref[...])
    for block, mask in enumerate(masks):
        piece = part[:, block * own : (block + 1) * own]
        if block == 0:
            piece = piece + emb
        at = pl.ds(pl.multiple_of((mask ^ sec) * own, own), own)
        for j in range(part.shape[0] // width // 2):
            low = piece[2 * j * width : (2 * j + 1) * width]
            high = piece[(2 * j + 1) * width : (2 * j + 2) * width]
            keep_ref[j ^ side, :, at] = jnp.where(core == 0, low, high)
            send_ref[j ^ side, :, at] = jnp.where(core == 0, high, low).astype(send_ref.dtype)


def build(n_sec, n_seq, n_dp):
    sizes = {"section": n_sec, "seq": n_seq, "dp": n_dp}

    def flip(x, **masks):
        names = tuple(a for a in AXES if masks.get(a))
        pairs = []
        total = math.prod(sizes[a] for a in names)
        for source in range(total):
            rest, coords = source, []
            for a in reversed(names):
                coords.append(rest % sizes[a])
                rest //= sizes[a]
            target = 0
            for a, c in zip(names, reversed(coords)):
                target = target * sizes[a] + (c ^ masks[a])
            pairs.append((source, target))
        return lax.ppermute(x, names if len(names) > 1 else names[0], pairs)

    def rotate(x, k):
        return lax.ppermute(x, "dp", [(i, (i + k) % n_dp) for i in range(n_dp)])

    def after(x, *others):
        return lax.optimization_barrier((x,) + others)[0]

    def absolute(blocks):
        stacked, sec = jnp.stack(blocks), lax.axis_index("section")
        return [lax.dynamic_index_in_dim(stacked, sec ^ j, 0, False) for j in range(n_sec)]

    def gather_section(x):
        across = flip(x, section=2)
        return [x, flip(after(x, across), section=1), across, flip(across, section=1)]

    def gather_rows(same, other, seq_at, dp_at):
        mats, rows, units = same.shape
        part = jnp.zeros((mats, n_dp * rows, units), same.dtype)
        for k in range(n_dp):
            block = rotate(other if k % 2 else same, k) if k else same
            part = lax.dynamic_update_slice(part, block, (0, ((dp_at - k) % n_dp) * rows, 0))
        whole = lax.all_gather(part, "seq", axis=1, tiled=True)
        return jnp.concatenate(absolute(jnp.split(whole, n_sec, axis=1)), axis=1)

    def row_of(y, k, rows):
        sec, seq_at, dp_at = (lax.axis_index(a) for a in AXES)
        block = (seq_at ^ y) * n_dp + (dp_at - k) % n_dp
        each = n_seq * n_dp // n_sec
        return ((block // each ^ sec) * each + block % each) * rows

    def place_rows(blocks):
        first = blocks[0, 2]
        mats, rows, units = first.shape
        whole = after(jnp.zeros((mats, n_seq * n_dp * rows, units), first.dtype), first)
        for (y, k), block in blocks.items():
            whole = lax.dynamic_update_slice(whole, block, (0, row_of(y, k, rows), 0))
        return whole

    def per_device(
        tile_feats,
        tile_gain,
        w_gate,
        w_up,
        w_down,
        w_proj,
        slide_gain,
        w_qkv,
        w_out,
        lengths,
        seg_len,
        rate,
    ):
        sec = lax.axis_index("section")
        seq_at = lax.axis_index("seq")
        dp_at = lax.axis_index("dp")
        core, side, odd = sec % 2, sec // 2, dp_at % 2
        mine = tile_feats[0]
        tokens, feats = mine.shape
        own_rows = tokens // n_sec
        half = w_gate.shape[1] // 2

        def halves(x, which):
            return lax.dynamic_slice_in_dim(x, which * half, half, x.ndim - 1)

        pair = jnp.stack([w_gate, w_up])
        pair_same, pair_other = halves(pair, odd), halves(pair, 1 - odd)
        down = w_down.T[None]
        down_same, down_other = halves(down, odd), halves(down, 1 - odd)
        ordered = n_seq == 2 and n_dp == 4

        if n_seq == 2:
            masks = (0, 2, 1, 3)
            span = jnp.arange(own_rows, dtype=jnp.int32)
            k_idx = jnp.concatenate(
                [(seq_at ^ y) * tokens + (sec ^ m) * own_rows + span for y in (0, 1) for m in masks]
            )
            q_idx = k_idx[:tokens]
        else:
            k_idx = jnp.arange(n_seq * tokens, dtype=jnp.int32)
            q_idx = seq_at * tokens + jnp.arange(tokens, dtype=jnp.int32)
        count = k_idx.shape[0]
        local_heads = seg_len.shape[0]
        heads = sec * local_heads + jnp.arange(local_heads, dtype=jnp.int32)

        def codes(index):
            slide, pos = slide_place(lengths[0], index)
            block = slide[None, :] * count + pos[None, :] // seg_len[:, None]
            return block, pos[None, :] % rate[:, None] == (heads % rate)[:, None]

        k_block, picked = codes(k_idx)
        k_code = jnp.where(picked, k_block, -1)
        code = jnp.concatenate([k_block, k_code], axis=0)

        own_at = sec * own_rows
        gain = jnp.concatenate(absolute(jnp.split(tile_gain, n_sec)))
        out_w = w_out.T

        if ordered:
            g, d = {(0, 0): pair_same}, {(0, 0): down_same}
            beside = flip(mine, dp=1)
            mine_x = flip(mine, section=2)
            g[0, 2] = rotate(pair_same, 2)
            g[1, 0] = flip(pair_same, seq=1)
            d[1, 0] = flip(down_same, seq=1)
            beside_x = flip(beside, section=2)
            proj_x = flip(after(w_proj, mine_x), section=2)
            for k in (1, 3):
                g[0, k] = rotate(after(pair_other, g[0, 2], d[1, 0], g[1, 0], mine_x), k)
            g[1, 2] = flip(g[0, 2], seq=1)
            across = after(jnp.concatenate([mine_x, beside_x], axis=0), g[0, 2], g[1, 2])
            both = after(jnp.concatenate([mine, beside], axis=0), across)
            both_c, across_c = flip(both, section=1), flip(across, section=1)
            far = rotate(after(down_same, g[0, 1], both_c), 2)
            rows = jnp.concatenate([both, both_c, across, across_c], axis=1)
            normed = layer_norm(rows.astype(jnp.float32), gain).astype(jnp.bfloat16)
            g[1, 1] = after(flip(g[0, 1], seq=1), normed)
            d[0, 2] = after(far, normed)
            for k in (1, 3):
                d[0, k] = rotate(after(down_other, d[0, 2], code, out_w), k)
            g[1, 3] = after(flip(g[0, 3], seq=1), d[0, 1], d[0, 3])
            gate_up = place_rows(g)
            proj_c = flip(after(w_proj, proj_x, d[0, 1]), section=1)
            proj_xc = flip(after(proj_x, d[0, 1]), section=1)
            proj = jnp.concatenate([w_proj, proj_c, proj_x, proj_xc], axis=0)
            for k in (2, 1, 3):
                d[1, k] = flip(d[0, k], seq=1)
        else:
            gate_up = gather_rows(pair_same, pair_other, seq_at, dp_at)
            down_all = gather_rows(down_same, down_other, seq_at, dp_at)[0]
            both = jnp.concatenate([mine, flip(mine, dp=1)], axis=0)
            rows = jnp.concatenate(gather_section(both), axis=1)
            normed = layer_norm(rows.astype(jnp.float32), gain).astype(jnp.bfloat16)
            proj = jnp.concatenate(gather_section(w_proj), axis=0)

        residual = jnp.dot(
            lax.dynamic_slice_in_dim(rows[:tokens], own_at, own_rows, 0),
            proj,
            preferred_element_type=jnp.float32,
        )
        normed = after(normed, residual)
        gate = jnp.dot(normed, gate_up[0], preferred_element_type=jnp.float32)
        up = jnp.dot(normed, gate_up[1], preferred_element_type=jnp.float32)
        hidden = (jax.nn.silu(gate) * up).astype(jnp.bfloat16)
        hidden = hidden.reshape(2, n_sec // 2, 2, own_rows, half)

        def fold(proj_rows, down_rows):
            return lax.dot_general(
                proj_rows, down_rows, (((0,), (0,)), ((), ())), preferred_element_type=jnp.float32
            )

        if ordered:
            late = [d.pop((1, 1)), d.pop((1, 3))]
            folded = fold(proj, after(place_rows(d)[0], hidden))
            for k, block in zip((1, 3), late):
                at = row_of(1, k, block.shape[1])
                folded = folded + fold(
                    lax.dynamic_slice_in_dim(proj, at, block.shape[1], 0), block[0]
                )
        else:
            folded = fold(proj, down_all)
        folded = folded.astype(jnp.bfloat16)

        def project(x):
            return lax.dot_general(
                x, folded, (((x.ndim - 1,), (1,)), ((), ())), preferred_element_type=jnp.float32
            )

        send = project(lax.dynamic_index_in_dim(hidden, 1 - core, 2, False)).astype(jnp.bfloat16)
        got = flip(send, section=1)
        kept = after(project(lax.dynamic_index_in_dim(hidden, core, 2, False)), send)
        kept = kept + got.astype(jnp.float32)
        here = lax.dynamic_index_in_dim(kept, side, 1, False)
        there = lax.dynamic_index_in_dim(kept, 1 - side, 1, False).astype(jnp.bfloat16)
        from_x = flip(there[0], section=2)
        from_z = flip(here[1].astype(jnp.bfloat16), dp=1)
        from_xz = flip(there[1], section=2, dp=1)
        emb = (
            residual
            + here[0]
            + from_x.astype(jnp.float32)
            + from_z.astype(jnp.float32)
            + from_xz.astype(jnp.float32)
        )
        slide_normed = layer_norm(emb, slide_gain).astype(jnp.bfloat16)

        vmem = pl.BlockSpec(memory_space=pltpu.VMEM)
        if n_seq == 2:
            keys = [
                slide_normed,
                flip(slide_normed, section=2),
                flip(slide_normed, seq=1),
                flip(slide_normed, section=2, seq=1),
            ]
            others = [flip(block, section=1) for block in keys]
            keys = keys[:2] + others[:2] + keys[2:] + others[2:]
        else:
            keys = lax.all_gather(slide_normed, ("seq", "section"), axis=0, tiled=True)

        width = w_qkv.shape[2]
        qkv = jnp.swapaxes(w_qkv, 1, 2)
        if n_seq == 2:
            keep, send = pl.pallas_call(
                lambda *refs: attend_kernel(*refs, heads=local_heads, masks=masks),
                out_shape=[
                    jax.ShapeDtypeStruct((2, width, tokens), jnp.float32),
                    jax.ShapeDtypeStruct((2, width, tokens), jnp.bfloat16),
                ],
                in_specs=[vmem] * 12,
                out_specs=[vmem] * 2,
                compiler_params=pltpu.CompilerParams(vmem_limit_bytes=16 * 2**20),
                cost_estimate=pl.CostEstimate(
                    flops=2 * count * width * (3 * 768 + 2 * local_heads * tokens),
                    bytes_accessed=8 * 2**20,
                    transcendentals=local_heads * tokens * count,
                ),
            )(*keys, qkv, out_w, emb, code)
        else:

            def by_head(x, matrix):
                x = jnp.dot(x, matrix.T, preferred_element_type=jnp.float32)
                x = x.astype(jnp.bfloat16).reshape(x.shape[0], local_heads, width // local_heads)
                return x.transpose(1, 0, 2)

            def one_head(args):
                q, k, v, q_row, k_row = args
                scores = jnp.dot(q, k.T, preferred_element_type=jnp.float32)
                scores = scores / math.sqrt(width // local_heads)
                ok = (q_row[:, None] == k_row[None, :]) | (q_idx[:, None] == k_idx[None, :])
                weight = jax.nn.softmax(jnp.where(ok, scores, NEG), axis=-1)
                return jnp.dot(weight, v, preferred_element_type=jnp.float32)

            queries = lax.dynamic_slice_in_dim(keys, seq_at * tokens, tokens, 0)
            att = lax.map(
                one_head,
                (by_head(queries, qkv[0]), by_head(keys, qkv[1]), by_head(keys, qkv[2]))
                + (codes(q_idx)[0], k_code),
            )
            att = att.transpose(1, 0, 2).reshape(tokens, width).astype(jnp.bfloat16)
            parts = jnp.dot(att, w_out, preferred_element_type=jnp.float32)
            old = lax.dynamic_slice_in_dim(parts, sec * own_rows, own_rows, 0)
            parts = lax.dynamic_update_slice_in_dim(parts, old + emb, sec * own_rows, 0)
            parts = jnp.stack(absolute(jnp.split(parts.T, n_sec, axis=0)))
            keep, send = parts[0::2], parts[1::2].astype(jnp.bfloat16)

        kept = keep + flip(send, section=1).astype(jnp.float32)
        out = kept[0] + flip(kept[1].astype(jnp.bfloat16), section=2).astype(jnp.float32)
        return out.astype(jnp.bfloat16).T[None]

    return per_device


def solution(mesh):
    placed = (
        P("dp", "seq", "section"),
        P(),
        P(("seq", "dp"), "section"),
        P(("seq", "dp"), "section"),
        P("section", ("seq", "dp")),
        P("section", None),
        P(),
        P(None, None, "section"),
        P("section", None),
        P("dp", None),
        P("section"),
        P("section"),
    )
    shape = mesh.shape
    return jax.shard_map(
        build(shape["section"], shape["seq"], shape["dp"]),
        mesh=mesh,
        in_specs=placed,
        out_specs=P("dp", "seq", "section"),
        check_vma=False,
    )
```

```python
import math

import jax
import jax.numpy as jnp
from jax import lax
from jax.experimental import pallas as pl
from jax.experimental.pallas import tpu as pltpu
from jax.sharding import PartitionSpec as P

NEG = -1e30
AXES = ("section", "seq", "dp")


def layer_norm(rows, gain):
    mean = jnp.mean(rows, axis=-1, keepdims=True)
    centered = rows - mean
    var = jnp.mean(centered * centered, axis=-1, keepdims=True)
    return centered * lax.rsqrt(var + 1e-06) * gain


def slide_place(lengths_row, index):
    ends = jnp.cumsum(lengths_row, dtype=jnp.int32)
    after = index[:, None] >= ends[None, :]
    slide = jnp.sum(after.astype(jnp.int32), axis=1, dtype=jnp.int32)
    before = jnp.sum(jnp.where(after, lengths_row[None, :], 0), axis=1, dtype=jnp.int32)
    return (slide, index - before)


def attend_kernel(*refs, heads, masks):
    blocks, (w_ref, out_w_ref, emb_ref, code_ref, keep_ref, send_ref) = refs[:-6], refs[-6:]
    sec = lax.axis_index("section")
    core, side = sec % 2, sec // 2
    own = blocks[0].shape[0]
    keys = jnp.concatenate([block[...] for block in blocks], axis=0)
    count, rows = keys.shape[0], own * len(masks)
    q_code = jnp.transpose(code_ref[:, :rows])
    width = w_ref.shape[1]
    size = width // heads
    scale = math.log2(math.e) / math.sqrt(size)

    def project(x, which):
        return lax.dot_general(
            x, w_ref[which], (((1,), (1,)), ((), ())), preferred_element_type=jnp.float32
        ).astype(jnp.bfloat16)

    key, query, value = project(keys, 1), project(keys[:rows], 0), project(keys, 2)
    lane_head = lax.broadcasted_iota(jnp.int32, (rows, width), 1) // size
    diag = lax.broadcasted_iota(jnp.int32, (rows, count), 0) == lax.broadcasted_iota(
        jnp.int32, (rows, count), 1
    )
    att = jnp.zeros((rows, width), jnp.float32)
    for h in range(heads):
        scores = lax.dot_general(
            jnp.where(lane_head == h, query, jnp.zeros_like(query)),
            key,
            (((1,), (1,)), ((), ())),
            preferred_element_type=jnp.float32,
        )
        ok = (q_code[:, h : h + 1] == code_ref[heads + h : heads + h + 1, :]) | diag
        scores = jnp.where(ok, scores, NEG)
        top = jnp.max(scores, axis=1, keepdims=True)
        weight = jnp.exp2((scores - top) * scale)
        total = jnp.sum(weight, axis=1, keepdims=True)
        mixed = jnp.dot(weight.astype(jnp.bfloat16), value, preferred_element_type=jnp.float32)
        att = jnp.where(lane_head == h, mixed / total, att)
    part = jnp.dot(
        out_w_ref[...], jnp.transpose(att).astype(jnp.bfloat16), preferred_element_type=jnp.float32
    )
    emb = jnp.transpose(emb_ref[...])
    for block, mask in enumerate(masks):
        piece = part[:, block * own : (block + 1) * own]
        if block == 0:
            piece = piece + emb
        at = pl.ds(pl.multiple_of((mask ^ sec) * own, own), own)
        for j in range(part.shape[0] // width // 2):
            low = piece[2 * j * width : (2 * j + 1) * width]
            high = piece[(2 * j + 1) * width : (2 * j + 2) * width]
            keep_ref[j ^ side, :, at] = jnp.where(core == 0, low, high)
            send_ref[j ^ side, :, at] = jnp.where(core == 0, high, low).astype(send_ref.dtype)


def build(n_sec, n_seq, n_dp):
    sizes = {"section": n_sec, "seq": n_seq, "dp": n_dp}

    def flip(x, **masks):
        names = tuple(a for a in AXES if masks.get(a))
        pairs = []
        total = math.prod(sizes[a] for a in names)
        for source in range(total):
            rest, coords = source, []
            for a in reversed(names):
                coords.append(rest % sizes[a])
                rest //= sizes[a]
            target = 0
            for a, c in zip(names, reversed(coords)):
                target = target * sizes[a] + (c ^ masks[a])
            pairs.append((source, target))
        return lax.ppermute(x, names if len(names) > 1 else names[0], pairs)

    def rotate(x, k):
        return lax.ppermute(x, "dp", [(i, (i + k) % n_dp) for i in range(n_dp)])

    def after(x, *others):
        return lax.optimization_barrier((x,) + others)[0]

    def absolute(blocks):
        stacked, sec = jnp.stack(blocks), lax.axis_index("section")
        return [lax.dynamic_index_in_dim(stacked, sec ^ j, 0, False) for j in range(n_sec)]

    def gather_section(x):
        across = flip(x, section=2)
        return [x, flip(after(x, across), section=1), across, flip(across, section=1)]

    def gather_rows(same, other, seq_at, dp_at):
        mats, rows, units = same.shape
        part = jnp.zeros((mats, n_dp * rows, units), same.dtype)
        for k in range(n_dp):
            block = rotate(other if k % 2 else same, k) if k else same
            part = lax.dynamic_update_slice(part, block, (0, ((dp_at - k) % n_dp) * rows, 0))
        whole = lax.all_gather(part, "seq", axis=1, tiled=True)
        return jnp.concatenate(absolute(jnp.split(whole, n_sec, axis=1)), axis=1)

    def row_of(y, k, rows):
        sec, seq_at, dp_at = (lax.axis_index(a) for a in AXES)
        block = (seq_at ^ y) * n_dp + (dp_at - k) % n_dp
        each = n_seq * n_dp // n_sec
        return ((block // each ^ sec) * each + block % each) * rows

    def place_rows(blocks):
        first = blocks[0, 2]
        mats, rows, units = first.shape
        whole = after(jnp.zeros((mats, n_seq * n_dp * rows, units), first.dtype), first)
        for (y, k), block in blocks.items():
            whole = lax.dynamic_update_slice(whole, block, (0, row_of(y, k, rows), 0))
        return whole

    def per_device(
        tile_feats,
        tile_gain,
        w_gate,
        w_up,
        w_down,
        w_proj,
        slide_gain,
        w_qkv,
        w_out,
        lengths,
        seg_len,
        rate,
    ):
        sec = lax.axis_index("section")
        seq_at = lax.axis_index("seq")
        dp_at = lax.axis_index("dp")
        core, side, odd = sec % 2, sec // 2, dp_at % 2
        mine = tile_feats[0]
        tokens, feats = mine.shape
        own_rows = tokens // n_sec
        half = w_gate.shape[1] // 2

        def halves(x, which):
            return lax.dynamic_slice_in_dim(x, which * half, half, x.ndim - 1)

        pair = jnp.stack([w_gate, w_up])
        pair_same, pair_other = halves(pair, odd), halves(pair, 1 - odd)
        down = w_down.T[None]
        down_same, down_other = halves(down, odd), halves(down, 1 - odd)
        ordered = n_seq == 2 and n_dp == 4

        if n_seq == 2:
            masks = (0, 2, 1, 3)
            span = jnp.arange(own_rows, dtype=jnp.int32)
            k_idx = jnp.concatenate(
                [(seq_at ^ y) * tokens + (sec ^ m) * own_rows + span for y in (0, 1) for m in masks]
            )
            q_idx = k_idx[:tokens]
        else:
            k_idx = jnp.arange(n_seq * tokens, dtype=jnp.int32)
            q_idx = seq_at * tokens + jnp.arange(tokens, dtype=jnp.int32)
        count = k_idx.shape[0]
        local_heads = seg_len.shape[0]
        heads = sec * local_heads + jnp.arange(local_heads, dtype=jnp.int32)

        def codes(index):
            slide, pos = slide_place(lengths[0], index)
            block = slide[None, :] * count + pos[None, :] // seg_len[:, None]
            return block, pos[None, :] % rate[:, None] == (heads % rate)[:, None]

        k_block, picked = codes(k_idx)
        k_code = jnp.where(picked, k_block, -1)
        code = jnp.concatenate([k_block, k_code], axis=0)

        own_at = sec * own_rows
        gain = jnp.concatenate(absolute(jnp.split(tile_gain, n_sec)))
        out_w = w_out.T

        if ordered:
            g, d = {(0, 0): pair_same}, {(0, 0): down_same}
            beside = flip(mine, dp=1)
            mine_x = flip(mine, section=2)
            g[0, 2] = rotate(pair_same, 2)
            g[1, 0] = flip(pair_same, seq=1)
            d[1, 0] = flip(down_same, seq=1)
            beside_x = flip(beside, section=2)
            proj_x = flip(after(w_proj, mine_x), section=2)
            for k in (1, 3):
                g[0, k] = rotate(after(pair_other, g[0, 2], d[1, 0], g[1, 0], mine_x), k)
            g[1, 2] = flip(g[0, 2], seq=1)
            tiles = after(
                jnp.concatenate([mine, beside, mine_x, beside_x], axis=0), g[0, 2], g[1, 2]
            )
            both, across = jnp.split(tiles, 2, axis=0)
            both_c, across_c = jnp.split(flip(tiles, section=1), 2, axis=0)
            far = rotate(after(down_same, g[0, 1]), 2)
            rows = jnp.concatenate([both, both_c, across, across_c], axis=1)
            normed = layer_norm(rows.astype(jnp.float32), gain).astype(jnp.bfloat16)
            g[1, 1] = after(flip(g[0, 1], seq=1), normed)
            d[0, 2] = after(far, normed)
            for k in (1, 3):
                d[0, k] = rotate(after(down_other, d[0, 2], code, out_w), k)
            g[1, 3] = after(flip(g[0, 3], seq=1), d[0, 1], d[0, 3])
            gate_up = place_rows(g)
            proj_c = flip(after(w_proj, proj_x, d[0, 1]), section=1)
            proj_xc = flip(after(proj_x, d[0, 1]), section=1)
            proj = jnp.concatenate([w_proj, proj_c, proj_x, proj_xc], axis=0)
            for k in (2, 1, 3):
                d[1, k] = flip(d[0, k], seq=1)
        else:
            gate_up = gather_rows(pair_same, pair_other, seq_at, dp_at)
            down_all = gather_rows(down_same, down_other, seq_at, dp_at)[0]
            both = jnp.concatenate([mine, flip(mine, dp=1)], axis=0)
            rows = jnp.concatenate(gather_section(both), axis=1)
            normed = layer_norm(rows.astype(jnp.float32), gain).astype(jnp.bfloat16)
            proj = jnp.concatenate(gather_section(w_proj), axis=0)

        residual = jnp.dot(
            lax.dynamic_slice_in_dim(rows[:tokens], own_at, own_rows, 0),
            proj,
            preferred_element_type=jnp.float32,
        )
        normed = after(normed, residual)
        gate = jnp.dot(normed, gate_up[0], preferred_element_type=jnp.float32)
        up = jnp.dot(normed, gate_up[1], preferred_element_type=jnp.float32)
        hidden = (jax.nn.silu(gate) * up).astype(jnp.bfloat16)
        hidden = hidden.reshape(2, n_sec // 2, 2, own_rows, half)

        def fold(proj_rows, down_rows):
            return lax.dot_general(
                proj_rows, down_rows, (((0,), (0,)), ((), ())), preferred_element_type=jnp.float32
            )

        if ordered:
            late = [d.pop((1, 1)), d.pop((1, 3))]
            folded = fold(proj, after(place_rows(d)[0], hidden))
            for k, block in zip((1, 3), late):
                at = row_of(1, k, block.shape[1])
                folded = folded + fold(
                    lax.dynamic_slice_in_dim(proj, at, block.shape[1], 0), block[0]
                )
        else:
            folded = fold(proj, down_all)
        folded = folded.astype(jnp.bfloat16)

        def project(x):
            return lax.dot_general(
                x, folded, (((x.ndim - 1,), (1,)), ((), ())), preferred_element_type=jnp.float32
            )

        send = project(lax.dynamic_index_in_dim(hidden, 1 - core, 2, False)).astype(jnp.bfloat16)
        got = flip(send, section=1)
        kept = after(project(lax.dynamic_index_in_dim(hidden, core, 2, False)), send)
        kept = kept + got.astype(jnp.float32)
        here = lax.dynamic_index_in_dim(kept, side, 1, False)
        there = lax.dynamic_index_in_dim(kept, 1 - side, 1, False).astype(jnp.bfloat16)
        from_x = flip(there[0], section=2)
        from_z = flip(here[1].astype(jnp.bfloat16), dp=1)
        from_xz = flip(there[1], section=2, dp=1)
        emb = (
            residual
            + here[0]
            + from_x.astype(jnp.float32)
            + from_z.astype(jnp.float32)
            + from_xz.astype(jnp.float32)
        )
        slide_normed = layer_norm(emb, slide_gain).astype(jnp.bfloat16)

        vmem = pl.BlockSpec(memory_space=pltpu.VMEM)
        if n_seq == 2:
            keys = [
                slide_normed,
                flip(slide_normed, section=2),
                flip(slide_normed, seq=1),
                flip(slide_normed, section=2, seq=1),
            ]
            others = [flip(block, section=1) for block in keys]
            keys = keys[:2] + others[:2] + keys[2:] + others[2:]
        else:
            keys = lax.all_gather(slide_normed, ("seq", "section"), axis=0, tiled=True)

        width = w_qkv.shape[2]
        qkv = jnp.swapaxes(w_qkv, 1, 2)
        if n_seq == 2:
            keep, send = pl.pallas_call(
                lambda *refs: attend_kernel(*refs, heads=local_heads, masks=masks),
                out_shape=[
                    jax.ShapeDtypeStruct((2, width, tokens), jnp.float32),
                    jax.ShapeDtypeStruct((2, width, tokens), jnp.bfloat16),
                ],
                in_specs=[vmem] * 12,
                out_specs=[vmem] * 2,
                compiler_params=pltpu.CompilerParams(vmem_limit_bytes=16 * 2**20),
                cost_estimate=pl.CostEstimate(
                    flops=2 * count * width * (3 * 768 + 2 * local_heads * tokens),
                    bytes_accessed=8 * 2**20,
                    transcendentals=local_heads * tokens * count,
                ),
            )(*keys, qkv, out_w, emb, code)
        else:

            def by_head(x, matrix):
                x = jnp.dot(x, matrix.T, preferred_element_type=jnp.float32)
                x = x.astype(jnp.bfloat16).reshape(x.shape[0], local_heads, width // local_heads)
                return x.transpose(1, 0, 2)

            def one_head(args):
                q, k, v, q_row, k_row = args
                scores = jnp.dot(q, k.T, preferred_element_type=jnp.float32)
                scores = scores / math.sqrt(width // local_heads)
                ok = (q_row[:, None] == k_row[None, :]) | (q_idx[:, None] == k_idx[None, :])
                weight = jax.nn.softmax(jnp.where(ok, scores, NEG), axis=-1)
                return jnp.dot(weight, v, preferred_element_type=jnp.float32)

            queries = lax.dynamic_slice_in_dim(keys, seq_at * tokens, tokens, 0)
            att = lax.map(
                one_head,
                (by_head(queries, qkv[0]), by_head(keys, qkv[1]), by_head(keys, qkv[2]))
                + (codes(q_idx)[0], k_code),
            )
            att = att.transpose(1, 0, 2).reshape(tokens, width).astype(jnp.bfloat16)
            parts = jnp.dot(att, w_out, preferred_element_type=jnp.float32)
            old = lax.dynamic_slice_in_dim(parts, sec * own_rows, own_rows, 0)
            parts = lax.dynamic_update_slice_in_dim(parts, old + emb, sec * own_rows, 0)
            parts = jnp.stack(absolute(jnp.split(parts.T, n_sec, axis=0)))
            keep, send = parts[0::2], parts[1::2].astype(jnp.bfloat16)

        kept = keep + flip(send, section=1).astype(jnp.float32)
        out = kept[0] + flip(kept[1].astype(jnp.bfloat16), section=2).astype(jnp.float32)
        return out.astype(jnp.bfloat16).T[None]

    return per_device


def solution(mesh):
    placed = (
        P("dp", "seq", "section"),
        P(),
        P(("seq", "dp"), "section"),
        P(("seq", "dp"), "section"),
        P("section", ("seq", "dp")),
        P("section", None),
        P(),
        P(None, None, "section"),
        P("section", None),
        P("dp", None),
        P("section"),
        P("section"),
    )
    shape = mesh.shape
    return jax.shard_map(
        build(shape["section"], shape["seq"], shape["dp"]),
        mesh=mesh,
        in_specs=placed,
        out_specs=P("dp", "seq", "section"),
        check_vma=False,
    )
```
